32 devices in a mesh: rep: 8 (over y, x, core), shard: 4 (over z).
Axes of the slice: x: 2, y: 2, z: 4, core: 2. Of those that a mesh axis runs over, the one named last changes fastest.
Arguments:
- hidden_in: bfloat16 [32768, 768], P(('rep', 'shard')), may hold values from -6 to 6
- segment: int32 [32, 1024], P(('rep', 'shard')), may hold values from 0 to 32, as said below
- cotangent: bfloat16 [32768, 768], P(('rep', 'shard')), may hold values from -6 to 6
- ln1_gain: bfloat16 [768], P('shard'), may hold values from 0.5 to 1.5
- ln1_bias: bfloat16 [768], P('shard'), may hold values from -1.75 to 1.75
- qkv_weight: bfloat16 [768, 2304], P('shard'), may hold values from -0.21875 to 0.21875
- query_bias: bfloat16 [768], P('shard'), may hold values from -3 to 3
- value_bias: bfloat16 [768], P('shard'), may hold values from -3 to 3
- out_weight: bfloat16 [768, 768], P('shard'), may hold values from -2 to 2
- out_bias: bfloat16 [768], P('shard'), may hold values from -3 to 3
- ln2_gain: bfloat16 [768], P('shard'), may hold values from 0.5 to 1.5
- ln2_bias: bfloat16 [768], P('shard'), may hold values from -1.75 to 1.75
- fc_weight: bfloat16 [768, 3072], P('shard'), may hold values from -0.21875 to 0.21875
- fc_bias: bfloat16 [3072], P('shard'), may hold values from -3 to 3
- proj_weight: bfloat16 [3072, 768], P('shard'), may hold values from -0.109375 to 0.109375
- proj_bias: bfloat16 [768], P('shard'), may hold values from -3 to 3
Outputs:
- block_out: bfloat16 [32768, 768], P(('rep', 'shard'))
- input_grad: bfloat16 [32768, 768], P(('rep', 'shard'))
- grad_ln1_gain: float32 [768], P('shard')
- grad_ln1_bias: float32 [768], P('shard')
- grad_qkv_weight: float32 [768, 2304], P('shard')
- grad_query_bias: float32 [768], P('shard')
- grad_value_bias: float32 [768], P('shard')
- grad_out_weight: float32 [768, 768], P('shard')
- grad_out_bias: float32 [768], P('shard')
- grad_ln2_gain: float32 [768], P('shard')
- grad_ln2_bias: float32 [768], P('shard')
- grad_fc_weight: float32 [768, 3072], P('shard')
- grad_fc_bias: float32 [3072], P('shard')
- grad_proj_weight: float32 [3072, 768], P('shard')
- grad_proj_bias: float32 [768], P('shard')
The draws below stay inside these ranges and needn't reach their ends.
Inputs may be any that keep to these rules, and one draw needn't show every extreme that they name: Each row holds one device's tokens; segment numbers start at 0 in every row and never fall along it; equal numbers in a row mark one sequence. One row in every draw holds a single sequence of 1024 tokens, and some row in every draw reaches the largest number.
All inputs are finite; a program needn't handle non-finite values.
Results may differ from the reference program's by a relative error of at most 0.019.
Values may be sent and summed in bfloat16 or wider, within the bound.
No kernel may reach another device: no remote copies, remote signals or barrier semaphores. Data moves between devices by JAX's collectives and lax.ppermute only.
A program may use at most 320 MiB of HBM per device.

```python
import jax
import jax.numpy as jnp
from jax import lax

D = 768
HEADS = 12
HEAD_DIM = 64
FF = 3072
TOK_DEV = 1024
ROWS = 32
TOKENS = 32768


def draw_segment(key, part):
    key = jax.random.fold_in(key, 11)
    key_rate, key_flag, key_full, key_dense = jax.random.split(key, 4)
    ceiling = max(TOK_DEV // 32, 3)
    picked = jax.random.randint(key_rate, (ROWS, 1), 0, 3)
    spacing = jnp.where(picked == 0, max(TOK_DEV // 24, 2), jnp.where(picked == 1, max(TOK_DEV // 6, 2), max(TOK_DEV // 2, 2)))
    ticket = jax.random.randint(key_flag, (ROWS, TOK_DEV), 0, 1 << 20)
    starts = (ticket % spacing == 0).astype(jnp.int32)
    column = jnp.arange(TOK_DEV)[None, :]
    starts = jnp.where(column == 0, 0, starts)
    row_index = jnp.arange(ROWS)[:, None]
    full_row = jax.random.randint(key_full, (), 0, ROWS)
    dense_row = (full_row + 1 + jax.random.randint(key_dense, (), 0, ROWS - 1)) % ROWS
    starts = jnp.where(row_index == full_row, 0, starts)
    counted = jnp.minimum(jnp.cumsum(starts, axis=1), ceiling)
    even_split = column * (ceiling + 1) // TOK_DEV
    counted = jnp.where(row_index == dense_row, even_split, counted)
    return counted.astype(jnp.int32)


def strengthened(values, key, source, target, shards_of, factor):
    def block_of(dim):
        return (jnp.arange(values.shape[dim]) // (values.shape[dim] // shards_of)).reshape((-1,) + (1,) * (values.ndim - 1 - dim))

    first = jax.random.permutation(key, shards_of)[block_of(target)]
    second = (block_of(target) + shards_of // 2) % shards_of
    return jnp.where((block_of(source) == first) | (block_of(source) == second), factor * values, values)


def steps_of(rng, shape, cuts, low, high):
    def one(dim, shards_of):
        draws = jax.random.uniform(jax.random.fold_in(jax.random.fold_in(rng, 6), dim), (shards_of,), jnp.float32, low / len(cuts), high / len(cuts))
        return jnp.repeat(jnp.exp(draws), shape[dim] // shards_of).reshape((-1,) + (1,) * (len(shape) - dim - 1))

    factor_of = one(*cuts[0])
    for cut in cuts[1:]:
        factor_of = factor_of * one(*cut)
    return factor_of


def normal_values(own_key, shape, scale, reach, cuts=(), held_as=jnp.bfloat16):
    array = jax.random.normal(own_key, shape, jnp.float32) * scale
    if len(cuts) > 0:
        array = steps_of(own_key, shape, cuts, -0.22, 0.18) * array
    return jnp.clip(array, min=-reach, max=reach).astype(held_as)


def bell_draw_with(stream_key, extent, deviation, reach, cuts, heavy, dtype=jnp.bfloat16):
    drawn = deviation * jax.random.normal(stream_key, extent, jnp.float32)
    if cuts:
        drawn = drawn * steps_of(stream_key, extent, cuts, -0.22, 0.18)
    return jnp.clip(strengthened(drawn, jax.random.fold_in(stream_key, 3), *heavy), -reach, reach).astype(dtype)


def setup_inputs(seed: int = 0) -> dict:
    splits = jax.random.split(jax.random.key(seed), 17)
    return {
        "hidden_in": normal_values(splits[0], (TOKENS, D), 1.0, 6.0, ((0, 32),)),
        "segment": draw_segment(jax.random.fold_in(splits[16], 71), 0),
        "cotangent": bell_draw_with(splits[2], (TOKENS, D), 1.0, 6.0, ((0, 32),), (0, 1, 32, 2.75)),
        "ln1_gain": jnp.clip(1.0 + 0.1 * jax.random.normal(splits[3], (D,), jnp.float32), 0.5, 1.5).astype(jnp.bfloat16),
        "ln1_bias": normal_values(splits[4], (D,), 0.3, 1.75, ((0, 4),)),
        "qkv_weight": normal_values(splits[5], (D, 3 * D), D ** -0.5, 0.21875, ((0, 4),)),
        "query_bias": normal_values(splits[6], (D,), 0.5, 3.0, ((0, 4),)),
        "value_bias": normal_values(splits[7], (D,), 0.5, 3.0, ((0, 4),)),
        "out_weight": normal_values(splits[8], (D, D), 8 ** -0.5, 2.0, ((0, 4),)),
        "out_bias": normal_values(splits[9], (D,), 0.5, 3.0, ((0, 4),)),
        "ln2_gain": jnp.clip(1.0 + 0.1 * jax.random.normal(splits[10], (D,), jnp.float32), 0.5, 1.5).astype(jnp.bfloat16),
        "ln2_bias": normal_values(splits[11], (D,), 0.3, 1.75, ((0, 4),)),
        "fc_weight": normal_values(splits[12], (D, FF), D ** -0.5, 0.21875, ((0, 4),)),
        "fc_bias": normal_values(splits[13], (FF,), 0.5, 3.0, ((0, 4),)),
        "proj_weight": normal_values(splits[14], (FF, D), FF ** -0.5, 0.109375, ((0, 4),)),
        "proj_bias": normal_values(splits[15], (D,), 0.5, 3.0, ((0, 4),)),
    }


@jax.custom_vjp
def low(v):
    return lax.optimization_barrier(v.astype(jnp.bfloat16)).astype(jnp.float32)

@jax.custom_vjp
def low_back(v):
    return v

def low_keep(v):
    return (low(v), None)

def low_pass(kept, grad):
    return (grad,)

def back_keep(v):
    return (v, None)

def back_low(kept, grad):
    return (low(grad),)
low.defvjp(low_keep, low_pass)
low_back.defvjp(back_keep, back_low)

def matmul(left, right):
    return jnp.dot(left, right, precision=lax.Precision.HIGHEST)

def layer_norm(values, gain, shift):
    center = values - lax.optimization_barrier(jnp.mean(values, axis=-1, keepdims=True))
    spread = lax.optimization_barrier(jnp.mean(center * center, axis=-1, keepdims=True))
    return center * lax.rsqrt(spread + 1e-05) * gain + shift

def row_forward(row_in, seg_row, params):
    ln1_gain, ln1_bias, qkv_weight, query_bias, value_bias, out_weight, out_bias, ln2_gain, ln2_bias, fc_weight, fc_bias, proj_weight, proj_bias = params
    length = row_in.shape[0]
    norm_one = low(layer_norm(row_in, ln1_gain, ln1_bias))
    joined = matmul(norm_one, qkv_weight)
    queries = low(low_back(joined[:, :D] + query_bias)).reshape(length, HEADS, HEAD_DIM)
    key_rows = low(low_back(joined[:, D:2 * D])).reshape(length, HEADS, HEAD_DIM)
    value_rows = low(low_back(joined[:, 2 * D:] + value_bias)).reshape(length, HEADS, HEAD_DIM)
    scores = jnp.einsum('qhd,khd->hqk', queries, key_rows, precision=lax.Precision.HIGHEST) * HEAD_DIM ** (-0.5)
    scores = low_back(scores)
    position = jnp.arange(length)
    allowed = (seg_row[:, None] == seg_row[None, :]) & (position[:, None] >= position[None, :])
    scores = jnp.where(allowed[None], scores, -1e+30)
    attn_low = low(jax.nn.softmax(scores, axis=-1))
    attended = jnp.einsum('hqk,khd->qhd', attn_low, value_rows, precision=lax.Precision.HIGHEST).reshape(length, D)
    attended = low(low_back(attended))
    resid = row_in + low_back(matmul(attended, out_weight) + out_bias)
    norm_two = low(layer_norm(resid, ln2_gain, ln2_bias))
    pre_act = low_back(matmul(norm_two, fc_weight) + fc_bias)
    gelu_low = low(jax.nn.gelu(pre_act, approximate=True))
    return resid + low_back(matmul(gelu_low, proj_weight) + proj_bias)

def reference(hidden_in, segment, cotangent, ln1_gain, ln1_bias, qkv_weight, query_bias, value_bias, out_weight, out_bias, ln2_gain, ln2_bias, fc_weight, fc_bias, proj_weight, proj_bias):
    params = tuple((item.astype(jnp.float32) for item in (ln1_gain, ln1_bias, qkv_weight, query_bias, value_bias, out_weight, out_bias, ln2_gain, ln2_bias, fc_weight, fc_bias, proj_weight, proj_bias)))
    inputs = hidden_in.astype(jnp.float32).reshape(ROWS, TOK_DEV, D)
    upstream = cotangent.astype(jnp.float32).reshape(ROWS, TOK_DEV, D)

    def forward(values, weights):

        def one_row(pair):
            return row_forward(pair[0], pair[1], weights)
        return lax.map(jax.checkpoint(one_row), (values, segment))
    outputs, pullback = jax.vjp(forward, inputs, params)
    grad_inputs, grads = pullback(upstream)
    block_out = outputs.reshape(TOKENS, D).astype(jnp.bfloat16)
    input_grad = grad_inputs.reshape(TOKENS, D).astype(jnp.bfloat16)
    return (block_out, input_grad, grads[0], grads[1], grads[2], grads[3], grads[4], grads[5], grads[6], grads[7], grads[8], grads[9], grads[10], grads[11], grads[12])
```

```python
import functools
import math

import jax
import jax.numpy as jnp
from jax import lax
from jax.experimental import pallas as pl
from jax.experimental.pallas import tpu as pltpu
from jax.sharding import PartitionSpec as P

HEADS = 12
HEAD_DIM = 64
LOG2E = math.log2(math.e)
NEG = -1e30
BF16 = jnp.bfloat16
F32 = jnp.float32
VMEM_LIMIT = 56 << 20


def dot_nt(a, b):
    return lax.dot_general(a, b, (((1,), (1,)), ((), ())), preferred_element_type=F32)


def dot_nn(a, b):
    return lax.dot_general(a, b, (((1,), (0,)), ((), ())), preferred_element_type=F32)


def dot_tn(a, b):
    return lax.dot_general(a, b, (((0,), (0,)), ((), ())), preferred_element_type=F32)


def params():
    return pltpu.CompilerParams(vmem_limit_bytes=VMEM_LIMIT)


def swap(value, axis, size, mask):
    return lax.ppermute(value, axis, [(i, i ^ mask) for i in range(size)])


def allowed_block(seg_col, seg_row, block, rows):
    keys = (block + 1) * rows
    same = seg_col[:keys, :] == seg_row[:, block * rows : keys]
    causal = lax.broadcasted_iota(jnp.int32, (rows, rows), 0) <= lax.broadcasted_iota(
        jnp.int32, (rows, rows), 1
    )
    if block == 0:
        return same & causal
    return jnp.concatenate([same[: keys - rows], same[keys - rows :] & causal], axis=0)


def attend_kernel(rows, seg_col, seg_row, q_ref, k_ref, v_ref, o_ref, lse_ref):
    length = q_ref.shape[0]
    lane = lax.broadcasted_iota(jnp.int32, (1, 128), 1)
    scale = HEAD_DIM ** (-0.5) * LOG2E
    v_turned = v_ref[...].T
    for block in range(length // rows):
        keys = (block + 1) * rows
        here = slice(block * rows, keys)
        q = q_ref[here, :]
        k = k_ref[:keys, :]
        allowed = allowed_block(seg_col, seg_row, block, rows)
        parts = []
        for head in range(2):
            mine = (lane < 64) if head == 0 else (lane >= 64)
            q_head = jnp.where(mine, q, jnp.zeros_like(q))
            scores = jnp.where(allowed, dot_nt(k, q_head), NEG)
            highest = jnp.max(scores, axis=0, keepdims=True)
            expo = jnp.exp2((scores - highest) * scale)
            summed = jnp.sum(expo, axis=0, keepdims=True)
            v_head = v_turned[head * 64 : (head + 1) * 64, :keys]
            parts.append(dot_nn(v_head, expo.astype(BF16)) * (1.0 / summed))
            lse_ref[head, :, here] = jnp.broadcast_to(
                highest * scale + jnp.log2(summed), (8, rows)
            )
        o_ref[here, :] = jnp.concatenate(parts, axis=0).T.astype(BF16)


def head_specs(length, start):
    groups = HEADS // 2
    return [
        pl.BlockSpec((length, 1), lambda h: (0, 0)),
        pl.BlockSpec((1, length), lambda h: (0, 0)),
        pl.BlockSpec((length, 128), lambda h: (0, start + h)),
        pl.BlockSpec((length, 128), lambda h: (0, groups + start + h)),
        pl.BlockSpec((length, 128), lambda h: (0, 2 * groups + start + h)),
    ]


def attend_forward(qkv, segment, start, count):
    length = qkv.shape[0]
    rows = length // 2
    return pl.pallas_call(
        functools.partial(attend_kernel, rows),
        grid=(count,),
        in_specs=head_specs(length, start),
        out_specs=[
            pl.BlockSpec((length, 128), lambda h: (0, h)),
            pl.BlockSpec((2, 8, length), lambda h: (h, 0, 0)),
        ],
        out_shape=[
            jax.ShapeDtypeStruct((length, 128 * count), BF16),
            jax.ShapeDtypeStruct((2 * count, 8, length), F32),
        ],
        compiler_params=params(),
        cost_estimate=pl.CostEstimate(
            flops=3 * 10**9 * count, bytes_accessed=count << 20, transcendentals=10**6 * count
        ),
        name="attend_forward",
    )(segment.reshape(length, 1), segment.reshape(1, length), qkv, qkv, qkv)


def attend_back_kernel(
    rows, seg_col, seg_row, q_ref, k_ref, v_ref, g_ref, lse_ref, dq_ref, dk_ref, dv_ref, dk_sum, dv_sum
):
    length = q_ref.shape[0]
    lane = lax.broadcasted_iota(jnp.int32, (1, 128), 1)
    scale = HEAD_DIM ** (-0.5) * LOG2E
    blocks = length // rows
    for block in reversed(range(blocks)):
        keys = (block + 1) * rows
        here = slice(block * rows, keys)
        q = q_ref[here, :]
        g = g_ref[here, :]
        k = k_ref[:keys, :]
        v = v_ref[:keys, :]
        allowed = allowed_block(seg_col, seg_row, block, rows)
        dq = dk = dv = None
        for head in range(2):
            mine = (lane < 64) if head == 0 else (lane >= 64)
            q_head = jnp.where(mine, q, jnp.zeros_like(q))
            g_head = jnp.where(mine, g, jnp.zeros_like(g))
            scores = dot_nt(k, q_head) * scale - lse_ref[head, 0:1, here]
            probs = jnp.exp2(jnp.where(allowed, scores, NEG))
            grad_probs = dot_nt(v, g_head)
            inner = jnp.sum(probs * grad_probs, axis=0, keepdims=True)
            grad_scores = (probs * (grad_probs - inner)).astype(BF16)
            dv_head = dot_nn(probs.astype(BF16), g_head)
            dk_head = dot_nn(grad_scores, q_head)
            dq_head = dot_tn(grad_scores, k)
            if head == 0:
                dq, dk, dv = dq_head, dk_head, dv_head
            else:
                dq, dk, dv = jnp.where(lane < 64, dq, dq_head), dk + dk_head, dv + dv_head
        dq_ref[here, :] = (dq * HEAD_DIM ** (-0.5)).astype(BF16)
        if block == blocks - 1:
            dk_sum[...] = dk
            dv_sum[...] = dv
        else:
            dk_sum[:keys, :] += dk
            dv_sum[:keys, :] += dv
    dk_ref[...] = (dk_sum[...] * HEAD_DIM ** (-0.5)).astype(BF16)
    dv_ref[...] = dv_sum[...].astype(BF16)


def attend_backward(qkv, segment, grad, lse, start, count):
    length = qkv.shape[0]
    rows = length // 2
    return pl.pallas_call(
        functools.partial(attend_back_kernel, rows),
        grid=(count,),
        in_specs=head_specs(length, start)
        + [
            pl.BlockSpec((length, 128), lambda h: (0, start + h)),
            pl.BlockSpec((2, 8, length), lambda h: (h, 0, 0)),
        ],
        out_specs=[pl.BlockSpec((length, 128), lambda h: (0, h))] * 3,
        out_shape=[jax.ShapeDtypeStruct((length, 128 * count), BF16)] * 3,
        scratch_shapes=[pltpu.VMEM((length, 128), F32)] * 2,
        compiler_params=params(),
        cost_estimate=pl.CostEstimate(
            flops=6 * 10**9 * count, bytes_accessed=2 * count << 20, transcendentals=10**6 * count
        ),
        name="attend_backward",
    )(segment.reshape(length, 1), segment.reshape(1, length), qkv, qkv, qkv, grad, lse)


def position_to_rel(slot, pieces, first):
    if pieces == 4 and first == 2:
        return (slot & 1) * 2 + slot // 2
    return slot


def place_rows(total, old_ref, outs, spots, pieces, first, by_shard):
    for slot in range(pieces):
        piece = position_to_rel(slot, pieces, first) ^ spots[1]
        for rel_z in range(outs[0].shape[1]):
            rows = outs[0].shape[2]
            owner = 0 if by_shard else rel_z ^ spots[2]
            start = pl.multiple_of((owner * pieces + piece) * rows, 16)
            value = total[pl.ds(start, rows), :]
            if old_ref is not None:
                value = value + old_ref[slot, rel_z].astype(F32)
            size = outs[0].shape[0]
            outs[slot // size][slot % size, rel_z] = value.astype(BF16)


def grad_proj_kernel(pieces, first, add, spots, x_ref, y_ref, *rest):
    total = rest[-1]
    total[...] = dot_tn(x_ref[...], y_ref[...])
    old_ref, outs = (rest[0], rest[1:-1]) if add else (None, rest[:-1])
    place_rows(total, old_ref, outs, spots, pieces, first, True)


def grad_two_kernel(pieces, first, add, tiles, spots, x_ref, y_ref, x2_ref, y2_ref, *rest):
    total = rest[-1]

    @pl.when(pl.program_id(0) < tiles)
    def _():
        total[...] = dot_tn(x_ref[...], y_ref[...])

    @pl.when(pl.program_id(0) >= tiles)
    def _():
        total[...] = dot_tn(x2_ref[...], y2_ref[...])

    old_ref, outs = (rest[0], rest[1:-1]) if add else (None, rest[:-1])
    place_rows(total, old_ref, outs, spots, pieces, first, False)


def grad_heads_kernel(pieces, first, add, spots, x_ref, q_ref, k_ref, v_ref, *rest):
    total = rest[-1]
    joined = jnp.concatenate([q_ref[...], k_ref[...], v_ref[...]], axis=1)
    total[...] = dot_tn(x_ref[...], joined)
    old_ref, outs = (rest[0], rest[1:-1]) if add else (None, rest[:-1])
    place_rows(total, old_ref, outs, spots, pieces, first, False)


def grad_call(kernel, grid, in_specs, operands, block, shape, pieces, scratch, spots, old, flops):
    if old is not None:
        in_specs = in_specs + [block(pieces)]
        operands = operands + [old]
        out_specs = [block(pieces // 2)] * 2
        out_shape = [shape(pieces // 2)] * 2
    else:
        out_specs = block(pieces)
        out_shape = shape(pieces)
    return pl.pallas_call(
        kernel,
        grid_spec=pltpu.PrefetchScalarGridSpec(
            num_scalar_prefetch=1,
            grid=grid,
            in_specs=in_specs,
            out_specs=out_specs,
            scratch_shapes=[scratch],
        ),
        out_shape=out_shape,
        compiler_params=params(),
        cost_estimate=pl.CostEstimate(flops=2 * flops, bytes_accessed=4 << 20, transcendentals=0),
        name="weight_grad",
    )(spots, *operands)


def side_of(add):
    return (lambda s: s[0]) if add else (lambda s: 1 - s[0])


def grad_proj(x, y, spots, shards, pieces, first, old=None):
    length, rows_all = x.shape
    half = y.shape[1] // 2
    rows = rows_all // (shards * pieces)
    side = side_of(old is not None)
    return grad_call(
        functools.partial(grad_proj_kernel, pieces, first, old is not None),
        (shards,),
        [
            pl.BlockSpec((length, rows_all // shards), lambda i, s: (0, i ^ s[2])),
            pl.BlockSpec((length, half), lambda i, s: (0, side(s))),
        ],
        [x, y],
        lambda n: pl.BlockSpec((n, 1, rows, half), lambda i, s: (0, i, 0, 0)),
        lambda n: jax.ShapeDtypeStruct((n, shards, rows, half), BF16),
        pieces,
        pltpu.VMEM((rows_all // shards, half), F32),
        spots,
        old,
        length * rows_all * half,
    )


def grad_two(x, y, x2, y2, spots, shards, pieces, first, old=None):
    length, rows_all = x.shape
    half, half2 = y.shape[1] // 2, y2.shape[1] // 2
    rows = rows_all // (shards * pieces)
    tiles = half // half2
    side = side_of(old is not None)
    return grad_call(
        functools.partial(grad_two_kernel, pieces, first, old is not None, tiles),
        (tiles + 1,),
        [
            pl.BlockSpec((length, rows_all), lambda i, s: (0, 0)),
            pl.BlockSpec(
                (length, half2), lambda i, s: (0, side(s) * tiles + jnp.minimum(i, tiles - 1))
            ),
            pl.BlockSpec((length, rows_all), lambda i, s: (0, 0)),
            pl.BlockSpec((length, half2), lambda i, s: (0, side(s))),
        ],
        [x, y, x2, y2],
        lambda n: pl.BlockSpec((n, shards, rows, half2), lambda i, s: (0, 0, 0, i)),
        lambda n: jax.ShapeDtypeStruct((n, shards, rows, half + half2), BF16),
        pieces,
        pltpu.VMEM((rows_all, half2), F32),
        spots,
        old,
        length * rows_all * (half + half2),
    )


def grad_heads(x, grads, spots, shards, pieces, first, old=None):
    length, rows_all = x.shape
    half = grads[0].shape[1] // 2
    rows = rows_all // (shards * pieces)
    side = side_of(old is not None)
    return grad_call(
        functools.partial(grad_heads_kernel, pieces, first, old is not None),
        (1,),
        [pl.BlockSpec((length, rows_all), lambda i, s: (0, 0))]
        + [pl.BlockSpec((length, half), lambda i, s: (0, side(s)))] * 3,
        [x, *grads],
        lambda n: pl.BlockSpec((n, shards, rows, 3 * half), lambda i, s: (0, 0, 0, 0)),
        lambda n: jax.ShapeDtypeStruct((n, shards, rows, 3 * half), BF16),
        pieces,
        pltpu.VMEM((rows_all, 3 * half), F32),
        spots,
        old,
        length * rows_all * 3 * half,
    )


def assemble_kernel(shards, pieces, rows, column, spots, own_ref, *rest):
    parts = rest[: 2 * pieces]
    full_ref, sems = rest[2 * pieces :]
    core, spot_u, spot_z = spots[0], spots[1], spots[2]
    shard_rows = own_ref.shape[0]
    half = own_ref.shape[1] // 2
    copies = [
        pltpu.make_async_copy(
            own_ref,
            full_ref.at[pl.ds(pl.multiple_of(spot_z * shard_rows, 16), shard_rows), :],
            sems.at[0],
        )
    ]
    for index, part in enumerate(parts):
        side = core if index < pieces else 1 - core
        piece = spot_u ^ (index % pieces)
        for step in range(1, shards):
            start = pl.multiple_of((spot_z ^ step) * shard_rows + piece * rows, 16)
            copies.append(
                pltpu.make_async_copy(
                    part.at[step - 1, pl.ds(0, rows), pl.ds(column, half)],
                    full_ref.at[pl.ds(start, rows), pl.ds(pl.multiple_of(side * half, 128), half)],
                    sems.at[len(copies)],
                )
            )
    for copy in copies:
        copy.start()
    for copy in copies:
        copy.wait()


def assemble(own, parts, column, spots, shards, pieces):
    shard_rows, width = own.shape
    rows = shard_rows // pieces
    anywhere = pl.BlockSpec(memory_space=pl.ANY)
    return pl.pallas_call(
        functools.partial(assemble_kernel, shards, pieces, rows, column),
        in_specs=[pl.BlockSpec(memory_space=pltpu.SMEM)] + [anywhere] * (1 + 2 * pieces),
        out_specs=pl.BlockSpec(memory_space=pltpu.VMEM),
        out_shape=jax.ShapeDtypeStruct((shards * shard_rows, width), BF16),
        scratch_shapes=[pltpu.SemaphoreType.DMA((1 + 2 * pieces * (shards - 1),))],
        compiler_params=params(),
        cost_estimate=pl.CostEstimate(
            flops=0, bytes_accessed=4 * shards * shard_rows * width, transcendentals=0
        ),
        name="assemble",
    )(spots, own, *parts)


def settle_kernel(pieces, every_ref, *outs):
    rows = every_ref.shape[1]
    for index in range(2 * pieces):
        piece, core = index // 2, index % 2
        column = 0
        for out_ref in outs:
            half = out_ref.shape[1] // 2
            out_ref[piece * rows : (piece + 1) * rows, core * half : (core + 1) * half] = every_ref[
                index, :, column : column + half
            ].astype(F32)
            column += half


def settle(every, widths, pieces):
    rows = every.shape[1]
    whole = pl.BlockSpec(memory_space=pltpu.VMEM)
    return pl.pallas_call(
        functools.partial(settle_kernel, pieces),
        in_specs=[whole],
        out_specs=[whole] * len(widths),
        out_shape=[jax.ShapeDtypeStruct((rows * pieces, width), F32) for width in widths],
        compiler_params=params(),
        name="settle",
    )(every)


def settle_heads_kernel(pieces, spots, every_ref, *rest):
    parts, out_ref = rest[: 2 * pieces], rest[2 * pieces]
    core, spot_u = spots[0], spots[1]
    rows = every_ref.shape[1]
    wide, narrow = every_ref.shape[2] // 3, parts[0].shape[1] // 3
    width = out_ref.shape[1] // 3
    for index in range(2 * pieces):
        for kind in range(3):
            column = kind * width + (index % 2) * wide
            out_ref[
                (index // 2) * rows : (index // 2 + 1) * rows, column : column + wide
            ] = every_ref[index, :, kind * wide : (kind + 1) * wide].astype(F32)
    for index, part in enumerate(parts):
        side = core if index < pieces else 1 - core
        start = pl.multiple_of((spot_u ^ (index % pieces)) * rows, 16)
        for kind in range(3):
            column = pl.multiple_of(kind * width + 2 * wide + side * narrow, 128)
            out_ref[pl.ds(start, rows), pl.ds(column, narrow)] = part[
                :, kind * narrow : (kind + 1) * narrow
            ].astype(F32)


def settle_heads(every, parts, spots, pieces):
    rows = every.shape[1]
    columns = 2 * (every.shape[2] + parts[0].shape[1])
    whole = pl.BlockSpec(memory_space=pltpu.VMEM)
    return pl.pallas_call(
        functools.partial(settle_heads_kernel, pieces),
        in_specs=[pl.BlockSpec(memory_space=pltpu.SMEM)] + [whole] * (1 + 2 * pieces),
        out_specs=whole,
        out_shape=jax.ShapeDtypeStruct((rows * pieces, columns), F32),
        compiler_params=params(),
        name="settle_heads",
    )(spots, every, *parts)


def layer_norm(values, gain, shift):
    center = values - jnp.mean(values, axis=-1, keepdims=True)
    spread_of = jnp.mean(center * center, axis=-1, keepdims=True)
    return center * lax.rsqrt(spread_of + 1e-05) * gain + shift


def norm_scale(values, gain):
    center = values - jnp.mean(values, axis=-1, keepdims=True)
    spread_of = jnp.mean(center * center, axis=-1, keepdims=True)
    return center * lax.rsqrt(spread_of + 1e-05) * gain


def gelu_tanh(values):
    return jax.nn.gelu(values, approximate=True)


def column_sum(values):
    return jnp.sum(values.astype(F32), axis=0)


def shards_of(
    reps,
    shards,
    hidden_in,
    segment,
    cotangent,
    ln1_gain,
    ln1_bias,
    qkv_weight,
    query_bias,
    value_bias,
    out_weight,
    out_bias,
    ln2_gain,
    ln2_bias,
    fc_weight,
    fc_bias,
    proj_weight,
    proj_bias,
):
    width = hidden_in.shape[1]
    shard_rows = qkv_weight.shape[0]
    pieces = 4 if shard_rows % 64 == 0 and reps % 8 == 0 else 2
    rep = lax.axis_index("rep")
    spot_z = lax.axis_index("shard")
    core = rep & 1
    spot_u = (rep >> 1) & (pieces - 1)
    spots = jnp.stack([core, spot_u, spot_z]).astype(jnp.int32)

    def own_piece(weight):
        rows, half = weight.shape[0] // pieces, weight.shape[1] // 2
        return lax.dynamic_slice(weight, (spot_u * rows, core * half), (rows, half))

    def across_chips(part, first):
        if pieces == 2:
            return [part, swap(part, "rep", reps, 2)]
        second = 6 - first
        by_first = swap(part, "rep", reps, first)
        by_second = swap(part, "rep", reps, second)
        by_both = swap(by_first, "rep", reps, second)
        if first == 2:
            return [part, by_first, by_second, by_both]
        return [part, by_second, by_first, by_both]

    def across_cores(parts):
        return parts + [swap(part, "rep", reps, 1) for part in parts]

    def along_shard(piece):
        return [swap(piece, "shard", shards, step) for step in range(1, shards)]

    out_half = width // 2
    fc_half = fc_weight.shape[1] // 2
    second_width = out_half + fc_half
    piece_rows = shard_rows // pieces
    qkv_slots = along_shard(own_piece(qkv_weight))
    small = jnp.concatenate(
        [
            ln1_gain,
            ln1_bias,
            query_bias,
            value_bias,
            out_bias,
            ln2_gain,
            ln2_bias,
            proj_bias,
            fc_bias,
        ]
    )
    small_rows = -(-small.shape[0] // second_width)
    small = jnp.pad(small, (0, 16 * second_width - small.shape[0])).reshape(16, second_width)
    second_payload = jnp.concatenate(
        [jnp.concatenate([own_piece(out_weight), own_piece(fc_weight)], axis=1), small], axis=0
    )
    second_slots = along_shard(second_payload)
    qkv_parts = across_chips(jnp.stack(qkv_slots), 2)
    proj_piece, second_slots = lax.optimization_barrier((own_piece(proj_weight), second_slots))
    proj_slots = along_shard(proj_piece)
    qkv_parts = across_cores(qkv_parts)
    second_stack, proj_slots, qkv_parts = lax.optimization_barrier(
        (jnp.stack(second_slots), proj_slots, qkv_parts)
    )
    second_parts = across_chips(second_stack, 2)
    proj_parts = across_chips(jnp.stack(proj_slots), 4)
    second_parts = across_cores(second_parts)
    proj_parts = across_cores(proj_parts)

    rows_of = [small[:small_rows]] + [
        slot[piece_rows : piece_rows + small_rows] for slot in second_slots
    ]
    ordered = []
    for index in range(shards):
        total = jnp.zeros_like(rows_of[0])
        for step, value in enumerate(rows_of):
            total = jnp.where((spot_z ^ step) == index, value, total)
        ordered.append(total.reshape(-1))
    vectors = jnp.stack(ordered).astype(F32)

    def vector(index):
        return vectors[:, index * shard_rows : (index + 1) * shard_rows].reshape(-1)

    gain_one, shift_one, bias_query, bias_value, bias_out, gain_two, shift_two, bias_proj = [
        vector(index) for index in range(8)
    ]
    fc_start = 8 * shard_rows
    bias_fc = vectors[:, fc_start : fc_start + fc_bias.shape[0]].reshape(-1)

    w_qkv = assemble(qkv_weight, qkv_parts, 0, spots, shards, pieces)
    w_out = assemble(out_weight, second_parts, 0, spots, shards, pieces)
    w_fc = assemble(fc_weight, second_parts, out_half, spots, shards, pieces)
    w_proj = assemble(proj_weight, proj_parts, 0, spots, shards, pieces)

    seg_row = segment[0]
    inputs = hidden_in.astype(F32)
    norm_one = layer_norm(inputs, gain_one, shift_one).astype(BF16)
    qkv_bias = jnp.concatenate([bias_query, jnp.zeros_like(bias_query), bias_value])
    qkv = (jnp.dot(norm_one, w_qkv, preferred_element_type=F32) + qkv_bias).astype(BF16)
    attended_one, lse_one = attend_forward(qkv, seg_row, 0, 4)
    attended_two, lse_two = attend_forward(qkv, seg_row, 4, 2)
    attended = jnp.concatenate([attended_one, attended_two], axis=1)
    resid = inputs + jnp.dot(attended, w_out, preferred_element_type=F32) + bias_out
    norm_two = layer_norm(resid, gain_two, shift_two).astype(BF16)
    pre_act = jnp.dot(norm_two, w_fc, preferred_element_type=F32) + bias_fc
    gelu_low = gelu_tanh(pre_act).astype(BF16)

    def reduce_chips(keep, send, first):
        came = swap(send, "rep", reps, first)
        held = keep[0].astype(F32) + came[0].astype(F32)
        if pieces == 2:
            return held
        onward = (keep[1].astype(F32) + came[1].astype(F32)).astype(BF16)
        came = swap(onward, "rep", reps, 6 - first)
        return held + came.astype(F32)

    def reduce_shard(held):
        total = held[0]
        for step in range(1, shards):
            total = total + swap(held[step].astype(BF16), "shard", shards, step).astype(F32)
        mask = 2 * pieces
        while mask < reps:
            total = total + swap(total.astype(BF16), "rep", reps, mask).astype(F32)
            mask *= 2
        return total.astype(BF16)

    def every_owner(piece):
        return lax.all_gather(piece, "rep", axis=0, tiled=False)[: 2 * pieces]

    call = (spots, shards, pieces)
    proj_far = grad_proj(gelu_low, cotangent, *call, 2)
    gelu_low, proj_far = lax.optimization_barrier((gelu_low, proj_far))
    proj_old = swap(proj_far, "rep", reps, 1)
    block_out = (
        resid + jnp.dot(gelu_low, w_proj, preferred_element_type=F32) + bias_proj
    ).astype(BF16)
    gelu_low, block_out = lax.optimization_barrier((gelu_low, block_out))
    proj_keep, proj_send = grad_proj(gelu_low, cotangent, *call, 2, proj_old)
    proj_keep, proj_send, cotangent = lax.optimization_barrier((proj_keep, proj_send, cotangent))
    proj_held = reduce_chips(proj_keep, proj_send, 2)

    grad_out = cotangent.astype(F32)
    d_proj_bias = column_sum(cotangent)
    grad_gelu = jnp.einsum("td,fd->tf", cotangent, w_proj, preferred_element_type=F32)
    _, gelu_pull = jax.vjp(gelu_tanh, pre_act)
    grad_pre = gelu_pull(grad_gelu)[0].astype(BF16)
    d_fc_bias = column_sum(grad_pre)
    grad_norm_two = jnp.einsum("tf,df->td", grad_pre, w_fc, preferred_element_type=F32)
    _, norm_pull_two = jax.vjp(norm_scale, resid, gain_two)
    grad_resid_norm, d_ln2_gain = norm_pull_two(grad_norm_two)
    d_ln2_bias = jnp.sum(grad_norm_two, axis=0)
    grad_resid = grad_out + grad_resid_norm
    grad_branch = grad_resid.astype(BF16)
    d_out_bias = column_sum(grad_branch)
    fc_far = grad_two(norm_two, grad_pre, attended, grad_branch, *call, 4)
    grad_branch, fc_far, proj_held = lax.optimization_barrier((grad_branch, fc_far, proj_held))
    fc_old = swap(fc_far, "rep", reps, 1)
    grad_attended = jnp.einsum(
        "te,de->td", grad_branch, w_out, preferred_element_type=F32
    ).astype(BF16)
    grad_attended, fc_old = lax.optimization_barrier((grad_attended, fc_old))
    fc_keep, fc_send = grad_two(norm_two, grad_pre, attended, grad_branch, *call, 4, fc_old)
    fc_keep, fc_send, grad_attended = lax.optimization_barrier((fc_keep, fc_send, grad_attended))
    fc_held = reduce_chips(fc_keep, fc_send, 4)
    proj_piece = reduce_shard(proj_held)
    heads_one = attend_backward(qkv, seg_row, grad_attended, lse_one, 0, 4)
    heads_one, proj_piece = lax.optimization_barrier((heads_one, proj_piece))
    one_far = grad_heads(norm_one, heads_one, *call, 2)
    one_far, grad_attended = lax.optimization_barrier((one_far, grad_attended))
    one_old = swap(one_far, "rep", reps, 1)
    heads_two = attend_backward(qkv, seg_row, grad_attended, lse_two, 4, 2)
    heads_two, one_old, fc_held = lax.optimization_barrier((heads_two, one_old, fc_held))
    two_far = grad_heads(norm_one, heads_two, *call, 4)
    two_old = swap(two_far, "rep", reps, 1)
    norm_one, two_far = lax.optimization_barrier((norm_one, two_far))
    one_keep, one_send = grad_heads(norm_one, heads_one, *call, 2, one_old)
    two_keep, two_send = grad_heads(norm_one, heads_two, *call, 4, two_old)
    heads_one, heads_two, one_send, two_send = lax.optimization_barrier(
        (heads_one, heads_two, one_send, two_send)
    )
    two_piece = reduce_shard(reduce_chips(two_keep, two_send, 4))
    one_piece = reduce_shard(reduce_chips(one_keep, one_send, 2))
    fc_piece = reduce_shard(fc_held)
    two_parts = across_cores(across_chips(two_piece, 2))
    d_qkv_weight = settle_heads(every_owner(one_piece), two_parts, spots, pieces)
    d_fc_weight, d_out_weight = settle(
        every_owner(fc_piece), (fc_weight.shape[1], width), pieces
    )
    (d_proj_weight,) = settle(every_owner(proj_piece), (width,), pieces)

    grad_queries, grad_keys, grad_values = [
        jnp.concatenate([one, two], axis=1) for one, two in zip(heads_one, heads_two)
    ]
    d_query_bias = column_sum(grad_queries)
    d_value_bias = column_sum(grad_values)
    grad_qkv = jnp.concatenate([grad_queries, grad_keys, grad_values], axis=1)
    grad_norm_one = jnp.einsum("te,de->td", grad_qkv, w_qkv, preferred_element_type=F32)
    _, norm_pull_one = jax.vjp(norm_scale, inputs, gain_one)
    grad_input_norm, d_ln1_gain = norm_pull_one(grad_norm_one)
    d_ln1_bias = jnp.sum(grad_norm_one, axis=0)
    input_grad = (grad_resid + grad_input_norm).astype(BF16)

    small_grads = jnp.stack(
        [
            d_ln1_gain,
            d_ln1_bias,
            d_query_bias,
            d_value_bias,
            d_out_bias,
            d_ln2_gain,
            d_ln2_bias,
            d_proj_bias,
        ]
        + [d_fc_bias[i * width : (i + 1) * width] for i in range(d_fc_bias.shape[0] // width)]
    )
    for axis, size in (("rep", reps), ("shard", shards)):
        mask = 1
        while mask < size:
            small_grads = small_grads + swap(small_grads, axis, size, mask)
            mask *= 2
    mine = lax.dynamic_slice(small_grads[:8], (0, spot_z * shard_rows), (8, shard_rows))
    fc_rows = fc_bias.shape[0]
    d_fc_bias = lax.dynamic_slice(small_grads[8:].reshape(-1), (spot_z * fc_rows,), (fc_rows,))
    return (
        block_out,
        input_grad,
        mine[0],
        mine[1],
        d_qkv_weight,
        mine[2],
        mine[3],
        d_out_weight,
        mine[4],
        mine[5],
        mine[6],
        d_fc_weight,
        d_fc_bias,
        d_proj_weight,
        mine[7],
    )


def solution(mesh):
    tokens = P(("rep", "shard"), None)
    flat = P("shard")
    rows = P("shard", None)
    in_specs = (
        tokens,
        tokens,
        tokens,
        flat,
        flat,
        rows,
        flat,
        flat,
        rows,
        flat,
        flat,
        flat,
        rows,
        flat,
        rows,
        flat,
    )
    out_specs = (
        tokens,
        tokens,
        flat,
        flat,
        rows,
        flat,
        flat,
        rows,
        flat,
        flat,
        flat,
        rows,
        flat,
        rows,
        flat,
    )
    body = functools.partial(shards_of, mesh.shape["rep"], mesh.shape["shard"])
    return jax.shard_map(
        body, mesh=mesh, in_specs=in_specs, out_specs=out_specs, check_vma=False
    )
```

```python
import functools
import math

import jax
import jax.numpy as jnp
from jax import lax
from jax.experimental import pallas as pl
from jax.experimental.pallas import tpu as pltpu
from jax.sharding import PartitionSpec as P

HEADS = 12
HEAD_DIM = 64
LOG2E = math.log2(math.e)
NEG = -1e30
BF16 = jnp.bfloat16
F32 = jnp.float32
VMEM_LIMIT = 56 << 20
SMALL_COST = pl.CostEstimate(flops=10**6, bytes_accessed=10**5, transcendentals=0)


def dot_nt(a, b):
    return lax.dot_general(a, b, (((1,), (1,)), ((), ())), preferred_element_type=F32)


def dot_nn(a, b):
    return lax.dot_general(a, b, (((1,), (0,)), ((), ())), preferred_element_type=F32)


def dot_tn(a, b):
    return lax.dot_general(a, b, (((0,), (0,)), ((), ())), preferred_element_type=F32)


def params():
    return pltpu.CompilerParams(vmem_limit_bytes=VMEM_LIMIT)


def swap(value, axis, size, mask):
    return lax.ppermute(value, axis, [(i, i ^ mask) for i in range(size)])


def allowed_block(seg_col, seg_row, block, rows):
    keys = (block + 1) * rows
    same = seg_col[:keys, :] == seg_row[:, block * rows : keys]
    causal = lax.broadcasted_iota(jnp.int32, (rows, rows), 0) <= lax.broadcasted_iota(
        jnp.int32, (rows, rows), 1
    )
    if block == 0:
        return same & causal
    return jnp.concatenate([same[: keys - rows], same[keys - rows :] & causal], axis=0)


def attend_kernel(rows, seg_col, seg_row, q_ref, k_ref, v_ref, o_ref, lse_ref):
    length = q_ref.shape[0]
    lane = lax.broadcasted_iota(jnp.int32, (1, 128), 1)
    scale = HEAD_DIM ** (-0.5) * LOG2E
    v_turned = v_ref[...].T
    for block in range(length // rows):
        keys = (block + 1) * rows
        here = slice(block * rows, keys)
        q = q_ref[here, :]
        k = k_ref[:keys, :]
        allowed = allowed_block(seg_col, seg_row, block, rows)
        parts = []
        for head in range(2):
            mine = (lane < 64) if head == 0 else (lane >= 64)
            q_head = jnp.where(mine, q, jnp.zeros_like(q))
            scores = jnp.where(allowed, dot_nt(k, q_head), NEG)
            highest = jnp.max(scores, axis=0, keepdims=True)
            expo = jnp.exp2((scores - highest) * scale)
            summed = jnp.sum(expo, axis=0, keepdims=True)
            v_head = v_turned[head * 64 : (head + 1) * 64, :keys]
            parts.append(dot_nn(v_head, expo.astype(BF16)) * (1.0 / summed))
            lse_ref[head, :, here] = jnp.broadcast_to(
                highest * scale + jnp.log2(summed), (8, rows)
            )
        o_ref[here, :] = jnp.concatenate(parts, axis=0).T.astype(BF16)


def head_specs(length, start):
    groups = HEADS // 2
    return [
        pl.BlockSpec((length, 1), lambda h: (0, 0)),
        pl.BlockSpec((1, length), lambda h: (0, 0)),
        pl.BlockSpec((length, 128), lambda h: (0, start + h)),
        pl.BlockSpec((length, 128), lambda h: (0, groups + start + h)),
        pl.BlockSpec((length, 128), lambda h: (0, 2 * groups + start + h)),
    ]


def attend_forward(qkv, segment, start, count):
    length = qkv.shape[0]
    rows = length // 2
    return pl.pallas_call(
        functools.partial(attend_kernel, rows),
        grid=(count,),
        in_specs=head_specs(length, start),
        out_specs=[
            pl.BlockSpec((length, 128), lambda h: (0, h)),
            pl.BlockSpec((2, 8, length), lambda h: (h, 0, 0)),
        ],
        out_shape=[
            jax.ShapeDtypeStruct((length, 128 * count), BF16),
            jax.ShapeDtypeStruct((2 * count, 8, length), F32),
        ],
        compiler_params=params(),
        cost_estimate=SMALL_COST,
        name="attend_forward",
    )(segment.reshape(length, 1), segment.reshape(1, length), qkv, qkv, qkv)


def attend_back_kernel(
    rows, seg_col, seg_row, q_ref, k_ref, v_ref, g_ref, lse_ref, dq_ref, dk_ref, dv_ref, sums_ref, dk_sum, dv_sum
):
    length = q_ref.shape[0]
    lane = lax.broadcasted_iota(jnp.int32, (1, 128), 1)
    scale = HEAD_DIM ** (-0.5) * LOG2E
    blocks = length // rows
    for block in reversed(range(blocks)):
        keys = (block + 1) * rows
        here = slice(block * rows, keys)
        q = q_ref[here, :]
        g = g_ref[here, :]
        k = k_ref[:keys, :]
        v = v_ref[:keys, :]
        allowed = allowed_block(seg_col, seg_row, block, rows)
        dq = dk = dv = None
        for head in range(2):
            mine = (lane < 64) if head == 0 else (lane >= 64)
            q_head = jnp.where(mine, q, jnp.zeros_like(q))
            g_head = jnp.where(mine, g, jnp.zeros_like(g))
            scores = dot_nt(k, q_head) * scale - lse_ref[head, 0:1, here]
            probs = jnp.exp2(jnp.where(allowed, scores, NEG))
            grad_probs = dot_nt(v, g_head)
            inner = jnp.sum(probs * grad_probs, axis=0, keepdims=True)
            grad_scores = (probs * (grad_probs - inner)).astype(BF16)
            dv_head = dot_nn(probs.astype(BF16), g_head)
            dk_head = dot_nn(grad_scores, q_head)
            dq_head = dot_tn(grad_scores, k)
            if head == 0:
                dq, dk, dv = dq_head, dk_head, dv_head
            else:
                dq, dk, dv = jnp.where(lane < 64, dq, dq_head), dk + dk_head, dv + dv_head
        dq_ref[here, :] = (dq * HEAD_DIM ** (-0.5)).astype(BF16)
        if block == blocks - 1:
            dk_sum[...] = dk
            dv_sum[...] = dv
        else:
            dk_sum[:keys, :] += dk
            dv_sum[:keys, :] += dv
    dk_ref[...] = (dk_sum[...] * HEAD_DIM ** (-0.5)).astype(BF16)
    dv_ref[...] = dv_sum[...].astype(BF16)
    sums_ref[0:1, :] = jnp.sum(dq_ref[...].astype(F32), axis=0, keepdims=True)
    sums_ref[1:2, :] = jnp.sum(dv_ref[...].astype(F32), axis=0, keepdims=True)
    sums_ref[2:8, :] = jnp.zeros((6, 128), F32)


def attend_backward(qkv, segment, grad, lse, start, count):
    length = qkv.shape[0]
    rows = length // 2
    return pl.pallas_call(
        functools.partial(attend_back_kernel, rows),
        grid=(count,),
        in_specs=head_specs(length, start)
        + [
            pl.BlockSpec((length, 128), lambda h: (0, start + h)),
            pl.BlockSpec((2, 8, length), lambda h: (h, 0, 0)),
        ],
        out_specs=[pl.BlockSpec((length, 128), lambda h: (0, h))] * 3
        + [pl.BlockSpec((8, 128), lambda h: (0, h))],
        out_shape=[jax.ShapeDtypeStruct((length, 128 * count), BF16)] * 3
        + [jax.ShapeDtypeStruct((8, 128 * count), F32)],
        scratch_shapes=[pltpu.VMEM((length, 128), F32)] * 2,
        compiler_params=params(),
        cost_estimate=SMALL_COST,
        name="attend_backward",
    )(segment.reshape(length, 1), segment.reshape(1, length), qkv, qkv, qkv, grad, lse)


def position_to_rel(slot, pieces, first):
    if pieces == 4 and first == 2:
        return (slot & 1) * 2 + slot // 2
    return slot


def place_rows(total, out_ref, spots, pieces, first, by_shard):
    shards_here, rows = out_ref.shape[1:3]
    for slot in range(pieces):
        piece = position_to_rel(slot, pieces, first) ^ spots[1]
        for rel_z in range(shards_here):
            owner = 0 if by_shard else rel_z ^ spots[2]
            start = pl.multiple_of((owner * pieces + piece) * rows, 16)
            out_ref[slot, rel_z] = total[pl.ds(start, rows), :].astype(BF16)


def grad_kernel(pieces, first, by_shard, spots, x_ref, far_y, near_y, far_ref, near_ref, total):
    for y_ref, out_ref in ((far_y, far_ref), (near_y, near_ref)):
        total[...] = dot_tn(x_ref[...], y_ref[...])
        place_rows(total, out_ref, spots, pieces, first, by_shard)


def grad_heads_kernel(pieces, first, extra, spots, x_ref, *rest):
    far_y, near_y = rest[:3], rest[3:6]
    far_ref, near_ref, total = rest[-3:]
    for side, (y_refs, out_ref) in enumerate(((far_y, far_ref), (near_y, near_ref))):
        joined = jnp.concatenate([y_ref[...] for y_ref in y_refs], axis=1)
        columns = joined.shape[1]
        total[:, :columns] = dot_tn(x_ref[...], joined)
        if extra:
            total[:, columns:] = dot_tn(rest[6][...], rest[7 + side][...])
        place_rows(total, out_ref, spots, pieces, first, False)


def grad_call(kernel, grid, in_specs, operands, out_spec, shape, scratch, spots):
    length, rows = operands[0].shape[0], shape[0] * shape[1] * shape[2]
    return pl.pallas_call(
        kernel,
        grid_spec=pltpu.PrefetchScalarGridSpec(
            num_scalar_prefetch=1,
            grid=grid,
            in_specs=in_specs,
            out_specs=[out_spec] * 2,
            scratch_shapes=[pltpu.VMEM(scratch, F32)],
        ),
        out_shape=[jax.ShapeDtypeStruct(shape, BF16)] * 2,
        compiler_params=params(),
        cost_estimate=SMALL_COST,
        name="weight_grad",
    )(spots, *operands)


def grad_proj(x, y, spots, shards, pieces, first):
    length, rows_all = x.shape
    half = y.shape[1] // 2
    rows = rows_all // (shards * pieces)
    return grad_call(
        functools.partial(grad_kernel, pieces, first, True),
        (shards,),
        [
            pl.BlockSpec((length, rows_all // shards), lambda i, s: (0, i ^ s[2])),
            pl.BlockSpec((length, half), lambda i, s: (0, 1 - s[0])),
            pl.BlockSpec((length, half), lambda i, s: (0, s[0])),
        ],
        [x, y, y],
        pl.BlockSpec((pieces, 1, rows, half), lambda i, s: (0, i, 0, 0)),
        (pieces, shards, rows, half),
        (rows_all // shards, half),
        spots,
    )


def grad_fc(x, y, spots, shards, pieces, first):
    length, rows_all = x.shape
    tile = rows_all // 2
    half = y.shape[1] // 2
    tiles = half // tile
    rows = rows_all // (shards * pieces)
    return grad_call(
        functools.partial(grad_kernel, pieces, first, False),
        (tiles,),
        [
            pl.BlockSpec((length, rows_all), lambda i, s: (0, 0)),
            pl.BlockSpec((length, tile), lambda i, s: (0, (1 - s[0]) * tiles + i)),
            pl.BlockSpec((length, tile), lambda i, s: (0, s[0] * tiles + i)),
        ],
        [x, y, y],
        pl.BlockSpec((pieces, shards, rows, tile), lambda i, s: (0, 0, 0, i)),
        (pieces, shards, rows, half),
        (rows_all, tile),
        spots,
    )


def grad_heads(x, grads, spots, shards, pieces, first, extra=()):
    length, rows_all = x.shape
    half = grads[0].shape[1] // 2
    rows = rows_all // (shards * pieces)
    columns = 3 * half
    far = pl.BlockSpec((length, half), lambda i, s: (0, 1 - s[0]))
    near = pl.BlockSpec((length, half), lambda i, s: (0, s[0]))
    in_specs = [pl.BlockSpec((length, rows_all), lambda i, s: (0, 0))] + [far] * 3 + [near] * 3
    operands = [x, *grads, *grads]
    if extra:
        half2 = extra[1].shape[1] // 2
        columns += half2
        in_specs += [
            pl.BlockSpec((length, rows_all), lambda i, s: (0, 0)),
            pl.BlockSpec((length, half2), lambda i, s: (0, 1 - s[0])),
            pl.BlockSpec((length, half2), lambda i, s: (0, s[0])),
        ]
        operands += [extra[0], extra[1], extra[1]]
    shape = (pieces, shards, rows, columns)
    return grad_call(
        functools.partial(grad_heads_kernel, pieces, first, bool(extra)),
        (1,),
        in_specs,
        operands,
        pl.BlockSpec(shape, lambda i, s: (0, 0, 0, 0)),
        shape,
        (rows_all, columns),
        spots,
    )


def piece_copies(full_ref, own_ref, parts, column, spots, sems, shards, pieces):
    core, spot_u, spot_z = spots[0], spots[1], spots[2]
    shard_rows = own_ref.shape[0]
    half = own_ref.shape[1] // 2
    rows = shard_rows // pieces
    copies = [
        pltpu.make_async_copy(
            own_ref,
            full_ref.at[pl.ds(pl.multiple_of(spot_z * shard_rows, 16), shard_rows), :],
            sems.at[0],
        )
    ]
    for index, part in enumerate(parts):
        side = core if index < pieces else 1 - core
        piece = spot_u ^ (index % pieces)
        for step in range(1, shards):
            start = pl.multiple_of((spot_z ^ step) * shard_rows + piece * rows, 16)
            copies.append(
                pltpu.make_async_copy(
                    part.at[step - 1, pl.ds(0, rows), pl.ds(column, half)],
                    full_ref.at[pl.ds(start, rows), pl.ds(pl.multiple_of(side * half, 128), half)],
                    sems.at[len(copies)],
                )
            )
    return copies


def at_first(work):
    @pl.when(pl.program_id(0) == 0)
    def _():
        work()


def start_all(copies):
    for copy in copies:
        copy.start()


def wait_all(copies):
    for copy in copies:
        copy.wait()


def row_call(kernel, name, steps, spots, rows_in, whole_in, parts_in, outs, sem_sets, sem_count):
    length = rows_in[0].shape[0]
    rows = length // steps

    def by_rows(width):
        return pl.BlockSpec((rows, width), lambda i, s: (i, 0))

    def whole(shape):
        return pl.BlockSpec(shape, lambda i, s: (0,) * len(shape))

    anywhere = pl.BlockSpec(memory_space=pl.ANY)
    return pl.pallas_call(
        kernel,
        grid_spec=pltpu.PrefetchScalarGridSpec(
            num_scalar_prefetch=1,
            grid=(steps,),
            in_specs=[by_rows(item.shape[1]) for item in rows_in]
            + [whole(item.shape) for item in whole_in]
            + [anywhere] * len(parts_in),
            out_specs=[
                by_rows(shape[1]) if tiled else whole(shape) for shape, _, tiled in outs
            ],
            scratch_shapes=[pltpu.SemaphoreType.DMA((sem_count,))] * sem_sets,
        ),
        out_shape=[jax.ShapeDtypeStruct(shape, dtype) for shape, dtype, _ in outs],
        compiler_params=params(),
        cost_estimate=SMALL_COST,
        name=name,
    )(spots, *rows_in, *whole_in, *parts_in)


def normed_rows(values):
    center = values - jnp.mean(values, axis=-1, keepdims=True)
    scale = lax.rsqrt(jnp.mean(center * center, axis=-1, keepdims=True) + 1e-05)
    return center * scale, scale


def norm_back(grad, values, gain):
    normed, scale = normed_rows(values)
    scaled = grad * gain
    inner = scaled - jnp.mean(scaled, axis=-1, keepdims=True)
    inner = inner - normed * jnp.mean(scaled * normed, axis=-1, keepdims=True)
    return scale * inner, normed


GAIN_ONE, SHIFT_ONE, BIAS_Q, BIAS_V, BIAS_OUT, GAIN_TWO, SHIFT_TWO, BIAS_PROJ = range(8)
GELU_SCALE = math.sqrt(2 / math.pi)
GELU_CUBE = 0.044715


def row_of(ref, index):
    return ref[index : index + 1, :]


def qkv_kernel(shards, pieces, spots, x_ref, vec_ref, own_ref, *rest):
    parts = rest[: 2 * pieces]
    w_ref, norm_ref, qkv_ref, sems = rest[2 * pieces :]
    copies = piece_copies(w_ref, own_ref, parts, 0, spots, sems, shards, pieces)
    at_first(lambda: start_all(copies))
    normed, _ = normed_rows(x_ref[...].astype(F32))
    norm_one = (normed * row_of(vec_ref, GAIN_ONE) + row_of(vec_ref, SHIFT_ONE)).astype(BF16)
    norm_ref[...] = norm_one
    at_first(lambda: wait_all(copies))
    width = norm_one.shape[1]
    for kind, row in enumerate((BIAS_Q, None, BIAS_V)):
        here = slice(kind * width, (kind + 1) * width)
        value = dot_nn(norm_one, w_ref[:, here])
        if row is not None:
            value = value + row_of(vec_ref, row)
        qkv_ref[:, here] = value.astype(BF16)


def fc_kernel(shards, pieces, spots, att_ref, x_ref, vec_ref, bias_ref, own_out, own_fc, *rest):
    parts = rest[: 2 * pieces]
    wo_ref, wf_ref, resid_ref, norm_ref, pre_ref, gelu_ref, sems_out, sems_fc = rest[2 * pieces :]
    half = own_out.shape[1] // 2
    copies_out = piece_copies(wo_ref, own_out, parts, 0, spots, sems_out, shards, pieces)
    copies_fc = piece_copies(wf_ref, own_fc, parts, half, spots, sems_fc, shards, pieces)
    at_first(lambda: start_all(copies_out + copies_fc))
    at_first(lambda: wait_all(copies_out))
    resid = x_ref[...].astype(F32) + dot_nn(att_ref[...], wo_ref[...]) + row_of(vec_ref, BIAS_OUT)
    resid_ref[...] = resid
    normed, _ = normed_rows(resid)
    norm_two = (normed * row_of(vec_ref, GAIN_TWO) + row_of(vec_ref, SHIFT_TWO)).astype(BF16)
    norm_ref[...] = norm_two
    at_first(lambda: wait_all(copies_fc))
    width = norm_two.shape[1]
    for tile in range(pre_ref.shape[1] // width):
        here = slice(tile * width, (tile + 1) * width)
        pre = dot_nn(norm_two, wf_ref[:, here]) + bias_ref[:, here]
        pre_ref[:, here] = pre
        curve = jnp.tanh(GELU_SCALE * (pre + GELU_CUBE * pre * pre * pre))
        gelu_ref[:, here] = (0.5 * pre * (1.0 + curve)).astype(BF16)


def proj_kernel(shards, pieces, spots, gelu_ref, resid_ref, vec_ref, own_ref, *rest):
    parts = rest[: 2 * pieces]
    w_ref, out_ref, sems = rest[2 * pieces :]
    copies = piece_copies(w_ref, own_ref, parts, 0, spots, sems, shards, pieces)
    at_first(lambda: start_all(copies))
    at_first(lambda: wait_all(copies))
    out_ref[...] = (
        resid_ref[...] + dot_nn(gelu_ref[...], w_ref[...]) + row_of(vec_ref, BIAS_PROJ)
    ).astype(BF16)


def clear_first(ref):
    def work():
        ref[...] = jnp.zeros_like(ref)

    at_first(work)


def column_sums(values):
    return jnp.sum(values, axis=0, keepdims=True)


def back_gelu_kernel(spots, g_ref, pre_ref, w_ref, grad_ref, fc_sums, proj_sums):
    clear_first(fc_sums)
    clear_first(proj_sums)
    grad = g_ref[...]
    proj_sums[0:1, :] += column_sums(grad.astype(F32))
    width = grad.shape[1]
    for tile in range(pre_ref.shape[1] // width):
        here = slice(tile * width, (tile + 1) * width)
        pre = pre_ref[:, here]
        square = pre * pre
        curve = jnp.tanh(GELU_SCALE * (pre + GELU_CUBE * square * pre))
        slope = 0.5 * (1.0 + curve) + (0.5 * GELU_SCALE) * pre * (1.0 - curve * curve) * (
            1.0 + (3.0 * GELU_CUBE) * square
        )
        grad_pre = (dot_nt(grad, w_ref[here, :]) * slope).astype(BF16)
        grad_ref[:, here] = grad_pre
        fc_sums[0:1, here] += column_sums(grad_pre.astype(F32))


def back_norm_kernel(
    spots, pre_ref, resid_ref, g_ref, vec_ref, wf_ref, wo_ref, sum_ref, low_ref, att_ref, sums_ref
):
    clear_first(sums_ref)
    grad = dot_nt(pre_ref[...], wf_ref[...])
    inner, normed = norm_back(grad, resid_ref[...], row_of(vec_ref, GAIN_TWO))
    total = g_ref[...].astype(F32) + inner
    sum_ref[...] = total
    low = total.astype(BF16)
    low_ref[...] = low
    sums_ref[0:1, :] += column_sums(low.astype(F32))
    sums_ref[1:2, :] += column_sums(grad * normed)
    sums_ref[2:3, :] += column_sums(grad)
    att_ref[...] = dot_nt(low, wo_ref[...]).astype(BF16)


def settle_kernel(pieces, every_ref, *outs):
    rows = every_ref.shape[1]
    for index in range(2 * pieces):
        piece, core = index // 2, index % 2
        column = 0
        for out_ref in outs:
            half = out_ref.shape[1] // 2
            out_ref[piece * rows : (piece + 1) * rows, core * half : (core + 1) * half] = every_ref[
                index, :, column : column + half
            ].astype(F32)
            column += half


def settle(every, widths, pieces):
    rows = every.shape[1]
    whole = pl.BlockSpec(memory_space=pltpu.VMEM)
    return pl.pallas_call(
        functools.partial(settle_kernel, pieces),
        in_specs=[whole],
        out_specs=[whole] * len(widths),
        out_shape=[jax.ShapeDtypeStruct((rows * pieces, width), F32) for width in widths],
        compiler_params=params(),
        name="settle",
    )(every)


def settle_last_kernel(pieces, wide, spots, *rest):
    parts, qkv_ref, out_ref = rest[: 2 * pieces], rest[-2], rest[-1]
    core, spot_u = spots[0], spots[1]
    rows = parts[0].shape[0]
    width = out_ref.shape[1]
    narrow = width // 2 - wide
    for index, part in enumerate(parts):
        side = core if index < pieces else 1 - core
        here = pl.ds(pl.multiple_of((spot_u ^ (index % pieces)) * rows, 16), rows)
        source = 0
        for base, size in ((0, wide), (2 * wide, narrow)):
            for kind in range(3):
                column = pl.multiple_of(kind * width + base + side * size, 128)
                qkv_ref[here, pl.ds(column, size)] = part[:, source : source + size].astype(F32)
                source += size
            if base == 0:
                column = pl.multiple_of(side * (width // 2), 128)
                out_ref[here, pl.ds(column, width // 2)] = part[
                    :, source : source + width // 2
                ].astype(F32)
                source += width // 2


def settle_last(parts, spots, pieces, wide, width):
    rows = parts[0].shape[0]
    whole = pl.BlockSpec(memory_space=pltpu.VMEM)
    return pl.pallas_call(
        functools.partial(settle_last_kernel, pieces, wide),
        in_specs=[pl.BlockSpec(memory_space=pltpu.SMEM)] + [whole] * (2 * pieces),
        out_specs=[whole] * 2,
        out_shape=[
            jax.ShapeDtypeStruct((rows * pieces, columns), F32) for columns in (3 * width, width)
        ],
        compiler_params=params(),
        name="settle_last",
    )(spots, *parts)


def back_product(w_ref, grads, start):
    total = None
    width = w_ref.shape[0]
    for kind, grad in enumerate(grads):
        first = kind * width + start
        part = dot_nt(grad[...], w_ref[:, first : first + grad.shape[1]])
        total = part if total is None else total + part
    return total


def back_one_kernel(w_ref, q_ref, k_ref, v_ref, out_ref):
    out_ref[...] = back_product(w_ref, (q_ref, k_ref, v_ref), 0)


def back_two_kernel(
    start, w_ref, q_ref, k_ref, v_ref, part_ref, x_ref, vec_ref, resid_ref, out_ref, sums_ref
):
    clear_first(sums_ref)
    grad = part_ref[...] + back_product(w_ref, (q_ref, k_ref, v_ref), start)
    inner, normed = norm_back(grad, x_ref[...].astype(F32), row_of(vec_ref, GAIN_ONE))
    out_ref[...] = (resid_ref[...] + inner).astype(BF16)
    sums_ref[0:1, :] += column_sums(grad * normed)
    sums_ref[1:2, :] += column_sums(grad)


def back_one(w, grads):
    length, width = grads[0].shape[0], w.shape[0]
    rows = length // 4
    return pl.pallas_call(
        back_one_kernel,
        grid=(4,),
        in_specs=[pl.BlockSpec(w.shape, lambda i: (0, 0))]
        + [pl.BlockSpec((rows, grads[0].shape[1]), lambda i: (i, 0))] * 3,
        out_specs=pl.BlockSpec((rows, width), lambda i: (i, 0)),
        out_shape=jax.ShapeDtypeStruct((length, width), F32),
        compiler_params=params(),
        cost_estimate=SMALL_COST,
        name="back_one",
    )(w, *grads)


def back_two(w, grads, start, part, values, vectors, resid):
    length, width = values.shape
    rows = length // 4
    block = pl.BlockSpec((rows, width), lambda i: (i, 0))
    return pl.pallas_call(
        functools.partial(back_two_kernel, start),
        grid=(4,),
        in_specs=[pl.BlockSpec(w.shape, lambda i: (0, 0))]
        + [pl.BlockSpec((rows, grads[0].shape[1]), lambda i: (i, 0))] * 3
        + [block, block, pl.BlockSpec((8, width), lambda i: (0, 0)), block],
        out_specs=[block, pl.BlockSpec((8, width), lambda i: (0, 0))],
        out_shape=[
            jax.ShapeDtypeStruct((length, width), BF16),
            jax.ShapeDtypeStruct((8, width), F32),
        ],
        compiler_params=params(),
        cost_estimate=SMALL_COST,
        name="back_two",
    )(w, *grads, part, values, vectors, resid)


def pack_kernel(ln1_ref, one_ref, two_ref, resid_ref, proj_ref, fc_ref, out_ref):
    width = out_ref.shape[1]
    wide = one_ref.shape[1]
    out_ref[0:2, :] = ln1_ref[0:2, :]
    out_ref[2:4, :wide] = one_ref[0:2, :]
    out_ref[2:4, wide:] = two_ref[0:2, :]
    out_ref[4:7, :] = resid_ref[0:3, :]
    out_ref[7:8, :] = proj_ref[0:1, :]
    count = fc_ref.shape[1] // width
    for index in range(count):
        out_ref[8 + index : 9 + index, :] = fc_ref[0:1, index * width : (index + 1) * width]
    out_ref[8 + count : 16, :] = jnp.zeros((8 - count, width), F32)


def pack(*sums):
    whole = pl.BlockSpec(memory_space=pltpu.VMEM)
    return pl.pallas_call(
        pack_kernel,
        in_specs=[whole] * len(sums),
        out_specs=whole,
        out_shape=jax.ShapeDtypeStruct((16, sums[0].shape[1]), F32),
        compiler_params=params(),
        cost_estimate=SMALL_COST,
        name="pack",
    )(*sums)


def shards_of(
    reps,
    shards,
    hidden_in,
    segment,
    cotangent,
    ln1_gain,
    ln1_bias,
    qkv_weight,
    query_bias,
    value_bias,
    out_weight,
    out_bias,
    ln2_gain,
    ln2_bias,
    fc_weight,
    fc_bias,
    proj_weight,
    proj_bias,
):
    width = hidden_in.shape[1]
    shard_rows = qkv_weight.shape[0]
    pieces = 4 if shard_rows % 64 == 0 and reps % 8 == 0 else 2
    rep = lax.axis_index("rep")
    spot_z = lax.axis_index("shard")
    core = rep & 1
    spot_u = (rep >> 1) & (pieces - 1)
    spots = jnp.stack([core, spot_u, spot_z]).astype(jnp.int32)

    def own_piece(weight):
        rows, half = weight.shape[0] // pieces, weight.shape[1] // 2
        return lax.dynamic_slice(weight, (spot_u * rows, core * half), (rows, half))

    def across_chips(part, first):
        if pieces == 2:
            return [part, swap(part, "rep", reps, 2)]
        second = 6 - first
        by_first = swap(part, "rep", reps, first)
        by_second = swap(part, "rep", reps, second)
        by_both = swap(part, "rep", reps, 6)
        if first == 2:
            return [part, by_first, by_second, by_both]
        return [part, by_second, by_first, by_both]

    def across_cores(parts):
        return parts + [swap(part, "rep", reps, 1) for part in parts]

    def along_shard(piece):
        return [swap(piece, "shard", shards, step) for step in range(1, shards)]

    piece_rows = shard_rows // pieces
    flat = [
        ln1_gain,
        ln1_bias,
        query_bias,
        value_bias,
        out_bias,
        ln2_gain,
        ln2_bias,
        proj_bias,
        fc_bias,
    ]
    flat_size = sum(item.shape[0] for item in flat)
    qkv_half = qkv_weight.shape[1] // 2
    small_rows = -(-flat_size // qkv_half)
    small = jnp.zeros((small_rows * qkv_half,), BF16)
    offset = 0
    for item in flat:
        size = item.shape[0]
        small = small + jnp.pad(item, (offset, small.shape[0] - offset - size))
        offset += size
    small = small.reshape(small_rows, qkv_half)
    tie = lax.optimization_barrier
    qkv_payload = jnp.concatenate(
        [own_piece(qkv_weight), jnp.pad(small, ((0, 16 - small_rows), (0, 0)))], axis=0
    )
    second_payload = jnp.concatenate([own_piece(out_weight), own_piece(fc_weight)], axis=1)
    qkv_slots = along_shard(qkv_payload)
    qkv_slots, second_payload = tie((qkv_slots, second_payload))
    qkv_parts = across_chips(jnp.stack([slot[:piece_rows] for slot in qkv_slots]), 2)
    second_slots = along_shard(second_payload)
    qkv_parts, proj_piece = tie((qkv_parts, own_piece(proj_weight)))
    qkv_parts = across_cores(qkv_parts)
    second_stack, qkv_parts, proj_piece = tie((jnp.stack(second_slots), qkv_parts, proj_piece))
    second_parts = across_chips(second_stack, 2)
    proj_slots = along_shard(proj_piece)

    rows_of = [small] + [slot[piece_rows : piece_rows + small_rows] for slot in qkv_slots]
    ordered = []
    for index in range(shards):
        total = jnp.zeros_like(rows_of[0])
        for step, value in enumerate(rows_of):
            total = jnp.where((spot_z ^ step) == index, value, total)
        ordered.append(total.reshape(-1)[:flat_size])
    vectors = jnp.stack(ordered).astype(F32)
    bias_fc = vectors[:, 8 * shard_rows :].reshape(1, -1)
    vectors = vectors[:, : 8 * shard_rows].reshape(shards, 8, shard_rows)
    vectors = vectors.transpose(1, 0, 2).reshape(8, width)

    seg_row = segment[0]
    length = hidden_in.shape[0]
    ff = fc_weight.shape[1]
    steps = 4
    sem_count = 1 + 2 * pieces * (shards - 1)
    kernel_of = lambda body: functools.partial(body, shards, pieces)
    w_qkv, norm_one, qkv = row_call(
        kernel_of(qkv_kernel),
        "qkv",
        steps,
        spots,
        [hidden_in],
        [vectors],
        [qkv_weight, *qkv_parts],
        [
            ((width, 3 * width), BF16, False),
            ((length, width), BF16, True),
            ((length, 3 * width), BF16, True),
        ],
        1,
        sem_count,
    )
    attended_one, lse_one = attend_forward(qkv, seg_row, 0, 4)
    attended_one, proj_slots, qkv = tie((attended_one, proj_slots, qkv))
    proj_parts = across_chips(jnp.stack(proj_slots), 4)
    attended_two, lse_two = attend_forward(qkv, seg_row, 4, 2)
    attended_two, second_parts = tie((attended_two, second_parts))
    second_parts = across_cores(second_parts)
    attended = jnp.concatenate([attended_one, attended_two], axis=1)
    w_out, w_fc, resid, norm_two, pre_act, gelu_low = row_call(
        kernel_of(fc_kernel),
        "fc",
        steps,
        spots,
        [attended, hidden_in],
        [vectors, bias_fc],
        [out_weight, fc_weight, *second_parts],
        [
            ((width, width), BF16, False),
            ((width, ff), BF16, False),
            ((length, width), F32, True),
            ((length, width), BF16, True),
            ((length, ff), F32, True),
            ((length, ff), BF16, True),
        ],
        2,
        sem_count,
    )

    half_pieces = pieces // 2

    def summed(near, old):
        return near.astype(F32) + old.astype(F32)

    def sent_part(near, old):
        return summed(near[half_pieces:], old[half_pieces:]).astype(BF16)

    def after_first(near, old, came):
        kept = summed(near[:half_pieces], old[:half_pieces]) + came.astype(F32)
        return kept[0], kept[half_pieces - 1].astype(BF16)

    def second_swap(onward, mask):
        return jnp.zeros_like(onward) if pieces == 2 else swap(onward, "rep", reps, mask)

    def shard_swaps(held):
        low = held.astype(BF16)
        return [swap(low[step], "shard", shards, step) for step in range(1, shards)]

    def shard_total(held, came):
        total = held[0]
        for value in came:
            total = total + value.astype(F32)
        mask = 2 * pieces
        while mask < reps:
            total = total + swap(total.astype(BF16), "rep", reps, mask).astype(F32)
            mask *= 2
        return total.astype(BF16)

    def every_owner(piece):
        return lax.all_gather(piece, "rep", axis=0, tiled=False)[: 2 * pieces]

    call = (spots, shards, pieces)
    first_of = 2 if pieces == 2 else 4
    gelu_low, proj_parts = tie((gelu_low, proj_parts))
    proj_parts = across_cores(proj_parts)
    proj_far, proj_near = grad_proj(gelu_low, cotangent, *call, 2)
    gelu_low, proj_far, proj_near, proj_parts = tie((gelu_low, proj_far, proj_near, proj_parts))
    proj_old = swap(proj_far, "rep", reps, 1)
    w_proj, block_out = row_call(
        kernel_of(proj_kernel),
        "proj",
        steps,
        spots,
        [gelu_low, resid],
        [vectors],
        [proj_weight, *proj_parts],
        [((width * 4, width), BF16, False), ((length, width), BF16, True)],
        1,
        sem_count,
    )
    w_proj, proj_old = tie((w_proj, proj_old))
    proj_send = sent_part(proj_near, proj_old)
    proj_send, w_proj = tie((proj_send, w_proj))
    proj_came = swap(proj_send, "rep", reps, 2)
    grad_pre, fc_sums, proj_sums = row_call(
        back_gelu_kernel,
        "back_gelu",
        steps,
        spots,
        [cotangent, pre_act],
        [w_proj],
        [],
        [((length, ff), BF16, True), ((8, ff), F32, False), ((8, width), F32, False)],
        0,
        0,
    )
    fc_far, fc_near = grad_fc(norm_two, grad_pre, *call, first_of)
    grad_pre, fc_far, fc_near, proj_came = tie((grad_pre, fc_far, fc_near, proj_came))
    fc_old = swap(fc_far, "rep", reps, 1)
    proj_held, proj_onward = after_first(proj_near, proj_old, proj_came)
    grad_pre, proj_onward = tie((grad_pre, proj_onward))
    proj_came = second_swap(proj_onward, 4)
    grad_resid, grad_branch, grad_attended, resid_sums = row_call(
        back_norm_kernel,
        "back_norm",
        steps,
        spots,
        [grad_pre, resid, cotangent],
        [vectors, w_fc, w_out],
        [],
        [
            ((length, width), F32, True),
            ((length, width), BF16, True),
            ((length, width), BF16, True),
            ((8, width), F32, False),
        ],
        0,
        0,
    )
    grad_attended, fc_old = tie((grad_attended, fc_old))
    fc_send = sent_part(fc_near, fc_old)
    grad_attended, fc_send, proj_came = tie((grad_attended, fc_send, proj_came))
    fc_came = swap(fc_send, "rep", reps, first_of)
    *heads_one, sums_one = attend_backward(qkv, seg_row, grad_attended, lse_one, 0, 4)
    heads_one, fc_came, grad_attended, proj_came = tie(
        (heads_one, fc_came, grad_attended, proj_came)
    )
    proj_held = proj_held + proj_came.astype(F32)
    proj_shards = shard_swaps(proj_held)
    fc_held, fc_onward = after_first(fc_near, fc_old, fc_came)
    fc_onward, heads_one = tie((fc_onward, heads_one))
    fc_came = second_swap(fc_onward, 2)
    one_far, one_near = grad_heads(norm_one, heads_one, *call, first_of, (attended, grad_branch))
    heads_one, one_far, one_near, proj_shards = tie((heads_one, one_far, one_near, proj_shards))
    one_old = swap(one_far, "rep", reps, 1)
    proj_piece = shard_total(proj_held, proj_shards)
    proj_piece, heads_one = tie((proj_piece, heads_one))
    part_one = back_one(w_qkv, heads_one)
    part_one, one_old, grad_attended, fc_came = tie((part_one, one_old, grad_attended, fc_came))
    one_send = sent_part(one_near, one_old)
    fc_held = fc_held + fc_came.astype(F32)
    one_send, grad_attended, fc_held = tie((one_send, grad_attended, fc_held))
    one_came = swap(one_send, "rep", reps, first_of)
    fc_shards = shard_swaps(fc_held)
    *heads_two, sums_two = attend_backward(qkv, seg_row, grad_attended, lse_two, 4, 2)
    heads_two, fc_shards = tie((heads_two, fc_shards))
    two_far, two_near = grad_heads(norm_one, heads_two, *call, 2)
    heads_two, two_far, two_near, one_came = tie((heads_two, two_far, two_near, one_came))
    two_old = swap(two_far, "rep", reps, 1)
    one_held, one_onward = after_first(one_near, one_old, one_came)
    fc_piece = shard_total(fc_held, fc_shards)
    two_old, one_onward, heads_two, fc_piece = tie((two_old, one_onward, heads_two, fc_piece))
    one_came = second_swap(one_onward, 2)
    two_send = sent_part(two_near, two_old)
    two_send, heads_two = tie((two_send, heads_two))
    two_came = swap(two_send, "rep", reps, 2)
    input_grad, ln1_sums = back_two(
        w_qkv, heads_two, 128 * 4, part_one, hidden_in, vectors, grad_resid
    )
    small_grads = pack(ln1_sums, sums_one, sums_two, resid_sums, proj_sums, fc_sums)
    masks = [("rep", reps, 1 << i) for i in range(reps.bit_length() - 1)]
    masks += [("shard", shards, 1 << i) for i in range(shards.bit_length() - 1)]

    def vector_step(total, count=1):
        for _ in range(count):
            axis, size, mask = masks.pop(0)
            total = total + swap(total, axis, size, mask)
        return total

    two_came, one_came, small_grads = tie((two_came, one_came, small_grads))
    two_held, two_onward = after_first(two_near, two_old, two_came)
    two_onward, small_grads = tie((two_onward, small_grads))
    two_came = second_swap(two_onward, 4)
    one_held = one_held + one_came.astype(F32)
    small_grads = vector_step(small_grads)
    two_came, one_held, small_grads = tie((two_came, one_held, small_grads))
    last_held = jnp.concatenate([one_held, two_held + two_came.astype(F32)], axis=-1)
    last_shards = shard_swaps(last_held)
    small_grads = vector_step(small_grads, 2)
    last_shards, small_grads = tie((last_shards, small_grads))
    last_parts = across_chips(shard_total(last_held, last_shards), 2)
    small_grads = vector_step(small_grads, len(masks))
    last_parts, small_grads, every_fc, every_proj = tie(
        (last_parts, small_grads, every_owner(fc_piece), every_owner(proj_piece))
    )
    last_parts = across_cores(last_parts)
    (d_fc_weight,) = settle(every_fc, (fc_weight.shape[1],), pieces)
    (d_proj_weight,) = settle(every_proj, (width,), pieces)
    d_qkv_weight, d_out_weight = settle_last(
        last_parts, spots, pieces, heads_one[0].shape[1] // 2, width
    )
    mine = lax.dynamic_slice(small_grads[:8], (0, spot_z * shard_rows), (8, shard_rows))
    fc_rows = fc_bias.shape[0]
    fc_row = small_grads[8 : 8 + ff // width].reshape(-1)
    d_fc_bias = lax.dynamic_slice(fc_row, (spot_z * fc_rows,), (fc_rows,))
    return (
        block_out,
        input_grad,
        mine[0],
        mine[1],
        d_qkv_weight,
        mine[2],
        mine[3],
        d_out_weight,
        mine[4],
        mine[5],
        mine[6],
        d_fc_weight,
        d_fc_bias,
        d_proj_weight,
        mine[7],
    )


def solution(mesh):
    tokens = P(("rep", "shard"), None)
    flat = P("shard")
    rows = P("shard", None)
    in_specs = (
        tokens,
        tokens,
        tokens,
        flat,
        flat,
        rows,
        flat,
        flat,
        rows,
        flat,
        flat,
        flat,
        rows,
        flat,
        rows,
        flat,
    )
    out_specs = (
        tokens,
        tokens,
        flat,
        flat,
        rows,
        flat,
        flat,
        rows,
        flat,
        flat,
        flat,
        rows,
        flat,
        rows,
        flat,
    )
    body = functools.partial(shards_of, mesh.shape["rep"], mesh.shape["shard"])
    return jax.shard_map(
        body, mesh=mesh, in_specs=in_specs, out_specs=out_specs, check_vma=False
    )
```

```python
import functools
import math

import jax
import jax.numpy as jnp
from jax import lax
from jax.experimental import pallas as pl
from jax.experimental.pallas import tpu as pltpu
from jax.sharding import PartitionSpec as P

HEADS = 12
HEAD_DIM = 64
LOG2E = math.log2(math.e)
NEG = -1e30
BF16 = jnp.bfloat16
F32 = jnp.float32
VMEM_LIMIT = 56 << 20
SMALL_COST = pl.CostEstimate(flops=10**6, bytes_accessed=10**5, transcendentals=0)


def dot_nt(a, b):
    return lax.dot_general(a, b, (((1,), (1,)), ((), ())), preferred_element_type=F32)


def dot_nn(a, b):
    return lax.dot_general(a, b, (((1,), (0,)), ((), ())), preferred_element_type=F32)


def dot_tn(a, b):
    return lax.dot_general(a, b, (((0,), (0,)), ((), ())), preferred_element_type=F32)


def params():
    return pltpu.CompilerParams(vmem_limit_bytes=VMEM_LIMIT)


def swap(value, axis, size, mask):
    return lax.ppermute(value, axis, [(i, i ^ mask) for i in range(size)])


def allowed_block(seg_col, seg_row, block, rows):
    keys = (block + 1) * rows
    same = seg_col[:keys, :] == seg_row[:, block * rows : keys]
    causal = lax.broadcasted_iota(jnp.int32, (rows, rows), 0) <= lax.broadcasted_iota(
        jnp.int32, (rows, rows), 1
    )
    if block == 0:
        return same & causal
    return jnp.concatenate([same[: keys - rows], same[keys - rows :] & causal], axis=0)


def attend_kernel(rows, seg_col, seg_row, q_ref, k_ref, v_ref, o_ref, lse_ref):
    length = q_ref.shape[0]
    lane = lax.broadcasted_iota(jnp.int32, (1, 128), 1)
    scale = HEAD_DIM ** (-0.5) * LOG2E
    v_turned = v_ref[...].T
    for block in range(length // rows):
        keys = (block + 1) * rows
        here = slice(block * rows, keys)
        q = q_ref[here, :]
        k = k_ref[:keys, :]
        allowed = allowed_block(seg_col, seg_row, block, rows)
        parts = []
        for head in range(2):
            mine = (lane < 64) if head == 0 else (lane >= 64)
            q_head = jnp.where(mine, q, jnp.zeros_like(q))
            scores = jnp.where(allowed, dot_nt(k, q_head), NEG)
            highest = jnp.max(scores, axis=0, keepdims=True)
            expo = jnp.exp2((scores - highest) * scale)
            summed = jnp.sum(expo, axis=0, keepdims=True)
            v_head = v_turned[head * 64 : (head + 1) * 64, :keys]
            parts.append(dot_nn(v_head, expo.astype(BF16)) * (1.0 / summed))
            lse_ref[head, :, here] = jnp.broadcast_to(
                highest * scale + jnp.log2(summed), (8, rows)
            )
        o_ref[here, :] = jnp.concatenate(parts, axis=0).T.astype(BF16)


def head_specs(length, start):
    groups = HEADS // 2
    return [
        pl.BlockSpec((length, 1), lambda h: (0, 0)),
        pl.BlockSpec((1, length), lambda h: (0, 0)),
        pl.BlockSpec((length, 128), lambda h: (0, start + h)),
        pl.BlockSpec((length, 128), lambda h: (0, groups + start + h)),
        pl.BlockSpec((length, 128), lambda h: (0, 2 * groups + start + h)),
    ]


def attend_forward(qkv, segment, start, count):
    length = qkv.shape[0]
    rows = length // 2
    return pl.pallas_call(
        functools.partial(attend_kernel, rows),
        grid=(count,),
        in_specs=head_specs(length, start),
        out_specs=[
            pl.BlockSpec((length, 128), lambda h: (0, h)),
            pl.BlockSpec((2, 8, length), lambda h: (h, 0, 0)),
        ],
        out_shape=[
            jax.ShapeDtypeStruct((length, 128 * count), BF16),
            jax.ShapeDtypeStruct((2 * count, 8, length), F32),
        ],
        compiler_params=params(),
        cost_estimate=SMALL_COST,
        name="attend_forward",
    )(segment.reshape(length, 1), segment.reshape(1, length), qkv, qkv, qkv)


def attend_back_kernel(
    rows, seg_col, seg_row, q_ref, k_ref, v_ref, g_ref, lse_ref, dq_ref, dk_ref, dv_ref, sums_ref, dk_sum, dv_sum
):
    length = q_ref.shape[0]
    lane = lax.broadcasted_iota(jnp.int32, (1, 128), 1)
    scale = HEAD_DIM ** (-0.5) * LOG2E
    blocks = length // rows
    for block in reversed(range(blocks)):
        keys = (block + 1) * rows
        here = slice(block * rows, keys)
        q = q_ref[here, :]
        g = g_ref[here, :]
        k = k_ref[:keys, :]
        v = v_ref[:keys, :]
        allowed = allowed_block(seg_col, seg_row, block, rows)
        dq = dk = dv = None
        for head in range(2):
            mine = (lane < 64) if head == 0 else (lane >= 64)
            q_head = jnp.where(mine, q, jnp.zeros_like(q))
            g_head = jnp.where(mine, g, jnp.zeros_like(g))
            scores = dot_nt(k, q_head) * scale - lse_ref[head, 0:1, here]
            probs = jnp.exp2(jnp.where(allowed, scores, NEG))
            grad_probs = dot_nt(v, g_head)
            inner = jnp.sum(probs * grad_probs, axis=0, keepdims=True)
            grad_scores = (probs * (grad_probs - inner)).astype(BF16)
            dv_head = dot_nn(probs.astype(BF16), g_head)
            dk_head = dot_nn(grad_scores, q_head)
            dq_head = dot_tn(grad_scores, k)
            if head == 0:
                dq, dk, dv = dq_head, dk_head, dv_head
            else:
                dq, dk, dv = jnp.where(lane < 64, dq, dq_head), dk + dk_head, dv + dv_head
        dq_ref[here, :] = (dq * HEAD_DIM ** (-0.5)).astype(BF16)
        if block == blocks - 1:
            dk_sum[...] = dk
            dv_sum[...] = dv
        else:
            dk_sum[:keys, :] += dk
            dv_sum[:keys, :] += dv
    dk_ref[...] = (dk_sum[...] * HEAD_DIM ** (-0.5)).astype(BF16)
    dv_ref[...] = dv_sum[...].astype(BF16)
    sums_ref[0:1, :] = jnp.sum(dq_ref[...].astype(F32), axis=0, keepdims=True)
    sums_ref[1:2, :] = jnp.sum(dv_ref[...].astype(F32), axis=0, keepdims=True)
    sums_ref[2:8, :] = jnp.zeros((6, 128), F32)


def attend_backward(qkv, segment, grad, lse, start, count):
    length = qkv.shape[0]
    rows = length // 2
    return pl.pallas_call(
        functools.partial(attend_back_kernel, rows),
        grid=(count,),
        in_specs=head_specs(length, start)
        + [
            pl.BlockSpec((length, 128), lambda h: (0, start + h)),
            pl.BlockSpec((2, 8, length), lambda h: (h, 0, 0)),
        ],
        out_specs=[pl.BlockSpec((length, 128), lambda h: (0, h))] * 3
        + [pl.BlockSpec((8, 128), lambda h: (0, h))],
        out_shape=[jax.ShapeDtypeStruct((length, 128 * count), BF16)] * 3
        + [jax.ShapeDtypeStruct((8, 128 * count), F32)],
        scratch_shapes=[pltpu.VMEM((length, 128), F32)] * 2,
        compiler_params=params(),
        cost_estimate=SMALL_COST,
        name="attend_backward",
    )(segment.reshape(length, 1), segment.reshape(1, length), qkv, qkv, qkv, grad, lse)


def position_to_rel(slot, pieces, first):
    if pieces == 4 and first == 2:
        return (slot & 1) * 2 + slot // 2
    return slot


def place_rows(total, out_ref, spots, pieces, first, by_shard):
    shards_here, rows = out_ref.shape[1:3]
    for slot in range(pieces):
        piece = position_to_rel(slot, pieces, first) ^ spots[1]
        for rel_z in range(shards_here):
            owner = 0 if by_shard else rel_z ^ spots[2]
            start = pl.multiple_of((owner * pieces + piece) * rows, 16)
            out_ref[slot, rel_z] = total[pl.ds(start, rows), :].astype(BF16)


def grad_kernel(pieces, first, by_shard, spots, x_ref, far_y, near_y, far_ref, near_ref, total):
    for y_ref, out_ref in ((far_y, far_ref), (near_y, near_ref)):
        total[...] = dot_tn(x_ref[...], y_ref[...])
        place_rows(total, out_ref, spots, pieces, first, by_shard)


def grad_heads_kernel(pieces, first, extra, spots, x_ref, *rest):
    far_y, near_y = rest[:3], rest[3:6]
    far_ref, near_ref, total = rest[-3:]
    for side, (y_refs, out_ref) in enumerate(((far_y, far_ref), (near_y, near_ref))):
        joined = jnp.concatenate([y_ref[...] for y_ref in y_refs], axis=1)
        columns = joined.shape[1]
        total[:, :columns] = dot_tn(x_ref[...], joined)
        if extra:
            total[:, columns:] = dot_tn(rest[6][...], rest[7 + side][...])
        place_rows(total, out_ref, spots, pieces, first, False)


def grad_call(kernel, grid, in_specs, operands, out_spec, shape, scratch, spots):
    length, rows = operands[0].shape[0], shape[0] * shape[1] * shape[2]
    return pl.pallas_call(
        kernel,
        grid_spec=pltpu.PrefetchScalarGridSpec(
            num_scalar_prefetch=1,
            grid=grid,
            in_specs=in_specs,
            out_specs=[out_spec] * 2,
            scratch_shapes=[pltpu.VMEM(scratch, F32)],
        ),
        out_shape=[jax.ShapeDtypeStruct(shape, BF16)] * 2,
        compiler_params=params(),
        cost_estimate=SMALL_COST,
        name="weight_grad",
    )(spots, *operands)


def grad_proj(x, y, spots, shards, pieces, first):
    length, rows_all = x.shape
    half = y.shape[1] // 2
    rows = rows_all // (shards * pieces)
    return grad_call(
        functools.partial(grad_kernel, pieces, first, True),
        (shards,),
        [
            pl.BlockSpec((length, rows_all // shards), lambda i, s: (0, i ^ s[2])),
            pl.BlockSpec((length, half), lambda i, s: (0, 1 - s[0])),
            pl.BlockSpec((length, half), lambda i, s: (0, s[0])),
        ],
        [x, y, y],
        pl.BlockSpec((pieces, 1, rows, half), lambda i, s: (0, i, 0, 0)),
        (pieces, shards, rows, half),
        (rows_all // shards, half),
        spots,
    )


def grad_fc(x, y, spots, shards, pieces, first):
    length, rows_all = x.shape
    tile = rows_all // 2
    half = y.shape[1] // 2
    tiles = half // tile
    rows = rows_all // (shards * pieces)
    return grad_call(
        functools.partial(grad_kernel, pieces, first, False),
        (tiles,),
        [
            pl.BlockSpec((length, rows_all), lambda i, s: (0, 0)),
            pl.BlockSpec((length, tile), lambda i, s: (0, (1 - s[0]) * tiles + i)),
            pl.BlockSpec((length, tile), lambda i, s: (0, s[0] * tiles + i)),
        ],
        [x, y, y],
        pl.BlockSpec((pieces, shards, rows, tile), lambda i, s: (0, 0, 0, i)),
        (pieces, shards, rows, half),
        (rows_all, tile),
        spots,
    )


def grad_heads(x, grads, spots, shards, pieces, first, extra=()):
    length, rows_all = x.shape
    half = grads[0].shape[1] // 2
    rows = rows_all // (shards * pieces)
    columns = 3 * half
    far = pl.BlockSpec((length, half), lambda i, s: (0, 1 - s[0]))
    near = pl.BlockSpec((length, half), lambda i, s: (0, s[0]))
    in_specs = [pl.BlockSpec((length, rows_all), lambda i, s: (0, 0))] + [far] * 3 + [near] * 3
    operands = [x, *grads, *grads]
    if extra:
        half2 = extra[1].shape[1] // 2
        columns += half2
        in_specs += [
            pl.BlockSpec((length, rows_all), lambda i, s: (0, 0)),
            pl.BlockSpec((length, half2), lambda i, s: (0, 1 - s[0])),
            pl.BlockSpec((length, half2), lambda i, s: (0, s[0])),
        ]
        operands += [extra[0], extra[1], extra[1]]
    shape = (pieces, shards, rows, columns)
    return grad_call(
        functools.partial(grad_heads_kernel, pieces, first, bool(extra)),
        (1,),
        in_specs,
        operands,
        pl.BlockSpec(shape, lambda i, s: (0, 0, 0, 0)),
        shape,
        (rows_all, columns),
        spots,
    )


def piece_copies(full_ref, own_ref, parts, column, spots, sems, shards, pieces):
    core, spot_u, spot_z = spots[0], spots[1], spots[2]
    shard_rows = own_ref.shape[0]
    half = own_ref.shape[1] // 2
    rows = shard_rows // pieces
    copies = [
        pltpu.make_async_copy(
            own_ref,
            full_ref.at[pl.ds(pl.multiple_of(spot_z * shard_rows, 16), shard_rows), :],
            sems.at[0],
        )
    ]
    for index, part in enumerate(parts):
        side = core if index < pieces else 1 - core
        piece = spot_u ^ (index % pieces)
        for step in range(1, shards):
            start = pl.multiple_of((spot_z ^ step) * shard_rows + piece * rows, 16)
            copies.append(
                pltpu.make_async_copy(
                    part.at[step - 1, pl.ds(0, rows), pl.ds(column, half)],
                    full_ref.at[pl.ds(start, rows), pl.ds(pl.multiple_of(side * half, 128), half)],
                    sems.at[len(copies)],
                )
            )
    return copies


def at_first(work):
    @pl.when(pl.program_id(0) == 0)
    def _():
        work()


def start_all(copies):
    for copy in copies:
        copy.start()


def wait_all(copies):
    for copy in copies:
        copy.wait()


def row_call(kernel, name, steps, spots, rows_in, whole_in, parts_in, outs, sem_sets, sem_count):
    length = rows_in[0].shape[0]
    rows = length // steps

    def by_rows(width):
        return pl.BlockSpec((rows, width), lambda i, s: (i, 0))

    def whole(shape):
        return pl.BlockSpec(shape, lambda i, s: (0,) * len(shape))

    anywhere = pl.BlockSpec(memory_space=pl.ANY)
    return pl.pallas_call(
        kernel,
        grid_spec=pltpu.PrefetchScalarGridSpec(
            num_scalar_prefetch=1,
            grid=(steps,),
            in_specs=[by_rows(item.shape[1]) for item in rows_in]
            + [whole(item.shape) for item in whole_in]
            + [anywhere] * len(parts_in),
            out_specs=[
                by_rows(shape[1]) if tiled else whole(shape) for shape, _, tiled in outs
            ],
            scratch_shapes=[pltpu.SemaphoreType.DMA((sem_count,))] * sem_sets,
        ),
        out_shape=[jax.ShapeDtypeStruct(shape, dtype) for shape, dtype, _ in outs],
        compiler_params=params(),
        cost_estimate=SMALL_COST,
        name=name,
    )(spots, *rows_in, *whole_in, *parts_in)


def normed_rows(values):
    center = values - jnp.mean(values, axis=-1, keepdims=True)
    scale = lax.rsqrt(jnp.mean(center * center, axis=-1, keepdims=True) + 1e-05)
    return center * scale, scale


def norm_back(grad, values, gain):
    normed, scale = normed_rows(values)
    scaled = grad * gain
    inner = scaled - jnp.mean(scaled, axis=-1, keepdims=True)
    inner = inner - normed * jnp.mean(scaled * normed, axis=-1, keepdims=True)
    return scale * inner, normed


GAIN_ONE, SHIFT_ONE, BIAS_Q, BIAS_V, BIAS_OUT, GAIN_TWO, SHIFT_TWO, BIAS_PROJ = range(8)
GELU_SCALE = math.sqrt(2 / math.pi)
GELU_CUBE = 0.044715


def row_of(ref, index):
    return ref[index : index + 1, :]


def qkv_kernel(shards, pieces, spots, x_ref, vec_ref, own_ref, *rest):
    parts = rest[: 2 * pieces]
    w_ref, norm_ref, qkv_ref, sems = rest[2 * pieces :]
    copies = piece_copies(w_ref, own_ref, parts, 0, spots, sems, shards, pieces)
    at_first(lambda: start_all(copies))
    normed, _ = normed_rows(x_ref[...].astype(F32))
    norm_one = (normed * row_of(vec_ref, GAIN_ONE) + row_of(vec_ref, SHIFT_ONE)).astype(BF16)
    norm_ref[...] = norm_one
    at_first(lambda: wait_all(copies))
    width = norm_one.shape[1]
    for kind, row in enumerate((BIAS_Q, None, BIAS_V)):
        here = slice(kind * width, (kind + 1) * width)
        value = dot_nn(norm_one, w_ref[:, here])
        if row is not None:
            value = value + row_of(vec_ref, row)
        qkv_ref[:, here] = value.astype(BF16)


def fc_kernel(shards, pieces, spots, att_ref, x_ref, vec_ref, bias_ref, own_out, own_fc, *rest):
    parts = rest[: 2 * pieces]
    wo_ref, wf_ref, resid_ref, norm_ref, slope_ref, gelu_ref, sems_out, sems_fc = rest[2 * pieces :]
    half = own_out.shape[1] // 2
    copies_out = piece_copies(wo_ref, own_out, parts, 0, spots, sems_out, shards, pieces)
    copies_fc = piece_copies(wf_ref, own_fc, parts, half, spots, sems_fc, shards, pieces)
    at_first(lambda: start_all(copies_out + copies_fc))
    at_first(lambda: wait_all(copies_out))
    resid = x_ref[...].astype(F32) + dot_nn(att_ref[...], wo_ref[...]) + row_of(vec_ref, BIAS_OUT)
    resid_ref[...] = resid
    normed, _ = normed_rows(resid)
    norm_two = (normed * row_of(vec_ref, GAIN_TWO) + row_of(vec_ref, SHIFT_TWO)).astype(BF16)
    norm_ref[...] = norm_two
    at_first(lambda: wait_all(copies_fc))
    width = norm_two.shape[1]
    for tile in range(slope_ref.shape[1] // width):
        here = slice(tile * width, (tile + 1) * width)
        pre = dot_nn(norm_two, wf_ref[:, here]) + bias_ref[:, here]
        square = pre * pre
        curve = jnp.tanh(pre * (GELU_SCALE + (GELU_SCALE * GELU_CUBE) * square))
        above = 0.5 + 0.5 * curve
        gelu_ref[:, here] = (pre * above).astype(BF16)
        bend = pre * (0.5 - 0.5 * curve * curve)
        slope = above + bend * (GELU_SCALE + (3.0 * GELU_SCALE * GELU_CUBE) * square)
        slope_ref[:, here] = slope.astype(BF16)


def proj_kernel(shards, pieces, spots, gelu_ref, resid_ref, vec_ref, own_ref, *rest):
    parts = rest[: 2 * pieces]
    w_ref, out_ref, sems = rest[2 * pieces :]
    copies = piece_copies(w_ref, own_ref, parts, 0, spots, sems, shards, pieces)
    at_first(lambda: start_all(copies))
    at_first(lambda: wait_all(copies))
    out_ref[...] = (
        resid_ref[...] + dot_nn(gelu_ref[...], w_ref[...]) + row_of(vec_ref, BIAS_PROJ)
    ).astype(BF16)


def clear_first(ref):
    def work():
        ref[...] = jnp.zeros_like(ref)

    at_first(work)


def column_sums(values):
    return jnp.sum(values, axis=0, keepdims=True)


def back_gelu_kernel(spots, g_ref, slope_ref, w_ref, grad_ref, fc_sums, proj_sums):
    clear_first(fc_sums)
    clear_first(proj_sums)
    grad = g_ref[...]
    proj_sums[0:1, :] += column_sums(grad.astype(F32))
    width = grad.shape[1]
    for tile in range(slope_ref.shape[1] // width):
        here = slice(tile * width, (tile + 1) * width)
        grad_pre = (dot_nt(grad, w_ref[here, :]) * slope_ref[:, here].astype(F32)).astype(BF16)
        grad_ref[:, here] = grad_pre
        fc_sums[0:1, here] += column_sums(grad_pre.astype(F32))


def back_norm_kernel(
    spots, pre_ref, resid_ref, g_ref, vec_ref, wf_ref, wo_ref, sum_ref, low_ref, att_ref, sums_ref
):
    clear_first(sums_ref)
    grad = dot_nt(pre_ref[...], wf_ref[...])
    inner, normed = norm_back(grad, resid_ref[...], row_of(vec_ref, GAIN_TWO))
    total = g_ref[...].astype(F32) + inner
    sum_ref[...] = total
    low = total.astype(BF16)
    low_ref[...] = low
    sums_ref[0:1, :] += column_sums(low.astype(F32))
    sums_ref[1:2, :] += column_sums(grad * normed)
    sums_ref[2:3, :] += column_sums(grad)
    att_ref[...] = dot_nt(low, wo_ref[...]).astype(BF16)


def settle_kernel(pieces, every_ref, *outs):
    rows = every_ref.shape[1]
    for index in range(2 * pieces):
        piece, core = index // 2, index % 2
        column = 0
        for out_ref in outs:
            half = out_ref.shape[1] // 2
            out_ref[piece * rows : (piece + 1) * rows, core * half : (core + 1) * half] = every_ref[
                index, :, column : column + half
            ].astype(F32)
            column += half


def settle(every, widths, pieces):
    rows = every.shape[1]
    whole = pl.BlockSpec(memory_space=pltpu.VMEM)
    return pl.pallas_call(
        functools.partial(settle_kernel, pieces),
        in_specs=[whole],
        out_specs=[whole] * len(widths),
        out_shape=[jax.ShapeDtypeStruct((rows * pieces, width), F32) for width in widths],
        compiler_params=params(),
        name="settle",
    )(every)


def settle_last_kernel(pieces, wide, spots, *rest):
    parts, qkv_ref, out_ref = rest[: 2 * pieces], rest[-2], rest[-1]
    core, spot_u = spots[0], spots[1]
    rows = parts[0].shape[0]
    width = out_ref.shape[1]
    narrow = width // 2 - wide
    for index, part in enumerate(parts):
        side = core if index < pieces else 1 - core
        here = pl.ds(pl.multiple_of((spot_u ^ (index % pieces)) * rows, 16), rows)
        source = 0
        for base, size in ((0, wide), (2 * wide, narrow)):
            for kind in range(3):
                column = pl.multiple_of(kind * width + base + side * size, 128)
                qkv_ref[here, pl.ds(column, size)] = part[:, source : source + size].astype(F32)
                source += size
            if base == 0:
                column = pl.multiple_of(side * (width // 2), 128)
                out_ref[here, pl.ds(column, width // 2)] = part[
                    :, source : source + width // 2
                ].astype(F32)
                source += width // 2


def settle_last(parts, spots, pieces, wide, width):
    rows = parts[0].shape[0]
    whole = pl.BlockSpec(memory_space=pltpu.VMEM)
    return pl.pallas_call(
        functools.partial(settle_last_kernel, pieces, wide),
        in_specs=[pl.BlockSpec(memory_space=pltpu.SMEM)] + [whole] * (2 * pieces),
        out_specs=[whole] * 2,
        out_shape=[
            jax.ShapeDtypeStruct((rows * pieces, columns), F32) for columns in (3 * width, width)
        ],
        compiler_params=params(),
        name="settle_last",
    )(spots, *parts)


def back_product(w_ref, grads, start):
    total = None
    width = w_ref.shape[0]
    for kind, grad in enumerate(grads):
        first = kind * width + start
        part = dot_nt(grad[...], w_ref[:, first : first + grad.shape[1]])
        total = part if total is None else total + part
    return total


def back_one_kernel(w_ref, q_ref, k_ref, v_ref, out_ref):
    out_ref[...] = back_product(w_ref, (q_ref, k_ref, v_ref), 0)


def back_two_kernel(
    start, w_ref, q_ref, k_ref, v_ref, part_ref, x_ref, vec_ref, resid_ref, out_ref, sums_ref
):
    clear_first(sums_ref)
    grad = part_ref[...] + back_product(w_ref, (q_ref, k_ref, v_ref), start)
    inner, normed = norm_back(grad, x_ref[...].astype(F32), row_of(vec_ref, GAIN_ONE))
    out_ref[...] = (resid_ref[...] + inner).astype(BF16)
    sums_ref[0:1, :] += column_sums(grad * normed)
    sums_ref[1:2, :] += column_sums(grad)


def back_one(w, grads):
    length, width = grads[0].shape[0], w.shape[0]
    rows = length // 4
    return pl.pallas_call(
        back_one_kernel,
        grid=(4,),
        in_specs=[pl.BlockSpec(w.shape, lambda i: (0, 0))]
        + [pl.BlockSpec((rows, grads[0].shape[1]), lambda i: (i, 0))] * 3,
        out_specs=pl.BlockSpec((rows, width), lambda i: (i, 0)),
        out_shape=jax.ShapeDtypeStruct((length, width), F32),
        compiler_params=params(),
        cost_estimate=SMALL_COST,
        name="back_one",
    )(w, *grads)


def back_two(w, grads, start, part, values, vectors, resid):
    length, width = values.shape
    rows = length // 4
    block = pl.BlockSpec((rows, width), lambda i: (i, 0))
    return pl.pallas_call(
        functools.partial(back_two_kernel, start),
        grid=(4,),
        in_specs=[pl.BlockSpec(w.shape, lambda i: (0, 0))]
        + [pl.BlockSpec((rows, grads[0].shape[1]), lambda i: (i, 0))] * 3
        + [block, block, pl.BlockSpec((8, width), lambda i: (0, 0)), block],
        out_specs=[block, pl.BlockSpec((8, width), lambda i: (0, 0))],
        out_shape=[
            jax.ShapeDtypeStruct((length, width), BF16),
            jax.ShapeDtypeStruct((8, width), F32),
        ],
        compiler_params=params(),
        cost_estimate=SMALL_COST,
        name="back_two",
    )(w, *grads, part, values, vectors, resid)


def pack_kernel(ln1_ref, one_ref, two_ref, resid_ref, proj_ref, fc_ref, out_ref):
    width = out_ref.shape[1]
    wide = one_ref.shape[1]
    out_ref[0:2, :] = ln1_ref[0:2, :]
    out_ref[2:4, :wide] = one_ref[0:2, :]
    out_ref[2:4, wide:] = two_ref[0:2, :]
    out_ref[4:7, :] = resid_ref[0:3, :]
    out_ref[7:8, :] = proj_ref[0:1, :]
    count = fc_ref.shape[1] // width
    for index in range(count):
        out_ref[8 + index : 9 + index, :] = fc_ref[0:1, index * width : (index + 1) * width]
    out_ref[8 + count : 16, :] = jnp.zeros((8 - count, width), F32)


def pack(*sums):
    whole = pl.BlockSpec(memory_space=pltpu.VMEM)
    return pl.pallas_call(
        pack_kernel,
        in_specs=[whole] * len(sums),
        out_specs=whole,
        out_shape=jax.ShapeDtypeStruct((16, sums[0].shape[1]), F32),
        compiler_params=params(),
        cost_estimate=SMALL_COST,
        name="pack",
    )(*sums)


def shards_of(
    reps,
    shards,
    hidden_in,
    segment,
    cotangent,
    ln1_gain,
    ln1_bias,
    qkv_weight,
    query_bias,
    value_bias,
    out_weight,
    out_bias,
    ln2_gain,
    ln2_bias,
    fc_weight,
    fc_bias,
    proj_weight,
    proj_bias,
):
    width = hidden_in.shape[1]
    shard_rows = qkv_weight.shape[0]
    pieces = 4 if shard_rows % 64 == 0 and reps % 8 == 0 else 2
    rep = lax.axis_index("rep")
    spot_z = lax.axis_index("shard")
    core = rep & 1
    spot_u = (rep >> 1) & (pieces - 1)
    spots = jnp.stack([core, spot_u, spot_z]).astype(jnp.int32)

    def own_piece(weight):
        rows, half = weight.shape[0] // pieces, weight.shape[1] // 2
        return lax.dynamic_slice(weight, (spot_u * rows, core * half), (rows, half))

    def across_chips(part, first):
        if pieces == 2:
            return [part, swap(part, "rep", reps, 2)]
        second = 6 - first
        by_first = swap(part, "rep", reps, first)
        by_second = swap(part, "rep", reps, second)
        by_both = swap(part, "rep", reps, 6)
        if first == 2:
            return [part, by_first, by_second, by_both]
        return [part, by_second, by_first, by_both]

    def across_cores(parts):
        return parts + [swap(part, "rep", reps, 1) for part in parts]

    def along_shard(piece):
        return [swap(piece, "shard", shards, step) for step in range(1, shards)]

    piece_rows = shard_rows // pieces
    flat = [
        ln1_gain,
        ln1_bias,
        query_bias,
        value_bias,
        out_bias,
        ln2_gain,
        ln2_bias,
        proj_bias,
        fc_bias,
    ]
    flat_size = sum(item.shape[0] for item in flat)
    qkv_half = qkv_weight.shape[1] // 2
    small_rows = -(-flat_size // qkv_half)
    small = jnp.zeros((small_rows * qkv_half,), BF16)
    offset = 0
    for item in flat:
        size = item.shape[0]
        small = small + jnp.pad(item, (offset, small.shape[0] - offset - size))
        offset += size
    small = small.reshape(small_rows, qkv_half)
    tie = lax.optimization_barrier
    qkv_payload = jnp.concatenate(
        [own_piece(qkv_weight), jnp.pad(small, ((0, 16 - small_rows), (0, 0)))], axis=0
    )
    second_payload = jnp.concatenate([own_piece(out_weight), own_piece(fc_weight)], axis=1)
    qkv_slots = along_shard(qkv_payload)
    qkv_slots, second_payload = tie((qkv_slots, second_payload))
    qkv_parts = across_chips(jnp.stack([slot[:piece_rows] for slot in qkv_slots]), 2)
    second_slots = along_shard(second_payload)
    rows_of = [small] + [slot[piece_rows : piece_rows + small_rows] for slot in qkv_slots]
    ordered = []
    for index in range(shards):
        total = jnp.zeros_like(rows_of[0])
        for step, value in enumerate(rows_of):
            total = jnp.where((spot_z ^ step) == index, value, total)
        ordered.append(total.reshape(-1)[:flat_size])
    vectors = jnp.stack(ordered).astype(F32)
    bias_fc = vectors[:, 8 * shard_rows :].reshape(1, -1)
    vectors = vectors[:, : 8 * shard_rows].reshape(shards, 8, shard_rows)
    vectors = vectors.transpose(1, 0, 2).reshape(8, width)
    qkv_parts, proj_piece, vectors, bias_fc = tie(
        (qkv_parts, own_piece(proj_weight), vectors, bias_fc)
    )
    qkv_parts = across_cores(qkv_parts)
    second_stack, qkv_parts = tie((jnp.stack(second_slots), qkv_parts))
    second_parts = across_chips(second_stack, 2)

    seg_row = segment[0]
    length = hidden_in.shape[0]
    ff = fc_weight.shape[1]
    steps = 4
    sem_count = 1 + 2 * pieces * (shards - 1)
    kernel_of = lambda body: functools.partial(body, shards, pieces)
    w_qkv, norm_one, qkv = row_call(
        kernel_of(qkv_kernel),
        "qkv",
        steps,
        spots,
        [hidden_in],
        [vectors],
        [qkv_weight, *qkv_parts],
        [
            ((width, 3 * width), BF16, False),
            ((length, width), BF16, True),
            ((length, 3 * width), BF16, True),
        ],
        1,
        sem_count,
    )
    attended_one, lse_one = attend_forward(qkv, seg_row, 0, 4)
    attended_one, proj_piece, qkv, second_parts = tie((attended_one, proj_piece, qkv, second_parts))
    proj_slots = along_shard(proj_piece)
    attended_two, lse_two = attend_forward(qkv, seg_row, 4, 2)
    attended_two, second_parts, proj_slots = tie((attended_two, second_parts, proj_slots))
    second_parts = across_cores(second_parts)
    proj_parts = across_chips(jnp.stack(proj_slots), 4)
    attended = jnp.concatenate([attended_one, attended_two], axis=1)
    w_out, w_fc, resid, norm_two, slope, gelu_low = row_call(
        kernel_of(fc_kernel),
        "fc",
        steps,
        spots,
        [attended, hidden_in],
        [vectors, bias_fc],
        [out_weight, fc_weight, *second_parts],
        [
            ((width, width), BF16, False),
            ((width, ff), BF16, False),
            ((length, width), F32, True),
            ((length, width), BF16, True),
            ((length, ff), BF16, True),
            ((length, ff), BF16, True),
        ],
        2,
        sem_count,
    )

    half_pieces = pieces // 2

    def summed(near, old):
        return near.astype(F32) + old.astype(F32)

    def sent_part(near, old):
        return summed(near[half_pieces:], old[half_pieces:]).astype(BF16)

    def after_first(near, old, came):
        kept = summed(near[:half_pieces], old[:half_pieces]) + came.astype(F32)
        return kept[0], kept[half_pieces - 1].astype(BF16)

    def second_swap(onward, mask):
        return jnp.zeros_like(onward) if pieces == 2 else swap(onward, "rep", reps, mask)

    def shard_swaps(held):
        low = held.astype(BF16)
        return [swap(low[step], "shard", shards, step) for step in range(1, shards)]

    def shard_total(held, came):
        total = held[0]
        for value in came:
            total = total + value.astype(F32)
        mask = 2 * pieces
        while mask < reps:
            total = total + swap(total.astype(BF16), "rep", reps, mask).astype(F32)
            mask *= 2
        return total.astype(BF16)

    def every_owner(piece):
        return lax.all_gather(piece, "rep", axis=0, tiled=False)[: 2 * pieces]

    call = (spots, shards, pieces)
    first_of = 2 if pieces == 2 else 4
    gelu_low, proj_parts = tie((gelu_low, proj_parts))
    proj_parts = across_cores(proj_parts)
    proj_far, proj_near = grad_proj(gelu_low, cotangent, *call, 2)
    gelu_low, proj_far, proj_near, proj_parts = tie((gelu_low, proj_far, proj_near, proj_parts))
    proj_old = swap(proj_far, "rep", reps, 1)
    w_proj, block_out = row_call(
        kernel_of(proj_kernel),
        "proj",
        steps,
        spots,
        [gelu_low, resid],
        [vectors],
        [proj_weight, *proj_parts],
        [((width * 4, width), BF16, False), ((length, width), BF16, True)],
        1,
        sem_count,
    )
    w_proj, proj_old = tie((w_proj, proj_old))
    proj_send = sent_part(proj_near, proj_old)
    proj_send, w_proj = tie((proj_send, w_proj))
    proj_came = swap(proj_send, "rep", reps, 2)
    grad_pre, fc_sums, proj_sums = row_call(
        back_gelu_kernel,
        "back_gelu",
        steps,
        spots,
        [cotangent, slope],
        [w_proj],
        [],
        [((length, ff), BF16, True), ((8, ff), F32, False), ((8, width), F32, False)],
        0,
        0,
    )
    fc_far, fc_near = grad_fc(norm_two, grad_pre, *call, first_of)
    grad_pre, fc_far, fc_near, proj_came = tie((grad_pre, fc_far, fc_near, proj_came))
    fc_old = swap(fc_far, "rep", reps, 1)
    proj_held, proj_onward = after_first(proj_near, proj_old, proj_came)
    grad_pre, proj_onward = tie((grad_pre, proj_onward))
    proj_came = second_swap(proj_onward, 4)
    grad_resid, grad_branch, grad_attended, resid_sums = row_call(
        back_norm_kernel,
        "back_norm",
        steps,
        spots,
        [grad_pre, resid, cotangent],
        [vectors, w_fc, w_out],
        [],
        [
            ((length, width), F32, True),
            ((length, width), BF16, True),
            ((length, width), BF16, True),
            ((8, width), F32, False),
        ],
        0,
        0,
    )
    grad_attended, fc_old = tie((grad_attended, fc_old))
    fc_send = sent_part(fc_near, fc_old)
    grad_attended, fc_send, proj_came = tie((grad_attended, fc_send, proj_came))
    fc_came = swap(fc_send, "rep", reps, first_of)
    *heads_one, sums_one = attend_backward(qkv, seg_row, grad_attended, lse_one, 0, 4)
    heads_one, fc_came, grad_attended, proj_came = tie(
        (heads_one, fc_came, grad_attended, proj_came)
    )
    proj_held = proj_held + proj_came.astype(F32)
    proj_shards = shard_swaps(proj_held)
    fc_held, fc_onward = after_first(fc_near, fc_old, fc_came)
    fc_onward, heads_one = tie((fc_onward, heads_one))
    fc_came = second_swap(fc_onward, 2)
    one_far, one_near = grad_heads(norm_one, heads_one, *call, first_of, (attended, grad_branch))
    heads_one, one_far, one_near, proj_shards, fc_came = tie(
        (heads_one, one_far, one_near, proj_shards, fc_came)
    )
    one_old = swap(one_far, "rep", reps, 1)
    proj_piece = shard_total(proj_held, proj_shards)
    fc_held = fc_held + fc_came.astype(F32)
    proj_piece, heads_one, fc_held = tie((proj_piece, heads_one, fc_held))
    fc_shards = shard_swaps(fc_held)
    part_one = back_one(w_qkv, heads_one)
    part_one, one_old, grad_attended = tie((part_one, one_old, grad_attended))
    one_send = sent_part(one_near, one_old)
    one_send, grad_attended = tie((one_send, grad_attended))
    one_came = swap(one_send, "rep", reps, first_of)
    *heads_two, sums_two = attend_backward(qkv, seg_row, grad_attended, lse_two, 4, 2)
    heads_two, fc_shards = tie((heads_two, fc_shards))
    two_far, two_near = grad_heads(norm_one, heads_two, *call, first_of)
    heads_two, two_far, two_near, one_came = tie((heads_two, two_far, two_near, one_came))
    two_old = swap(two_far, "rep", reps, 1)
    one_held, one_onward = after_first(one_near, one_old, one_came)
    fc_piece = shard_total(fc_held, fc_shards)
    two_old, one_onward, heads_two, fc_piece = tie((two_old, one_onward, heads_two, fc_piece))
    one_came = second_swap(one_onward, 2)
    two_send = sent_part(two_near, two_old)
    two_send, heads_two = tie((two_send, heads_two))
    two_came = swap(two_send, "rep", reps, first_of)
    input_grad, ln1_sums = back_two(
        w_qkv, heads_two, 128 * 4, part_one, hidden_in, vectors, grad_resid
    )
    small_grads = pack(ln1_sums, sums_one, sums_two, resid_sums, proj_sums, fc_sums)
    masks = [1 << i for i in range(reps.bit_length() - 1)]

    def vector_step(total, count=1):
        for mask in masks[:count]:
            total = total + swap(total, "rep", reps, mask)
        del masks[:count]
        return total

    small_grads = vector_step(small_grads)
    two_came, one_came, small_grads = tie((two_came, one_came, small_grads))
    two_held, two_onward = after_first(two_near, two_old, two_came)
    two_onward, small_grads = tie((two_onward, small_grads))
    two_came = second_swap(two_onward, 2)
    one_held = one_held + one_came.astype(F32)
    one_shards = shard_swaps(one_held)
    small_grads = vector_step(small_grads)
    every_fc, every_proj = every_owner(fc_piece), every_owner(proj_piece)
    two_came, one_held, small_grads = tie((two_came, one_held, small_grads))
    two_held = two_held + two_came.astype(F32)
    two_shards = shard_swaps(two_held)
    small_grads = vector_step(small_grads, len(masks))
    two_shards, one_shards, small_grads, every_fc, every_proj = tie(
        (two_shards, one_shards, small_grads, every_fc, every_proj)
    )
    last_piece = jnp.concatenate(
        [shard_total(one_held, one_shards), shard_total(two_held, two_shards)], axis=-1
    )
    last_parts = across_chips(last_piece, 2)
    small_shards = along_shard(small_grads)
    (d_fc_weight,) = settle(every_fc, (fc_weight.shape[1],), pieces)
    (d_proj_weight,) = settle(every_proj, (width,), pieces)
    last_parts, small_shards, d_fc_weight, d_proj_weight = tie(
        (last_parts, small_shards, d_fc_weight, d_proj_weight)
    )
    last_parts = across_cores(last_parts)
    for value in small_shards:
        small_grads = small_grads + value
    d_qkv_weight, d_out_weight = settle_last(
        last_parts, spots, pieces, heads_one[0].shape[1] // 2, width
    )
    mine = lax.dynamic_slice(small_grads[:8], (0, spot_z * shard_rows), (8, shard_rows))
    fc_rows = fc_bias.shape[0]
    fc_row = small_grads[8 : 8 + ff // width].reshape(-1)
    d_fc_bias = lax.dynamic_slice(fc_row, (spot_z * fc_rows,), (fc_rows,))
    return (
        block_out,
        input_grad,
        mine[0],
        mine[1],
        d_qkv_weight,
        mine[2],
        mine[3],
        d_out_weight,
        mine[4],
        mine[5],
        mine[6],
        d_fc_weight,
        d_fc_bias,
        d_proj_weight,
        mine[7],
    )


def solution(mesh):
    tokens = P(("rep", "shard"), None)
    flat = P("shard")
    rows = P("shard", None)
    in_specs = (
        tokens,
        tokens,
        tokens,
        flat,
        flat,
        rows,
        flat,
        flat,
        rows,
        flat,
        flat,
        flat,
        rows,
        flat,
        rows,
        flat,
    )
    out_specs = (
        tokens,
        tokens,
        flat,
        flat,
        rows,
        flat,
        flat,
        rows,
        flat,
        flat,
        flat,
        rows,
        flat,
        rows,
        flat,
    )
    body = functools.partial(shards_of, mesh.shape["rep"], mesh.shape["shard"])
    return jax.shard_map(
        body, mesh=mesh, in_specs=in_specs, out_specs=out_specs, check_vma=False
    )
```

```python
import functools
import math

import jax
import jax.numpy as jnp
from jax import lax
from jax.experimental import pallas as pl
from jax.experimental.pallas import tpu as pltpu
from jax.sharding import PartitionSpec as P

HEADS = 12
HEAD_DIM = 64
LOG2E = math.log2(math.e)
NEG = -1e30
BF16 = jnp.bfloat16
F32 = jnp.float32
VMEM_LIMIT = 24 << 20
SMALL_COST = pl.CostEstimate(flops=10**6, bytes_accessed=10**5, transcendentals=0)


def dot_nt(a, b):
    return lax.dot_general(a, b, (((1,), (1,)), ((), ())), preferred_element_type=F32)


def dot_nn(a, b):
    return lax.dot_general(a, b, (((1,), (0,)), ((), ())), preferred_element_type=F32)


def dot_tn(a, b):
    return lax.dot_general(a, b, (((0,), (0,)), ((), ())), preferred_element_type=F32)


def params():
    return pltpu.CompilerParams(vmem_limit_bytes=VMEM_LIMIT)


def swap(value, axis, size, mask):
    return lax.ppermute(value, axis, [(i, i ^ mask) for i in range(size)])


def allowed_block(seg_col, seg_row, block, rows):
    keys = (block + 1) * rows
    same = seg_col[:keys, :] == seg_row[:, block * rows : keys]
    causal = lax.broadcasted_iota(jnp.int32, (rows, rows), 0) <= lax.broadcasted_iota(
        jnp.int32, (rows, rows), 1
    )
    if block == 0:
        return same & causal
    return jnp.concatenate([same[: keys - rows], same[keys - rows :] & causal], axis=0)


def attend_kernel(rows, seg_col, seg_row, q_ref, k_ref, v_ref, o_ref, lse_ref):
    length = q_ref.shape[0]
    lane = lax.broadcasted_iota(jnp.int32, (1, 128), 1)
    scale = HEAD_DIM ** (-0.5) * LOG2E
    v_turned = v_ref[...].T
    for block in range(length // rows):
        keys = (block + 1) * rows
        here = slice(block * rows, keys)
        q = q_ref[here, :]
        k = k_ref[:keys, :]
        allowed = allowed_block(seg_col, seg_row, block, rows)
        parts = []
        for head in range(2):
            mine = (lane < 64) if head == 0 else (lane >= 64)
            q_head = jnp.where(mine, q, jnp.zeros_like(q))
            scores = jnp.where(allowed, dot_nt(k, q_head), NEG)
            highest = jnp.max(scores, axis=0, keepdims=True)
            expo = jnp.exp2((scores - highest) * scale)
            summed = jnp.sum(expo, axis=0, keepdims=True)
            v_head = v_turned[head * 64 : (head + 1) * 64, :keys]
            parts.append(dot_nn(v_head, expo.astype(BF16)) * (1.0 / summed))
            lse_ref[head, :, here] = jnp.broadcast_to(
                highest * scale + jnp.log2(summed), (8, rows)
            )
        o_ref[here, :] = jnp.concatenate(parts, axis=0).T.astype(BF16)


def head_specs(length, start):
    groups = HEADS // 2
    return [
        pl.BlockSpec((length, 1), lambda h: (0, 0)),
        pl.BlockSpec((1, length), lambda h: (0, 0)),
        pl.BlockSpec((length, 128), lambda h: (0, start + h)),
        pl.BlockSpec((length, 128), lambda h: (0, groups + start + h)),
        pl.BlockSpec((length, 128), lambda h: (0, 2 * groups + start + h)),
    ]


def attend_forward(qkv, segment, start, count):
    length = qkv.shape[0]
    rows = length // 2
    return pl.pallas_call(
        functools.partial(attend_kernel, rows),
        grid=(count,),
        in_specs=head_specs(length, start),
        out_specs=[
            pl.BlockSpec((length, 128), lambda h: (0, h)),
            pl.BlockSpec((2, 8, length), lambda h: (h, 0, 0)),
        ],
        out_shape=[
            jax.ShapeDtypeStruct((length, 128 * count), BF16),
            jax.ShapeDtypeStruct((2 * count, 8, length), F32),
        ],
        compiler_params=params(),
        cost_estimate=SMALL_COST,
        name="attend_forward",
    )(segment.reshape(length, 1), segment.reshape(1, length), qkv, qkv, qkv)


def attend_back_kernel(
    rows, seg_col, seg_row, q_ref, k_ref, v_ref, g_ref, lse_ref, dq_ref, dk_ref, dv_ref, sums_ref, dk_sum, dv_sum
):
    length = q_ref.shape[0]
    lane = lax.broadcasted_iota(jnp.int32, (1, 128), 1)
    scale = HEAD_DIM ** (-0.5) * LOG2E
    blocks = length // rows
    for block in reversed(range(blocks)):
        keys = (block + 1) * rows
        here = slice(block * rows, keys)
        q = q_ref[here, :]
        g = g_ref[here, :]
        k = k_ref[:keys, :]
        v = v_ref[:keys, :]
        allowed = allowed_block(seg_col, seg_row, block, rows)
        dq = dk = dv = None
        for head in range(2):
            mine = (lane < 64) if head == 0 else (lane >= 64)
            q_head = jnp.where(mine, q, jnp.zeros_like(q))
            g_head = jnp.where(mine, g, jnp.zeros_like(g))
            scores = dot_nt(k, q_head) * scale - lse_ref[head, 0:1, here]
            probs = jnp.exp2(jnp.where(allowed, scores, NEG))
            grad_probs = dot_nt(v, g_head)
            inner = jnp.sum(probs * grad_probs, axis=0, keepdims=True)
            grad_scores = (probs * (grad_probs - inner)).astype(BF16)
            dv_head = dot_nn(probs.astype(BF16), g_head)
            dk_head = dot_nn(grad_scores, q_head)
            dq_head = dot_tn(grad_scores, k)
            if head == 0:
                dq, dk, dv = dq_head, dk_head, dv_head
            else:
                dq, dk, dv = jnp.where(lane < 64, dq, dq_head), dk + dk_head, dv + dv_head
        dq_ref[here, :] = (dq * HEAD_DIM ** (-0.5)).astype(BF16)
        if block == blocks - 1:
            dk_sum[...] = dk
            dv_sum[...] = dv
        else:
            dk_sum[:keys, :] += dk
            dv_sum[:keys, :] += dv
    dk_ref[...] = (dk_sum[...] * HEAD_DIM ** (-0.5)).astype(BF16)
    dv_ref[...] = dv_sum[...].astype(BF16)
    sums_ref[0:1, :] = jnp.sum(dq_ref[...].astype(F32), axis=0, keepdims=True)
    sums_ref[1:2, :] = jnp.sum(dv_ref[...].astype(F32), axis=0, keepdims=True)
    sums_ref[2:8, :] = jnp.zeros((6, 128), F32)


def attend_backward(qkv, segment, grad, lse, start, count):
    length = qkv.shape[0]
    rows = length // 2
    return pl.pallas_call(
        functools.partial(attend_back_kernel, rows),
        grid=(count,),
        in_specs=head_specs(length, start)
        + [
            pl.BlockSpec((length, 128), lambda h: (0, start + h)),
            pl.BlockSpec((2, 8, length), lambda h: (h, 0, 0)),
        ],
        out_specs=[pl.BlockSpec((length, 128), lambda h: (0, h))] * 3
        + [pl.BlockSpec((8, 128), lambda h: (0, h))],
        out_shape=[jax.ShapeDtypeStruct((length, 128 * count), BF16)] * 3
        + [jax.ShapeDtypeStruct((8, 128 * count), F32)],
        scratch_shapes=[pltpu.VMEM((length, 128), F32)] * 2,
        compiler_params=params(),
        cost_estimate=SMALL_COST,
        name="attend_backward",
    )(segment.reshape(length, 1), segment.reshape(1, length), qkv, qkv, qkv, grad, lse)


def position_to_rel(slot, pieces, first):
    if pieces == 4 and first == 2:
        return (slot & 1) * 2 + slot // 2
    return slot


def place_rows(total, out_ref, spots, pieces, first, by_shard):
    shards_here, rows = out_ref.shape[1:3]
    for slot in range(pieces):
        piece = position_to_rel(slot, pieces, first) ^ spots[1]
        for rel_z in range(shards_here):
            owner = 0 if by_shard else rel_z ^ spots[2]
            start = pl.multiple_of((owner * pieces + piece) * rows, 16)
            out_ref[slot, rel_z] = total[pl.ds(start, rows), :].astype(BF16)


def grad_kernel(pieces, first, by_shard, spots, x_ref, far_y, near_y, far_ref, near_ref, total):
    for y_ref, out_ref in ((far_y, far_ref), (near_y, near_ref)):
        total[...] = dot_tn(x_ref[...], y_ref[...])
        place_rows(total, out_ref, spots, pieces, first, by_shard)


def grad_heads_kernel(pieces, first, extra, spots, x_ref, *rest):
    far_y, near_y = rest[:3], rest[3:6]
    far_ref, near_ref, total = rest[-3:]
    for side, (y_refs, out_ref) in enumerate(((far_y, far_ref), (near_y, near_ref))):
        joined = jnp.concatenate([y_ref[...] for y_ref in y_refs], axis=1)
        columns = joined.shape[1]
        total[:, :columns] = dot_tn(x_ref[...], joined)
        if extra:
            total[:, columns:] = dot_tn(rest[6][...], rest[7 + side][...])
        place_rows(total, out_ref, spots, pieces, first, False)


def grad_call(kernel, grid, in_specs, operands, out_spec, shape, scratch, spots):
    length, rows = operands[0].shape[0], shape[0] * shape[1] * shape[2]
    return pl.pallas_call(
        kernel,
        grid_spec=pltpu.PrefetchScalarGridSpec(
            num_scalar_prefetch=1,
            grid=grid,
            in_specs=in_specs,
            out_specs=[out_spec] * 2,
            scratch_shapes=[pltpu.VMEM(scratch, F32)],
        ),
        out_shape=[jax.ShapeDtypeStruct(shape, BF16)] * 2,
        compiler_params=params(),
        cost_estimate=SMALL_COST,
        name="weight_grad",
    )(spots, *operands)


def grad_proj(x, y, spots, shards, pieces, first):
    length, rows_all = x.shape
    half = y.shape[1] // 2
    rows = rows_all // (shards * pieces)
    return grad_call(
        functools.partial(grad_kernel, pieces, first, True),
        (shards,),
        [
            pl.BlockSpec((length, rows_all // shards), lambda i, s: (0, i ^ s[2])),
            pl.BlockSpec((length, half), lambda i, s: (0, 1 - s[0])),
            pl.BlockSpec((length, half), lambda i, s: (0, s[0])),
        ],
        [x, y, y],
        pl.BlockSpec((pieces, 1, rows, half), lambda i, s: (0, i, 0, 0)),
        (pieces, shards, rows, half),
        (rows_all // shards, half),
        spots,
    )


def grad_fc(x, y, spots, shards, pieces, first):
    length, rows_all = x.shape
    tile = rows_all // 2
    half = y.shape[1] // 2
    tiles = half // tile
    rows = rows_all // (shards * pieces)
    return grad_call(
        functools.partial(grad_kernel, pieces, first, False),
        (tiles,),
        [
            pl.BlockSpec((length, rows_all), lambda i, s: (0, 0)),
            pl.BlockSpec((length, tile), lambda i, s: (0, (1 - s[0]) * tiles + i)),
            pl.BlockSpec((length, tile), lambda i, s: (0, s[0] * tiles + i)),
        ],
        [x, y, y],
        pl.BlockSpec((pieces, shards, rows, tile), lambda i, s: (0, 0, 0, i)),
        (pieces, shards, rows, half),
        (rows_all, tile),
        spots,
    )


def grad_heads(x, grads, spots, shards, pieces, first, extra=()):
    length, rows_all = x.shape
    half = grads[0].shape[1] // 2
    rows = rows_all // (shards * pieces)
    columns = 3 * half
    far = pl.BlockSpec((length, half), lambda i, s: (0, 1 - s[0]))
    near = pl.BlockSpec((length, half), lambda i, s: (0, s[0]))
    in_specs = [pl.BlockSpec((length, rows_all), lambda i, s: (0, 0))] + [far] * 3 + [near] * 3
    operands = [x, *grads, *grads]
    if extra:
        half2 = extra[1].shape[1] // 2
        columns += half2
        in_specs += [
            pl.BlockSpec((length, rows_all), lambda i, s: (0, 0)),
            pl.BlockSpec((length, half2), lambda i, s: (0, 1 - s[0])),
            pl.BlockSpec((length, half2), lambda i, s: (0, s[0])),
        ]
        operands += [extra[0], extra[1], extra[1]]
    shape = (pieces, shards, rows, columns)
    return grad_call(
        functools.partial(grad_heads_kernel, pieces, first, bool(extra)),
        (1,),
        in_specs,
        operands,
        pl.BlockSpec(shape, lambda i, s: (0, 0, 0, 0)),
        shape,
        (rows_all, columns),
        spots,
    )


def piece_copies(full_ref, own_ref, parts, column, spots, sems, shards, pieces):
    core, spot_u, spot_z = spots[0], spots[1], spots[2]
    shard_rows = own_ref.shape[0]
    half = own_ref.shape[1] // 2
    rows = shard_rows // pieces
    copies = [
        pltpu.make_async_copy(
            own_ref,
            full_ref.at[pl.ds(pl.multiple_of(spot_z * shard_rows, 16), shard_rows), :],
            sems.at[0],
        )
    ]
    for index, part in enumerate(parts):
        side = core if index < pieces else 1 - core
        piece = spot_u ^ (index % pieces)
        for step in range(1, shards):
            start = pl.multiple_of((spot_z ^ step) * shard_rows + piece * rows, 16)
            copies.append(
                pltpu.make_async_copy(
                    part.at[step - 1, pl.ds(0, rows), pl.ds(column, half)],
                    full_ref.at[pl.ds(start, rows), pl.ds(pl.multiple_of(side * half, 128), half)],
                    sems.at[len(copies)],
                )
            )
    return copies


def at_first(work):
    @pl.when(pl.program_id(0) == 0)
    def _():
        work()


def start_all(copies):
    for copy in copies:
        copy.start()


def wait_all(copies):
    for copy in copies:
        copy.wait()


def row_call(kernel, name, steps, spots, rows_in, whole_in, parts_in, outs, sem_sets, sem_count):
    length = rows_in[0].shape[0]
    rows = length // steps

    def by_rows(width):
        return pl.BlockSpec((rows, width), lambda i, s: (i, 0))

    def whole(shape):
        return pl.BlockSpec(shape, lambda i, s: (0,) * len(shape))

    anywhere = pl.BlockSpec(memory_space=pl.ANY)
    return pl.pallas_call(
        kernel,
        grid_spec=pltpu.PrefetchScalarGridSpec(
            num_scalar_prefetch=1,
            grid=(steps,),
            in_specs=[by_rows(item.shape[1]) for item in rows_in]
            + [whole(item.shape) for item in whole_in]
            + [anywhere] * len(parts_in),
            out_specs=[
                by_rows(shape[1]) if tiled else whole(shape) for shape, _, tiled in outs
            ],
            scratch_shapes=[pltpu.SemaphoreType.DMA((sem_count,))] * sem_sets,
        ),
        out_shape=[jax.ShapeDtypeStruct(shape, dtype) for shape, dtype, _ in outs],
        compiler_params=params(),
        cost_estimate=SMALL_COST,
        name=name,
    )(spots, *rows_in, *whole_in, *parts_in)


def normed_rows(values):
    center = values - jnp.mean(values, axis=-1, keepdims=True)
    scale = lax.rsqrt(jnp.mean(center * center, axis=-1, keepdims=True) + 1e-05)
    return center * scale, scale


def norm_back(grad, values, gain):
    normed, scale = normed_rows(values)
    scaled = grad * gain
    inner = scaled - jnp.mean(scaled, axis=-1, keepdims=True)
    inner = inner - normed * jnp.mean(scaled * normed, axis=-1, keepdims=True)
    return scale * inner, normed


GAIN_ONE, SHIFT_ONE, BIAS_Q, BIAS_V, BIAS_OUT, GAIN_TWO, SHIFT_TWO, BIAS_PROJ = range(8)
GELU_SCALE = math.sqrt(2 / math.pi)
GELU_CUBE = 0.044715


def row_of(ref, index):
    return ref[index : index + 1, :]


def qkv_kernel(shards, pieces, spots, x_ref, vec_ref, own_ref, *rest):
    parts = rest[: 2 * pieces]
    w_ref, norm_ref, qkv_ref, sems = rest[2 * pieces :]
    copies = piece_copies(w_ref, own_ref, parts, 0, spots, sems, shards, pieces)
    at_first(lambda: start_all(copies))
    normed, _ = normed_rows(x_ref[...].astype(F32))
    norm_one = (normed * row_of(vec_ref, GAIN_ONE) + row_of(vec_ref, SHIFT_ONE)).astype(BF16)
    norm_ref[...] = norm_one
    at_first(lambda: wait_all(copies))
    width = norm_one.shape[1]
    for kind, row in enumerate((BIAS_Q, None, BIAS_V)):
        here = slice(kind * width, (kind + 1) * width)
        value = dot_nn(norm_one, w_ref[:, here])
        if row is not None:
            value = value + row_of(vec_ref, row)
        qkv_ref[:, here] = value.astype(BF16)


def fc_kernel(shards, pieces, spots, att_ref, x_ref, vec_ref, bias_ref, own_out, own_fc, *rest):
    parts = rest[: 2 * pieces]
    wo_ref, wf_ref, resid_ref, norm_ref, slope_ref, gelu_ref, sems_out, sems_fc = rest[2 * pieces :]
    half = own_out.shape[1] // 2
    copies_out = piece_copies(wo_ref, own_out, parts, 0, spots, sems_out, shards, pieces)
    copies_fc = piece_copies(wf_ref, own_fc, parts, half, spots, sems_fc, shards, pieces)
    at_first(lambda: start_all(copies_out + copies_fc))
    at_first(lambda: wait_all(copies_out))
    resid = x_ref[...].astype(F32) + dot_nn(att_ref[...], wo_ref[...]) + row_of(vec_ref, BIAS_OUT)
    resid_ref[...] = resid
    normed, _ = normed_rows(resid)
    norm_two = (normed * row_of(vec_ref, GAIN_TWO) + row_of(vec_ref, SHIFT_TWO)).astype(BF16)
    norm_ref[...] = norm_two
    at_first(lambda: wait_all(copies_fc))
    width = norm_two.shape[1]
    for tile in range(slope_ref.shape[1] // width):
        here = slice(tile * width, (tile + 1) * width)
        pre = dot_nn(norm_two, wf_ref[:, here]) + bias_ref[:, here]
        square = pre * pre
        curve = jnp.tanh(pre * (GELU_SCALE + (GELU_SCALE * GELU_CUBE) * square))
        above = 0.5 + 0.5 * curve
        gelu_ref[:, here] = (pre * above).astype(BF16)
        bend = pre * (0.5 - 0.5 * curve * curve)
        slope = above + bend * (GELU_SCALE + (3.0 * GELU_SCALE * GELU_CUBE) * square)
        slope_ref[:, here] = slope.astype(BF16)


def proj_kernel(shards, pieces, spots, gelu_ref, resid_ref, vec_ref, own_ref, *rest):
    parts = rest[: 2 * pieces]
    w_ref, out_ref, sems = rest[2 * pieces :]
    copies = piece_copies(w_ref, own_ref, parts, 0, spots, sems, shards, pieces)
    at_first(lambda: start_all(copies))
    at_first(lambda: wait_all(copies))
    out_ref[...] = (
        resid_ref[...] + dot_nn(gelu_ref[...], w_ref[...]) + row_of(vec_ref, BIAS_PROJ)
    ).astype(BF16)


def clear_first(ref):
    def work():
        ref[...] = jnp.zeros_like(ref)

    at_first(work)


def column_sums(values):
    return jnp.sum(values, axis=0, keepdims=True)


def back_gelu_kernel(spots, g_ref, slope_ref, w_ref, grad_ref, fc_sums, proj_sums):
    clear_first(fc_sums)
    clear_first(proj_sums)
    grad = g_ref[...]
    proj_sums[0:1, :] += column_sums(grad.astype(F32))
    width = grad.shape[1]
    for tile in range(slope_ref.shape[1] // width):
        here = slice(tile * width, (tile + 1) * width)
        grad_pre = (dot_nt(grad, w_ref[here, :]) * slope_ref[:, here].astype(F32)).astype(BF16)
        grad_ref[:, here] = grad_pre
        fc_sums[0:1, here] += column_sums(grad_pre.astype(F32))


def back_norm_kernel(
    spots, pre_ref, resid_ref, g_ref, vec_ref, wf_ref, wo_ref, sum_ref, low_ref, att_ref, sums_ref
):
    clear_first(sums_ref)
    grad = dot_nt(pre_ref[...], wf_ref[...])
    inner, normed = norm_back(grad, resid_ref[...], row_of(vec_ref, GAIN_TWO))
    total = g_ref[...].astype(F32) + inner
    sum_ref[...] = total
    low = total.astype(BF16)
    low_ref[...] = low
    sums_ref[0:1, :] += column_sums(low.astype(F32))
    sums_ref[1:2, :] += column_sums(grad * normed)
    sums_ref[2:3, :] += column_sums(grad)
    att_ref[...] = dot_nt(low, wo_ref[...]).astype(BF16)


def settle_kernel(pieces, every_ref, *outs):
    rows = every_ref.shape[1]
    for index in range(2 * pieces):
        piece, core = index // 2, index % 2
        column = 0
        for out_ref in outs:
            half = out_ref.shape[1] // 2
            out_ref[piece * rows : (piece + 1) * rows, core * half : (core + 1) * half] = every_ref[
                index, :, column : column + half
            ].astype(F32)
            column += half


def settle(every, widths, pieces):
    rows = every.shape[1]
    whole = pl.BlockSpec(memory_space=pltpu.VMEM)
    return pl.pallas_call(
        functools.partial(settle_kernel, pieces),
        in_specs=[whole],
        out_specs=[whole] * len(widths),
        out_shape=[jax.ShapeDtypeStruct((rows * pieces, width), F32) for width in widths],
        compiler_params=params(),
        name="settle",
    )(every)


def settle_last_kernel(pieces, wide, spots, *rest):
    parts, qkv_ref, out_ref = rest[: 2 * pieces], rest[-2], rest[-1]
    core, spot_u = spots[0], spots[1]
    rows = parts[0].shape[0]
    width = out_ref.shape[1]
    narrow = width // 2 - wide
    for index, part in enumerate(parts):
        side = core if index < pieces else 1 - core
        here = pl.ds(pl.multiple_of((spot_u ^ (index % pieces)) * rows, 16), rows)
        source = 0
        for base, size in ((0, wide), (2 * wide, narrow)):
            for kind in range(3):
                column = pl.multiple_of(kind * width + base + side * size, 128)
                qkv_ref[here, pl.ds(column, size)] = part[:, source : source + size].astype(F32)
                source += size
            if base == 0:
                column = pl.multiple_of(side * (width // 2), 128)
                out_ref[here, pl.ds(column, width // 2)] = part[
                    :, source : source + width // 2
                ].astype(F32)
                source += width // 2


def settle_last(parts, spots, pieces, wide, width):
    rows = parts[0].shape[0]
    whole = pl.BlockSpec(memory_space=pltpu.VMEM)
    return pl.pallas_call(
        functools.partial(settle_last_kernel, pieces, wide),
        in_specs=[pl.BlockSpec(memory_space=pltpu.SMEM)] + [whole] * (2 * pieces),
        out_specs=[whole] * 2,
        out_shape=[
            jax.ShapeDtypeStruct((rows * pieces, columns), F32) for columns in (3 * width, width)
        ],
        compiler_params=params(),
        name="settle_last",
    )(spots, *parts)


def back_product(w_ref, grads, start):
    total = None
    width = w_ref.shape[0]
    for kind, grad in enumerate(grads):
        first = kind * width + start
        part = dot_nt(grad[...], w_ref[:, first : first + grad.shape[1]])
        total = part if total is None else total + part
    return total


def back_one_kernel(w_ref, q_ref, k_ref, v_ref, out_ref):
    out_ref[...] = back_product(w_ref, (q_ref, k_ref, v_ref), 0)


def back_two_kernel(
    start, w_ref, q_ref, k_ref, v_ref, part_ref, x_ref, vec_ref, resid_ref, out_ref, sums_ref
):
    clear_first(sums_ref)
    grad = part_ref[...] + back_product(w_ref, (q_ref, k_ref, v_ref), start)
    inner, normed = norm_back(grad, x_ref[...].astype(F32), row_of(vec_ref, GAIN_ONE))
    out_ref[...] = (resid_ref[...] + inner).astype(BF16)
    sums_ref[0:1, :] += column_sums(grad * normed)
    sums_ref[1:2, :] += column_sums(grad)


def back_one(w, grads):
    length, width = grads[0].shape[0], w.shape[0]
    rows = length // 4
    return pl.pallas_call(
        back_one_kernel,
        grid=(4,),
        in_specs=[pl.BlockSpec(w.shape, lambda i: (0, 0))]
        + [pl.BlockSpec((rows, grads[0].shape[1]), lambda i: (i, 0))] * 3,
        out_specs=pl.BlockSpec((rows, width), lambda i: (i, 0)),
        out_shape=jax.ShapeDtypeStruct((length, width), F32),
        compiler_params=params(),
        cost_estimate=SMALL_COST,
        name="back_one",
    )(w, *grads)


def back_two(w, grads, start, part, values, vectors, resid):
    length, width = values.shape
    rows = length // 4
    block = pl.BlockSpec((rows, width), lambda i: (i, 0))
    return pl.pallas_call(
        functools.partial(back_two_kernel, start),
        grid=(4,),
        in_specs=[pl.BlockSpec(w.shape, lambda i: (0, 0))]
        + [pl.BlockSpec((rows, grads[0].shape[1]), lambda i: (i, 0))] * 3
        + [block, block, pl.BlockSpec((8, width), lambda i: (0, 0)), block],
        out_specs=[block, pl.BlockSpec((8, width), lambda i: (0, 0))],
        out_shape=[
            jax.ShapeDtypeStruct((length, width), BF16),
            jax.ShapeDtypeStruct((8, width), F32),
        ],
        compiler_params=params(),
        cost_estimate=SMALL_COST,
        name="back_two",
    )(w, *grads, part, values, vectors, resid)


def pack_kernel(ln1_ref, one_ref, two_ref, resid_ref, proj_ref, fc_ref, out_ref):
    width = out_ref.shape[1]
    wide = one_ref.shape[1]
    out_ref[0:2, :] = ln1_ref[0:2, :]
    out_ref[2:4, :wide] = one_ref[0:2, :]
    out_ref[2:4, wide:] = two_ref[0:2, :]
    out_ref[4:7, :] = resid_ref[0:3, :]
    out_ref[7:8, :] = proj_ref[0:1, :]
    count = fc_ref.shape[1] // width
    for index in range(count):
        out_ref[8 + index : 9 + index, :] = fc_ref[0:1, index * width : (index + 1) * width]
    out_ref[8 + count : 16, :] = jnp.zeros((8 - count, width), F32)


def pack(*sums):
    whole = pl.BlockSpec(memory_space=pltpu.VMEM)
    return pl.pallas_call(
        pack_kernel,
        in_specs=[whole] * len(sums),
        out_specs=whole,
        out_shape=jax.ShapeDtypeStruct((16, sums[0].shape[1]), F32),
        compiler_params=params(),
        cost_estimate=SMALL_COST,
        name="pack",
    )(*sums)


def shards_of(
    reps,
    shards,
    hidden_in,
    segment,
    cotangent,
    ln1_gain,
    ln1_bias,
    qkv_weight,
    query_bias,
    value_bias,
    out_weight,
    out_bias,
    ln2_gain,
    ln2_bias,
    fc_weight,
    fc_bias,
    proj_weight,
    proj_bias,
):
    width = hidden_in.shape[1]
    shard_rows = qkv_weight.shape[0]
    pieces = 4 if shard_rows % 64 == 0 and reps % 8 == 0 else 2
    rep = lax.axis_index("rep")
    spot_z = lax.axis_index("shard")
    core = rep & 1
    spot_u = (rep >> 1) & (pieces - 1)
    spots = jnp.stack([core, spot_u, spot_z]).astype(jnp.int32)

    def own_piece(weight):
        rows, half = weight.shape[0] // pieces, weight.shape[1] // 2
        return lax.dynamic_slice(weight, (spot_u * rows, core * half), (rows, half))

    def across_chips(part, first):
        if pieces == 2:
            return [part, swap(part, "rep", reps, 2)]
        second = 6 - first
        by_first = swap(part, "rep", reps, first)
        by_second = swap(part, "rep", reps, second)
        by_both = swap(part, "rep", reps, 6)
        if first == 2:
            return [part, by_first, by_second, by_both]
        return [part, by_second, by_first, by_both]

    def across_cores(parts):
        return parts + [swap(part, "rep", reps, 1) for part in parts]

    def along_shard(piece):
        return [swap(piece, "shard", shards, step) for step in range(1, shards)]

    piece_rows = shard_rows // pieces
    flat = [
        ln1_gain,
        ln1_bias,
        query_bias,
        value_bias,
        out_bias,
        ln2_gain,
        ln2_bias,
        proj_bias,
        fc_bias,
    ]
    flat_size = sum(item.shape[0] for item in flat)
    qkv_half = qkv_weight.shape[1] // 2
    small_rows = -(-flat_size // qkv_half)
    small = jnp.zeros((small_rows * qkv_half,), BF16)
    offset = 0
    for item in flat:
        size = item.shape[0]
        small = small + jnp.pad(item, (offset, small.shape[0] - offset - size))
        offset += size
    small = small.reshape(small_rows, qkv_half)
    tie = lax.optimization_barrier
    qkv_payload = jnp.concatenate(
        [own_piece(qkv_weight), jnp.pad(small, ((0, 16 - small_rows), (0, 0)))], axis=0
    )
    second_payload = jnp.concatenate([own_piece(out_weight), own_piece(fc_weight)], axis=1)
    qkv_slots = along_shard(qkv_payload)
    qkv_slots, second_payload = tie((qkv_slots, second_payload))
    qkv_parts = across_chips(jnp.stack([slot[:piece_rows] for slot in qkv_slots]), 2)
    second_slots = along_shard(second_payload)
    rows_of = [small] + [slot[piece_rows : piece_rows + small_rows] for slot in qkv_slots]
    ordered = []
    for index in range(shards):
        total = jnp.zeros_like(rows_of[0])
        for step, value in enumerate(rows_of):
            total = jnp.where((spot_z ^ step) == index, value, total)
        ordered.append(total.reshape(-1)[:flat_size])
    vectors = jnp.stack(ordered).astype(F32)
    bias_fc = vectors[:, 8 * shard_rows :].reshape(1, -1)
    vectors = vectors[:, : 8 * shard_rows].reshape(shards, 8, shard_rows)
    vectors = vectors.transpose(1, 0, 2).reshape(8, width)
    qkv_parts, proj_piece, vectors, bias_fc = tie(
        (qkv_parts, own_piece(proj_weight), vectors, bias_fc)
    )
    qkv_parts = across_cores(qkv_parts)
    second_stack, qkv_parts = tie((jnp.stack(second_slots), qkv_parts))
    second_parts = across_chips(second_stack, 2)

    seg_row = segment[0]
    length = hidden_in.shape[0]
    ff = fc_weight.shape[1]
    steps = 4
    sem_count = 1 + 2 * pieces * (shards - 1)
    kernel_of = lambda body: functools.partial(body, shards, pieces)
    w_qkv, norm_one, qkv = row_call(
        kernel_of(qkv_kernel),
        "qkv",
        steps,
        spots,
        [hidden_in],
        [vectors],
        [qkv_weight, *qkv_parts],
        [
            ((width, 3 * width), BF16, False),
            ((length, width), BF16, True),
            ((length, 3 * width), BF16, True),
        ],
        1,
        sem_count,
    )
    attended_one, lse_one = attend_forward(qkv, seg_row, 0, 4)
    attended_one, proj_piece, qkv, second_parts = tie((attended_one, proj_piece, qkv, second_parts))
    proj_slots = along_shard(proj_piece)
    attended_two, lse_two = attend_forward(qkv, seg_row, 4, 2)
    attended_two, second_parts, proj_slots = tie((attended_two, second_parts, proj_slots))
    second_parts = across_cores(second_parts)
    proj_parts = across_chips(jnp.stack(proj_slots), 4)
    attended = jnp.concatenate([attended_one, attended_two], axis=1)
    w_out, w_fc, resid, norm_two, slope, gelu_low = row_call(
        kernel_of(fc_kernel),
        "fc",
        steps,
        spots,
        [attended, hidden_in],
        [vectors, bias_fc],
        [out_weight, fc_weight, *second_parts],
        [
            ((width, width), BF16, False),
            ((width, ff), BF16, False),
            ((length, width), F32, True),
            ((length, width), BF16, True),
            ((length, ff), BF16, True),
            ((length, ff), BF16, True),
        ],
        2,
        sem_count,
    )

    half_pieces = pieces // 2

    def summed(near, old):
        return near.astype(F32) + old.astype(F32)

    def sent_part(near, old):
        return summed(near[half_pieces:], old[half_pieces:]).astype(BF16)

    def after_first(near, old, came):
        kept = summed(near[:half_pieces], old[:half_pieces]) + came.astype(F32)
        return kept[0], kept[half_pieces - 1].astype(BF16)

    def second_swap(onward, mask):
        return jnp.zeros_like(onward) if pieces == 2 else swap(onward, "rep", reps, mask)

    def shard_swaps(held):
        low = held.astype(BF16)
        return [swap(low[step], "shard", shards, step) for step in range(1, shards)]

    def shard_total(held, came):
        total = held[0]
        for value in came:
            total = total + value.astype(F32)
        mask = 2 * pieces
        while mask < reps:
            total = total + swap(total.astype(BF16), "rep", reps, mask).astype(F32)
            mask *= 2
        return total.astype(BF16)

    def every_owner(piece):
        return lax.all_gather(piece, "rep", axis=0, tiled=False)[: 2 * pieces]

    call = (spots, shards, pieces)
    first_of = 2 if pieces == 2 else 4
    gelu_low, proj_parts = tie((gelu_low, proj_parts))
    proj_parts = across_cores(proj_parts)
    proj_far, proj_near = grad_proj(gelu_low, cotangent, *call, 2)
    gelu_low, proj_far, proj_near, proj_parts = tie((gelu_low, proj_far, proj_near, proj_parts))
    proj_old = swap(proj_far, "rep", reps, 1)
    w_proj, block_out = row_call(
        kernel_of(proj_kernel),
        "proj",
        steps,
        spots,
        [gelu_low, resid],
        [vectors],
        [proj_weight, *proj_parts],
        [((width * 4, width), BF16, False), ((length, width), BF16, True)],
        1,
        sem_count,
    )
    w_proj, proj_old = tie((w_proj, proj_old))
    proj_send = sent_part(proj_near, proj_old)
    proj_send, w_proj = tie((proj_send, w_proj))
    proj_came = swap(proj_send, "rep", reps, 2)
    grad_pre, fc_sums, proj_sums = row_call(
        back_gelu_kernel,
        "back_gelu",
        steps,
        spots,
        [cotangent, slope],
        [w_proj],
        [],
        [((length, ff), BF16, True), ((8, ff), F32, False), ((8, width), F32, False)],
        0,
        0,
    )
    fc_far, fc_near = grad_fc(norm_two, grad_pre, *call, first_of)
    grad_pre, fc_far, fc_near, proj_came = tie((grad_pre, fc_far, fc_near, proj_came))
    fc_old = swap(fc_far, "rep", reps, 1)
    proj_held, proj_onward = after_first(proj_near, proj_old, proj_came)
    grad_pre, proj_onward = tie((grad_pre, proj_onward))
    proj_came = second_swap(proj_onward, 4)
    grad_resid, grad_branch, grad_attended, resid_sums = row_call(
        back_norm_kernel,
        "back_norm",
        steps,
        spots,
        [grad_pre, resid, cotangent],
        [vectors, w_fc, w_out],
        [],
        [
            ((length, width), F32, True),
            ((length, width), BF16, True),
            ((length, width), BF16, True),
            ((8, width), F32, False),
        ],
        0,
        0,
    )
    grad_attended, fc_old = tie((grad_attended, fc_old))
    fc_send = sent_part(fc_near, fc_old)
    grad_attended, fc_send, proj_came = tie((grad_attended, fc_send, proj_came))
    fc_came = swap(fc_send, "rep", reps, first_of)
    *heads_one, sums_one = attend_backward(qkv, seg_row, grad_attended, lse_one, 0, 4)
    heads_one, fc_came, grad_attended, proj_came = tie(
        (heads_one, fc_came, grad_attended, proj_came)
    )
    proj_held = proj_held + proj_came.astype(F32)
    proj_shards = shard_swaps(proj_held)
    fc_held, fc_onward = after_first(fc_near, fc_old, fc_came)
    fc_onward, heads_one = tie((fc_onward, heads_one))
    fc_came = second_swap(fc_onward, 2)
    one_far, one_near = grad_heads(norm_one, heads_one, *call, first_of, (attended, grad_branch))
    heads_one, one_far, one_near, proj_shards, fc_came = tie(
        (heads_one, one_far, one_near, proj_shards, fc_came)
    )
    one_old = swap(one_far, "rep", reps, 1)
    proj_piece = shard_total(proj_held, proj_shards)
    fc_held = fc_held + fc_came.astype(F32)
    proj_piece, heads_one, fc_held = tie((proj_piece, heads_one, fc_held))
    fc_shards = shard_swaps(fc_held)
    part_one = back_one(w_qkv, heads_one)
    part_one, one_old, grad_attended = tie((part_one, one_old, grad_attended))
    one_send = sent_part(one_near, one_old)
    one_send, grad_attended = tie((one_send, grad_attended))
    one_came = swap(one_send, "rep", reps, first_of)
    *heads_two, sums_two = attend_backward(qkv, seg_row, grad_attended, lse_two, 4, 2)
    heads_two, fc_shards = tie((heads_two, fc_shards))
    two_far, two_near = grad_heads(norm_one, heads_two, *call, first_of)
    heads_two, two_far, two_near, one_came = tie((heads_two, two_far, two_near, one_came))
    two_old = swap(two_far, "rep", reps, 1)
    one_held, one_onward = after_first(one_near, one_old, one_came)
    fc_piece = shard_total(fc_held, fc_shards)
    two_old, one_onward, heads_two, fc_piece = tie((two_old, one_onward, heads_two, fc_piece))
    one_came = second_swap(one_onward, 2)
    two_send = sent_part(two_near, two_old)
    two_send, heads_two = tie((two_send, heads_two))
    two_came = swap(two_send, "rep", reps, first_of)
    input_grad, ln1_sums = back_two(
        w_qkv, heads_two, 128 * 4, part_one, hidden_in, vectors, grad_resid
    )
    small_grads = pack(ln1_sums, sums_one, sums_two, resid_sums, proj_sums, fc_sums)
    masks = [1 << i for i in range(reps.bit_length() - 1)]

    def vector_step(total, count=1):
        for mask in masks[:count]:
            total = total + swap(total, "rep", reps, mask)
        del masks[:count]
        return total

    small_grads = vector_step(small_grads)
    two_came, one_came, small_grads = tie((two_came, one_came, small_grads))
    two_held, two_onward = after_first(two_near, two_old, two_came)
    two_onward, small_grads = tie((two_onward, small_grads))
    two_came = second_swap(two_onward, 2)
    one_held = one_held + one_came.astype(F32)
    one_shards = shard_swaps(one_held)
    small_grads = vector_step(small_grads)
    every_fc, every_proj = every_owner(fc_piece), every_owner(proj_piece)
    two_came, one_held, small_grads, every_proj = tie(
        (two_came, one_held, small_grads, every_proj)
    )
    (d_proj_weight,) = settle(every_proj, (width,), pieces)
    two_held = two_held + two_came.astype(F32)
    two_shards = shard_swaps(two_held)
    small_grads = vector_step(small_grads, len(masks))
    two_shards, one_shards, small_grads, every_fc, d_proj_weight = tie(
        (two_shards, one_shards, small_grads, every_fc, d_proj_weight)
    )
    last_piece = jnp.concatenate(
        [shard_total(one_held, one_shards), shard_total(two_held, two_shards)], axis=-1
    )
    last_parts = across_chips(last_piece, 2)
    masks = [1 << i for i in range(shards.bit_length() - 1)]
    for mask in masks[:-1]:
        small_grads = small_grads + swap(small_grads, "shard", shards, mask)
    (d_fc_weight,) = settle(every_fc, (fc_weight.shape[1],), pieces)
    last_parts, small_grads, d_fc_weight = tie((last_parts, small_grads, d_fc_weight))
    last_parts = across_cores(last_parts)
    small_grads = small_grads + swap(small_grads, "shard", shards, masks[-1])
    d_qkv_weight, d_out_weight = settle_last(
        last_parts, spots, pieces, heads_one[0].shape[1] // 2, width
    )
    mine = lax.dynamic_slice(small_grads[:8], (0, spot_z * shard_rows), (8, shard_rows))
    fc_rows = fc_bias.shape[0]
    fc_row = small_grads[8 : 8 + ff // width].reshape(-1)
    d_fc_bias = lax.dynamic_slice(fc_row, (spot_z * fc_rows,), (fc_rows,))
    return (
        block_out,
        input_grad,
        mine[0],
        mine[1],
        d_qkv_weight,
        mine[2],
        mine[3],
        d_out_weight,
        mine[4],
        mine[5],
        mine[6],
        d_fc_weight,
        d_fc_bias,
        d_proj_weight,
        mine[7],
    )


def solution(mesh):
    tokens = P(("rep", "shard"), None)
    flat = P("shard")
    rows = P("shard", None)
    in_specs = (
        tokens,
        tokens,
        tokens,
        flat,
        flat,
        rows,
        flat,
        flat,
        rows,
        flat,
        flat,
        flat,
        rows,
        flat,
        rows,
        flat,
    )
    out_specs = (
        tokens,
        tokens,
        flat,
        flat,
        rows,
        flat,
        flat,
        rows,
        flat,
        flat,
        flat,
        rows,
        flat,
        rows,
        flat,
    )
    body = functools.partial(shards_of, mesh.shape["rep"], mesh.shape["shard"])
    return jax.shard_map(
        body, mesh=mesh, in_specs=in_specs, out_specs=out_specs, check_vma=False
    )
```

```python
import functools
import math

import jax
import jax.numpy as jnp
from jax import lax
from jax.experimental import pallas as pl
from jax.experimental.pallas import tpu as pltpu
from jax.sharding import PartitionSpec as P

HEADS = 12
HEAD_DIM = 64
LOG2E = math.log2(math.e)
NEG = -1e30
BF16 = jnp.bfloat16
F32 = jnp.float32
VMEM_LIMIT = 24 << 20
WIDE_LIMIT = 56 << 20
SMALL_COST = pl.CostEstimate(flops=10**6, bytes_accessed=10**5, transcendentals=0)


def dot_nt(a, b):
    return lax.dot_general(a, b, (((1,), (1,)), ((), ())), preferred_element_type=F32)


def dot_nn(a, b):
    return lax.dot_general(a, b, (((1,), (0,)), ((), ())), preferred_element_type=F32)


def dot_tn(a, b):
    return lax.dot_general(a, b, (((0,), (0,)), ((), ())), preferred_element_type=F32)


def params(limit=VMEM_LIMIT):
    return pltpu.CompilerParams(vmem_limit_bytes=limit)


def swap(value, axis, size, mask):
    return lax.ppermute(value, axis, [(i, i ^ mask) for i in range(size)])


def allowed_block(seg_col, seg_row, block, rows):
    keys = (block + 1) * rows
    same = seg_col[:keys, :] == seg_row[:, block * rows : keys]
    causal = lax.broadcasted_iota(jnp.int32, (rows, rows), 0) <= lax.broadcasted_iota(
        jnp.int32, (rows, rows), 1
    )
    if block == 0:
        return same & causal
    return jnp.concatenate([same[: keys - rows], same[keys - rows :] & causal], axis=0)


def attend_kernel(rows, seg_col, seg_row, q_ref, k_ref, v_ref, o_ref, lse_ref):
    length = q_ref.shape[0]
    lane = lax.broadcasted_iota(jnp.int32, (1, 128), 1)
    scale = HEAD_DIM ** (-0.5) * LOG2E
    v_turned = v_ref[...].T
    for block in range(length // rows):
        keys = (block + 1) * rows
        here = slice(block * rows, keys)
        q = q_ref[here, :]
        k = k_ref[:keys, :]
        allowed = allowed_block(seg_col, seg_row, block, rows)
        parts = []
        for head in range(2):
            mine = (lane < 64) if head == 0 else (lane >= 64)
            q_head = jnp.where(mine, q, jnp.zeros_like(q))
            scores = jnp.where(allowed, dot_nt(k, q_head), NEG)
            highest = jnp.max(scores, axis=0, keepdims=True)
            expo = jnp.exp2((scores - highest) * scale)
            summed = jnp.sum(expo, axis=0, keepdims=True)
            v_head = v_turned[head * 64 : (head + 1) * 64, :keys]
            parts.append(dot_nn(v_head, expo.astype(BF16)) * (1.0 / summed))
            lse_ref[head, :, here] = jnp.broadcast_to(
                highest * scale + jnp.log2(summed), (8, rows)
            )
        o_ref[here, :] = jnp.concatenate(parts, axis=0).T.astype(BF16)


def head_specs(length, start):
    groups = HEADS // 2
    return [
        pl.BlockSpec((length, 1), lambda h: (0, 0)),
        pl.BlockSpec((1, length), lambda h: (0, 0)),
        pl.BlockSpec((length, 128), lambda h: (0, start + h)),
        pl.BlockSpec((length, 128), lambda h: (0, groups + start + h)),
        pl.BlockSpec((length, 128), lambda h: (0, 2 * groups + start + h)),
    ]


def attend_forward(qkv, segment, start, count):
    length = qkv.shape[0]
    rows = length // 2
    return pl.pallas_call(
        functools.partial(attend_kernel, rows),
        grid=(count,),
        in_specs=head_specs(length, start),
        out_specs=[
            pl.BlockSpec((length, 128), lambda h: (0, h)),
            pl.BlockSpec((2, 8, length), lambda h: (h, 0, 0)),
        ],
        out_shape=[
            jax.ShapeDtypeStruct((length, 128 * count), BF16),
            jax.ShapeDtypeStruct((2 * count, 8, length), F32),
        ],
        compiler_params=params(),
        cost_estimate=SMALL_COST,
        name="attend_forward",
    )(segment.reshape(length, 1), segment.reshape(1, length), qkv, qkv, qkv)


def attend_back_kernel(
    rows, seg_col, seg_row, q_ref, k_ref, v_ref, g_ref, lse_ref, dq_ref, dk_ref, dv_ref, sums_ref, dk_sum, dv_sum
):
    length = q_ref.shape[0]
    lane = lax.broadcasted_iota(jnp.int32, (1, 128), 1)
    scale = HEAD_DIM ** (-0.5) * LOG2E
    blocks = length // rows
    for block in reversed(range(blocks)):
        keys = (block + 1) * rows
        here = slice(block * rows, keys)
        q = q_ref[here, :]
        g = g_ref[here, :]
        k = k_ref[:keys, :]
        v = v_ref[:keys, :]
        allowed = allowed_block(seg_col, seg_row, block, rows)
        dq = dk = dv = None
        for head in range(2):
            mine = (lane < 64) if head == 0 else (lane >= 64)
            q_head = jnp.where(mine, q, jnp.zeros_like(q))
            g_head = jnp.where(mine, g, jnp.zeros_like(g))
            scores = dot_nt(k, q_head) * scale - lse_ref[head, 0:1, here]
            probs = jnp.exp2(jnp.where(allowed, scores, NEG))
            grad_probs = dot_nt(v, g_head)
            inner = jnp.sum(probs * grad_probs, axis=0, keepdims=True)
            grad_scores = (probs * (grad_probs - inner)).astype(BF16)
            dv_head = dot_nn(probs.astype(BF16), g_head)
            dk_head = dot_nn(grad_scores, q_head)
            dq_head = dot_tn(grad_scores, k)
            if head == 0:
                dq, dk, dv = dq_head, dk_head, dv_head
            else:
                dq, dk, dv = jnp.where(lane < 64, dq, dq_head), dk + dk_head, dv + dv_head
        dq_ref[here, :] = (dq * HEAD_DIM ** (-0.5)).astype(BF16)
        if block == blocks - 1:
            dk_sum[...] = dk
            dv_sum[...] = dv
        else:
            dk_sum[:keys, :] += dk
            dv_sum[:keys, :] += dv
    dk_ref[...] = (dk_sum[...] * HEAD_DIM ** (-0.5)).astype(BF16)
    dv_ref[...] = dv_sum[...].astype(BF16)
    sums_ref[0:1, :] = jnp.sum(dq_ref[...].astype(F32), axis=0, keepdims=True)
    sums_ref[1:2, :] = jnp.sum(dv_ref[...].astype(F32), axis=0, keepdims=True)
    sums_ref[2:8, :] = jnp.zeros((6, 128), F32)


def attend_backward(qkv, segment, grad, lse, start, count):
    length = qkv.shape[0]
    rows = length // 2
    return pl.pallas_call(
        functools.partial(attend_back_kernel, rows),
        grid=(count,),
        in_specs=head_specs(length, start)
        + [
            pl.BlockSpec((length, 128), lambda h: (0, start + h)),
            pl.BlockSpec((2, 8, length), lambda h: (h, 0, 0)),
        ],
        out_specs=[pl.BlockSpec((length, 128), lambda h: (0, h))] * 3
        + [pl.BlockSpec((8, 128), lambda h: (0, h))],
        out_shape=[jax.ShapeDtypeStruct((length, 128 * count), BF16)] * 3
        + [jax.ShapeDtypeStruct((8, 128 * count), F32)],
        scratch_shapes=[pltpu.VMEM((length, 128), F32)] * 2,
        compiler_params=params(),
        cost_estimate=SMALL_COST,
        name="attend_backward",
    )(segment.reshape(length, 1), segment.reshape(1, length), qkv, qkv, qkv, grad, lse)


def position_to_rel(slot, pieces, first):
    if pieces == 4 and first == 2:
        return (slot & 1) * 2 + slot // 2
    return slot


def place_rows(total, out_ref, spots, pieces, first, by_shard):
    shards_here, rows = out_ref.shape[1:3]
    for slot in range(pieces):
        piece = position_to_rel(slot, pieces, first) ^ spots[1]
        for rel_z in range(shards_here):
            owner = 0 if by_shard else rel_z ^ spots[2]
            start = pl.multiple_of((owner * pieces + piece) * rows, 16)
            out_ref[slot, rel_z] = total[pl.ds(start, rows), :].astype(BF16)


def grad_kernel(pieces, first, by_shard, spots, x_ref, far_y, near_y, far_ref, near_ref, total):
    for y_ref, out_ref in ((far_y, far_ref), (near_y, near_ref)):
        total[...] = dot_tn(x_ref[...], y_ref[...])
        place_rows(total, out_ref, spots, pieces, first, by_shard)


def grad_heads_kernel(pieces, first, extra, spots, x_ref, *rest):
    far_y, near_y = rest[:3], rest[3:6]
    far_ref, near_ref, total = rest[-3:]
    for side, (y_refs, out_ref) in enumerate(((far_y, far_ref), (near_y, near_ref))):
        joined = jnp.concatenate([y_ref[...] for y_ref in y_refs], axis=1)
        columns = joined.shape[1]
        total[:, :columns] = dot_tn(x_ref[...], joined)
        if extra:
            total[:, columns:] = dot_tn(rest[6][...], rest[7 + side][...])
        place_rows(total, out_ref, spots, pieces, first, False)


def grad_call(kernel, grid, in_specs, operands, out_spec, shape, scratch, spots):
    length, rows = operands[0].shape[0], shape[0] * shape[1] * shape[2]
    return pl.pallas_call(
        kernel,
        grid_spec=pltpu.PrefetchScalarGridSpec(
            num_scalar_prefetch=1,
            grid=grid,
            in_specs=in_specs,
            out_specs=[out_spec] * 2,
            scratch_shapes=[pltpu.VMEM(scratch, F32)],
        ),
        out_shape=[jax.ShapeDtypeStruct(shape, BF16)] * 2,
        compiler_params=params(),
        cost_estimate=SMALL_COST,
        name="weight_grad",
    )(spots, *operands)


def grad_proj(x, y, spots, shards, pieces, first):
    length, rows_all = x.shape
    half = y.shape[1] // 2
    rows = rows_all // (shards * pieces)
    return grad_call(
        functools.partial(grad_kernel, pieces, first, True),
        (shards,),
        [
            pl.BlockSpec((length, rows_all // shards), lambda i, s: (0, i ^ s[2])),
            pl.BlockSpec((length, half), lambda i, s: (0, 1 - s[0])),
            pl.BlockSpec((length, half), lambda i, s: (0, s[0])),
        ],
        [x, y, y],
        pl.BlockSpec((pieces, 1, rows, half), lambda i, s: (0, i, 0, 0)),
        (pieces, shards, rows, half),
        (rows_all // shards, half),
        spots,
    )


def grad_fc(x, y, spots, shards, pieces, first):
    length, rows_all = x.shape
    tile = rows_all // 2
    half = y.shape[1] // 2
    tiles = half // tile
    rows = rows_all // (shards * pieces)
    return grad_call(
        functools.partial(grad_kernel, pieces, first, False),
        (tiles,),
        [
            pl.BlockSpec((length, rows_all), lambda i, s: (0, 0)),
            pl.BlockSpec((length, tile), lambda i, s: (0, (1 - s[0]) * tiles + i)),
            pl.BlockSpec((length, tile), lambda i, s: (0, s[0] * tiles + i)),
        ],
        [x, y, y],
        pl.BlockSpec((pieces, shards, rows, tile), lambda i, s: (0, 0, 0, i)),
        (pieces, shards, rows, half),
        (rows_all, tile),
        spots,
    )


def grad_heads(x, grads, spots, shards, pieces, first, extra=()):
    length, rows_all = x.shape
    half = grads[0].shape[1] // 2
    rows = rows_all // (shards * pieces)
    columns = 3 * half
    far = pl.BlockSpec((length, half), lambda i, s: (0, 1 - s[0]))
    near = pl.BlockSpec((length, half), lambda i, s: (0, s[0]))
    in_specs = [pl.BlockSpec((length, rows_all), lambda i, s: (0, 0))] + [far] * 3 + [near] * 3
    operands = [x, *grads, *grads]
    if extra:
        half2 = extra[1].shape[1] // 2
        columns += half2
        in_specs += [
            pl.BlockSpec((length, rows_all), lambda i, s: (0, 0)),
            pl.BlockSpec((length, half2), lambda i, s: (0, 1 - s[0])),
            pl.BlockSpec((length, half2), lambda i, s: (0, s[0])),
        ]
        operands += [extra[0], extra[1], extra[1]]
    shape = (pieces, shards, rows, columns)
    return grad_call(
        functools.partial(grad_heads_kernel, pieces, first, bool(extra)),
        (1,),
        in_specs,
        operands,
        pl.BlockSpec(shape, lambda i, s: (0, 0, 0, 0)),
        shape,
        (rows_all, columns),
        spots,
    )


def piece_copies(full_ref, own_ref, parts, column, spots, sems, shards, pieces):
    core, spot_u, spot_z = spots[0], spots[1], spots[2]
    shard_rows = own_ref.shape[0]
    half = own_ref.shape[1] // 2
    rows = shard_rows // pieces
    copies = [
        pltpu.make_async_copy(
            own_ref,
            full_ref.at[pl.ds(pl.multiple_of(spot_z * shard_rows, 16), shard_rows), :],
            sems.at[0],
        )
    ]
    for index, part in enumerate(parts):
        side = core if index < pieces else 1 - core
        piece = spot_u ^ (index % pieces)
        for step in range(1, shards):
            start = pl.multiple_of((spot_z ^ step) * shard_rows + piece * rows, 16)
            copies.append(
                pltpu.make_async_copy(
                    part.at[step - 1, pl.ds(0, rows), pl.ds(column, half)],
                    full_ref.at[pl.ds(start, rows), pl.ds(pl.multiple_of(side * half, 128), half)],
                    sems.at[len(copies)],
                )
            )
    return copies


def at_first(work):
    @pl.when(pl.program_id(0) == 0)
    def _():
        work()


def start_all(copies):
    for copy in copies:
        copy.start()


def wait_all(copies):
    for copy in copies:
        copy.wait()


def row_call(kernel, name, steps, spots, rows_in, whole_in, parts_in, outs, sem_sets, sem_count):
    length = rows_in[0].shape[0]
    rows = length // steps

    def by_rows(width):
        return pl.BlockSpec((rows, width), lambda i, s: (i, 0))

    def whole(shape):
        return pl.BlockSpec(shape, lambda i, s: (0,) * len(shape))

    anywhere = pl.BlockSpec(memory_space=pl.ANY)
    return pl.pallas_call(
        kernel,
        grid_spec=pltpu.PrefetchScalarGridSpec(
            num_scalar_prefetch=1,
            grid=(steps,),
            in_specs=[by_rows(item.shape[1]) for item in rows_in]
            + [whole(item.shape) for item in whole_in]
            + [anywhere] * len(parts_in),
            out_specs=[
                by_rows(shape[1]) if tiled else whole(shape) for shape, _, tiled in outs
            ],
            scratch_shapes=[pltpu.SemaphoreType.DMA((sem_count,))] * sem_sets,
        ),
        out_shape=[jax.ShapeDtypeStruct(shape, dtype) for shape, dtype, _ in outs],
        compiler_params=params(WIDE_LIMIT if name == "qkv" else VMEM_LIMIT),
        cost_estimate=SMALL_COST,
        name=name,
    )(spots, *rows_in, *whole_in, *parts_in)


def normed_rows(values):
    center = values - jnp.mean(values, axis=-1, keepdims=True)
    scale = lax.rsqrt(jnp.mean(center * center, axis=-1, keepdims=True) + 1e-05)
    return center * scale, scale


def norm_back(grad, values, gain):
    normed, scale = normed_rows(values)
    scaled = grad * gain
    inner = scaled - jnp.mean(scaled, axis=-1, keepdims=True)
    inner = inner - normed * jnp.mean(scaled * normed, axis=-1, keepdims=True)
    return scale * inner, normed


GAIN_ONE, SHIFT_ONE, BIAS_Q, BIAS_V, BIAS_OUT, GAIN_TWO, SHIFT_TWO, BIAS_PROJ = range(8)
GELU_SCALE = math.sqrt(2 / math.pi)
GELU_CUBE = 0.044715


def row_of(ref, index):
    return ref[index : index + 1, :]


def qkv_kernel(shards, pieces, spots, x_ref, vec_ref, own_ref, *rest):
    parts = rest[: 2 * pieces]
    w_ref, norm_ref, qkv_ref, sems = rest[2 * pieces :]
    copies = piece_copies(w_ref, own_ref, parts, 0, spots, sems, shards, pieces)
    at_first(lambda: start_all(copies))
    normed, _ = normed_rows(x_ref[...].astype(F32))
    norm_one = (normed * row_of(vec_ref, GAIN_ONE) + row_of(vec_ref, SHIFT_ONE)).astype(BF16)
    norm_ref[...] = norm_one
    at_first(lambda: wait_all(copies))
    width = norm_one.shape[1]
    for kind, row in enumerate((BIAS_Q, None, BIAS_V)):
        here = slice(kind * width, (kind + 1) * width)
        value = dot_nn(norm_one, w_ref[:, here])
        if row is not None:
            value = value + row_of(vec_ref, row)
        qkv_ref[:, here] = value.astype(BF16)


def fc_kernel(shards, pieces, spots, att_ref, x_ref, vec_ref, bias_ref, own_out, own_fc, *rest):
    parts = rest[: 2 * pieces]
    wo_ref, wf_ref, resid_ref, norm_ref, slope_ref, gelu_ref, sems_out, sems_fc = rest[2 * pieces :]
    half = own_out.shape[1] // 2
    copies_out = piece_copies(wo_ref, own_out, parts, 0, spots, sems_out, shards, pieces)
    copies_fc = piece_copies(wf_ref, own_fc, parts, half, spots, sems_fc, shards, pieces)
    at_first(lambda: start_all(copies_out + copies_fc))
    at_first(lambda: wait_all(copies_out))
    resid = x_ref[...].astype(F32) + dot_nn(att_ref[...], wo_ref[...]) + row_of(vec_ref, BIAS_OUT)
    resid_ref[...] = resid
    normed, _ = normed_rows(resid)
    norm_two = (normed * row_of(vec_ref, GAIN_TWO) + row_of(vec_ref, SHIFT_TWO)).astype(BF16)
    norm_ref[...] = norm_two
    at_first(lambda: wait_all(copies_fc))
    width = norm_two.shape[1]
    for tile in range(slope_ref.shape[1] // width):
        here = slice(tile * width, (tile + 1) * width)
        pre = dot_nn(norm_two, wf_ref[:, here]) + bias_ref[:, here]
        square = pre * pre
        curve = jnp.tanh(pre * (GELU_SCALE + (GELU_SCALE * GELU_CUBE) * square))
        above = 0.5 + 0.5 * curve
        gelu_ref[:, here] = (pre * above).astype(BF16)
        bend = pre * (0.5 - 0.5 * curve * curve)
        slope = above + bend * (GELU_SCALE + (3.0 * GELU_SCALE * GELU_CUBE) * square)
        slope_ref[:, here] = slope.astype(BF16)


def proj_kernel(shards, pieces, spots, gelu_ref, resid_ref, vec_ref, own_ref, *rest):
    parts = rest[: 2 * pieces]
    w_ref, out_ref, sems = rest[2 * pieces :]
    copies = piece_copies(w_ref, own_ref, parts, 0, spots, sems, shards, pieces)
    at_first(lambda: start_all(copies))
    at_first(lambda: wait_all(copies))
    out_ref[...] = (
        resid_ref[...] + dot_nn(gelu_ref[...], w_ref[...]) + row_of(vec_ref, BIAS_PROJ)
    ).astype(BF16)


def clear_first(ref):
    def work():
        ref[...] = jnp.zeros_like(ref)

    at_first(work)


def column_sums(values):
    return jnp.sum(values, axis=0, keepdims=True)


def back_gelu_kernel(spots, g_ref, slope_ref, w_ref, grad_ref, fc_sums, proj_sums):
    clear_first(fc_sums)
    clear_first(proj_sums)
    grad = g_ref[...]
    proj_sums[0:1, :] += column_sums(grad.astype(F32))
    width = grad.shape[1]
    for tile in range(slope_ref.shape[1] // width):
        here = slice(tile * width, (tile + 1) * width)
        grad_pre = (dot_nt(grad, w_ref[here, :]) * slope_ref[:, here].astype(F32)).astype(BF16)
        grad_ref[:, here] = grad_pre
        fc_sums[0:1, here] += column_sums(grad_pre.astype(F32))


def back_norm_kernel(
    spots, pre_ref, resid_ref, g_ref, vec_ref, wf_ref, wo_ref, sum_ref, low_ref, att_ref, sums_ref
):
    clear_first(sums_ref)
    grad = dot_nt(pre_ref[...], wf_ref[...])
    inner, normed = norm_back(grad, resid_ref[...], row_of(vec_ref, GAIN_TWO))
    total = g_ref[...].astype(F32) + inner
    sum_ref[...] = total
    low = total.astype(BF16)
    low_ref[...] = low
    sums_ref[0:1, :] += column_sums(low.astype(F32))
    sums_ref[1:2, :] += column_sums(grad * normed)
    sums_ref[2:3, :] += column_sums(grad)
    att_ref[...] = dot_nt(low, wo_ref[...]).astype(BF16)


def settle_kernel(pieces, every_ref, *outs):
    rows = every_ref.shape[1]
    for index in range(2 * pieces):
        piece, core = index // 2, index % 2
        column = 0
        for out_ref in outs:
            half = out_ref.shape[1] // 2
            out_ref[piece * rows : (piece + 1) * rows, core * half : (core + 1) * half] = every_ref[
                index, :, column : column + half
            ].astype(F32)
            column += half


def settle(every, widths, pieces):
    rows = every.shape[1]
    whole = pl.BlockSpec(memory_space=pltpu.VMEM)
    return pl.pallas_call(
        functools.partial(settle_kernel, pieces),
        in_specs=[whole],
        out_specs=[whole] * len(widths),
        out_shape=[jax.ShapeDtypeStruct((rows * pieces, width), F32) for width in widths],
        compiler_params=params(),
        name="settle",
    )(every)


def settle_last_kernel(pieces, wide, spots, *rest):
    parts, qkv_ref, out_ref = rest[: 2 * pieces], rest[-2], rest[-1]
    core, spot_u = spots[0], spots[1]
    rows = parts[0].shape[0]
    width = out_ref.shape[1]
    narrow = width // 2 - wide
    for index, part in enumerate(parts):
        side = core if index < pieces else 1 - core
        here = pl.ds(pl.multiple_of((spot_u ^ (index % pieces)) * rows, 16), rows)
        source = 0
        for base, size in ((0, wide), (2 * wide, narrow)):
            for kind in range(3):
                column = pl.multiple_of(kind * width + base + side * size, 128)
                qkv_ref[here, pl.ds(column, size)] = part[:, source : source + size].astype(F32)
                source += size
            if base == 0:
                column = pl.multiple_of(side * (width // 2), 128)
                out_ref[here, pl.ds(column, width // 2)] = part[
                    :, source : source + width // 2
                ].astype(F32)
                source += width // 2


def settle_last(parts, spots, pieces, wide, width):
    rows = parts[0].shape[0]
    whole = pl.BlockSpec(memory_space=pltpu.VMEM)
    return pl.pallas_call(
        functools.partial(settle_last_kernel, pieces, wide),
        in_specs=[pl.BlockSpec(memory_space=pltpu.SMEM)] + [whole] * (2 * pieces),
        out_specs=[whole] * 2,
        out_shape=[
            jax.ShapeDtypeStruct((rows * pieces, columns), F32) for columns in (3 * width, width)
        ],
        compiler_params=params(),
        name="settle_last",
    )(spots, *parts)


def back_product(w_ref, grads, start):
    total = None
    width = w_ref.shape[0]
    for kind, grad in enumerate(grads):
        first = kind * width + start
        part = dot_nt(grad[...], w_ref[:, first : first + grad.shape[1]])
        total = part if total is None else total + part
    return total


def back_one_kernel(w_ref, q_ref, k_ref, v_ref, out_ref):
    out_ref[...] = back_product(w_ref, (q_ref, k_ref, v_ref), 0)


def back_two_kernel(
    start, w_ref, q_ref, k_ref, v_ref, part_ref, x_ref, vec_ref, resid_ref, out_ref, sums_ref
):
    clear_first(sums_ref)
    grad = part_ref[...] + back_product(w_ref, (q_ref, k_ref, v_ref), start)
    inner, normed = norm_back(grad, x_ref[...].astype(F32), row_of(vec_ref, GAIN_ONE))
    out_ref[...] = (resid_ref[...] + inner).astype(BF16)
    sums_ref[0:1, :] += column_sums(grad * normed)
    sums_ref[1:2, :] += column_sums(grad)


def back_one(w, grads):
    length, width = grads[0].shape[0], w.shape[0]
    rows = length // 4
    return pl.pallas_call(
        back_one_kernel,
        grid=(4,),
        in_specs=[pl.BlockSpec(w.shape, lambda i: (0, 0))]
        + [pl.BlockSpec((rows, grads[0].shape[1]), lambda i: (i, 0))] * 3,
        out_specs=pl.BlockSpec((rows, width), lambda i: (i, 0)),
        out_shape=jax.ShapeDtypeStruct((length, width), F32),
        compiler_params=params(),
        cost_estimate=SMALL_COST,
        name="back_one",
    )(w, *grads)


def back_two(w, grads, start, part, values, vectors, resid):
    length, width = values.shape
    rows = length // 4
    block = pl.BlockSpec((rows, width), lambda i: (i, 0))
    return pl.pallas_call(
        functools.partial(back_two_kernel, start),
        grid=(4,),
        in_specs=[pl.BlockSpec(w.shape, lambda i: (0, 0))]
        + [pl.BlockSpec((rows, grads[0].shape[1]), lambda i: (i, 0))] * 3
        + [block, block, pl.BlockSpec((8, width), lambda i: (0, 0)), block],
        out_specs=[block, pl.BlockSpec((8, width), lambda i: (0, 0))],
        out_shape=[
            jax.ShapeDtypeStruct((length, width), BF16),
            jax.ShapeDtypeStruct((8, width), F32),
        ],
        compiler_params=params(),
        cost_estimate=SMALL_COST,
        name="back_two",
    )(w, *grads, part, values, vectors, resid)


def pack_kernel(ln1_ref, one_ref, two_ref, resid_ref, proj_ref, fc_ref, out_ref):
    width = out_ref.shape[1]
    wide = one_ref.shape[1]
    out_ref[0:2, :] = ln1_ref[0:2, :]
    out_ref[2:4, :wide] = one_ref[0:2, :]
    out_ref[2:4, wide:] = two_ref[0:2, :]
    out_ref[4:7, :] = resid_ref[0:3, :]
    out_ref[7:8, :] = proj_ref[0:1, :]
    count = fc_ref.shape[1] // width
    for index in range(count):
        out_ref[8 + index : 9 + index, :] = fc_ref[0:1, index * width : (index + 1) * width]
    out_ref[8 + count : 16, :] = jnp.zeros((8 - count, width), F32)


def pack(*sums):
    whole = pl.BlockSpec(memory_space=pltpu.VMEM)
    return pl.pallas_call(
        pack_kernel,
        in_specs=[whole] * len(sums),
        out_specs=whole,
        out_shape=jax.ShapeDtypeStruct((16, sums[0].shape[1]), F32),
        compiler_params=params(),
        cost_estimate=SMALL_COST,
        name="pack",
    )(*sums)


def shards_of(
    reps,
    shards,
    hidden_in,
    segment,
    cotangent,
    ln1_gain,
    ln1_bias,
    qkv_weight,
    query_bias,
    value_bias,
    out_weight,
    out_bias,
    ln2_gain,
    ln2_bias,
    fc_weight,
    fc_bias,
    proj_weight,
    proj_bias,
):
    width = hidden_in.shape[1]
    shard_rows = qkv_weight.shape[0]
    pieces = 4 if shard_rows % 64 == 0 and reps % 8 == 0 else 2
    rep = lax.axis_index("rep")
    spot_z = lax.axis_index("shard")
    core = rep & 1
    spot_u = (rep >> 1) & (pieces - 1)
    spots = jnp.stack([core, spot_u, spot_z]).astype(jnp.int32)

    def own_piece(weight):
        rows, half = weight.shape[0] // pieces, weight.shape[1] // 2
        return lax.dynamic_slice(weight, (spot_u * rows, core * half), (rows, half))

    def across_chips(part, first):
        if pieces == 2:
            return [part, swap(part, "rep", reps, 2)]
        second = 6 - first
        by_first = swap(part, "rep", reps, first)
        by_second = swap(part, "rep", reps, second)
        by_both = swap(part, "rep", reps, 6)
        if first == 2:
            return [part, by_first, by_second, by_both]
        return [part, by_second, by_first, by_both]

    def across_cores(parts):
        return parts + [swap(part, "rep", reps, 1) for part in parts]

    def along_shard(piece):
        return [swap(piece, "shard", shards, step) for step in range(1, shards)]

    piece_rows = shard_rows // pieces
    flat = [
        ln1_gain,
        ln1_bias,
        query_bias,
        value_bias,
        out_bias,
        ln2_gain,
        ln2_bias,
        proj_bias,
        fc_bias,
    ]
    flat_size = sum(item.shape[0] for item in flat)
    qkv_half = qkv_weight.shape[1] // 2
    small_rows = -(-flat_size // qkv_half)
    small = jnp.zeros((small_rows * qkv_half,), BF16)
    offset = 0
    for item in flat:
        size = item.shape[0]
        small = small + jnp.pad(item, (offset, small.shape[0] - offset - size))
        offset += size
    small = small.reshape(small_rows, qkv_half)
    tie = lax.optimization_barrier
    qkv_payload = jnp.concatenate(
        [own_piece(qkv_weight), jnp.pad(small, ((0, 16 - small_rows), (0, 0)))], axis=0
    )
    second_payload = jnp.concatenate([own_piece(out_weight), own_piece(fc_weight)], axis=1)
    qkv_slots = along_shard(qkv_payload)
    qkv_slots, second_payload = tie((qkv_slots, second_payload))
    qkv_parts = across_chips(jnp.stack([slot[:piece_rows] for slot in qkv_slots]), 2)
    second_slots = along_shard(second_payload)
    rows_of = [small] + [slot[piece_rows : piece_rows + small_rows] for slot in qkv_slots]
    ordered = []
    for index in range(shards):
        total = jnp.zeros_like(rows_of[0])
        for step, value in enumerate(rows_of):
            total = jnp.where((spot_z ^ step) == index, value, total)
        ordered.append(total.reshape(-1)[:flat_size])
    vectors = jnp.stack(ordered).astype(F32)
    bias_fc = vectors[:, 8 * shard_rows :].reshape(1, -1)
    vectors = vectors[:, : 8 * shard_rows].reshape(shards, 8, shard_rows)
    vectors = vectors.transpose(1, 0, 2).reshape(8, width)
    qkv_parts, proj_piece, vectors, bias_fc = tie(
        (qkv_parts, own_piece(proj_weight), vectors, bias_fc)
    )
    qkv_parts = across_cores(qkv_parts)
    second_stack, qkv_parts = tie((jnp.stack(second_slots), qkv_parts))
    second_parts = across_chips(second_stack, 2)

    seg_row = segment[0]
    length = hidden_in.shape[0]
    ff = fc_weight.shape[1]
    steps = 4
    sem_count = 1 + 2 * pieces * (shards - 1)
    kernel_of = lambda body: functools.partial(body, shards, pieces)
    w_qkv, norm_one, qkv = row_call(
        kernel_of(qkv_kernel),
        "qkv",
        steps,
        spots,
        [hidden_in],
        [vectors],
        [qkv_weight, *qkv_parts],
        [
            ((width, 3 * width), BF16, False),
            ((length, width), BF16, True),
            ((length, 3 * width), BF16, True),
        ],
        1,
        sem_count,
    )
    attended_one, lse_one = attend_forward(qkv, seg_row, 0, 4)
    attended_one, proj_piece, qkv, second_parts = tie((attended_one, proj_piece, qkv, second_parts))
    proj_slots = along_shard(proj_piece)
    attended_two, lse_two = attend_forward(qkv, seg_row, 4, 2)
    attended_two, second_parts, proj_slots = tie((attended_two, second_parts, proj_slots))
    second_parts = across_cores(second_parts)
    proj_parts = across_chips(jnp.stack(proj_slots), 4)
    attended = jnp.concatenate([attended_one, attended_two], axis=1)
    w_out, w_fc, resid, norm_two, slope, gelu_low = row_call(
        kernel_of(fc_kernel),
        "fc",
        steps,
        spots,
        [attended, hidden_in],
        [vectors, bias_fc],
        [out_weight, fc_weight, *second_parts],
        [
            ((width, width), BF16, False),
            ((width, ff), BF16, False),
            ((length, width), F32, True),
            ((length, width), BF16, True),
            ((length, ff), BF16, True),
            ((length, ff), BF16, True),
        ],
        2,
        sem_count,
    )

    half_pieces = pieces // 2

    def summed(near, old):
        return near.astype(F32) + old.astype(F32)

    def sent_part(near, old):
        return summed(near[half_pieces:], old[half_pieces:]).astype(BF16)

    def after_first(near, old, came):
        kept = summed(near[:half_pieces], old[:half_pieces]) + came.astype(F32)
        return kept[0], kept[half_pieces - 1].astype(BF16)

    def second_swap(onward, mask):
        return jnp.zeros_like(onward) if pieces == 2 else swap(onward, "rep", reps, mask)

    def shard_swaps(held):
        low = held.astype(BF16)
        return [swap(low[step], "shard", shards, step) for step in range(1, shards)]

    def shard_total(held, came):
        total = held[0]
        for value in came:
            total = total + value.astype(F32)
        mask = 2 * pieces
        while mask < reps:
            total = total + swap(total.astype(BF16), "rep", reps, mask).astype(F32)
            mask *= 2
        return total.astype(BF16)

    def every_owner(piece):
        return lax.all_gather(piece, "rep", axis=0, tiled=False)[: 2 * pieces]

    call = (spots, shards, pieces)
    first_of = 2 if pieces == 2 else 4
    gelu_low, proj_parts = tie((gelu_low, proj_parts))
    proj_parts = across_cores(proj_parts)
    proj_far, proj_near = grad_proj(gelu_low, cotangent, *call, 2)
    gelu_low, proj_far, proj_near, proj_parts = tie((gelu_low, proj_far, proj_near, proj_parts))
    proj_old = swap(proj_far, "rep", reps, 1)
    w_proj, block_out = row_call(
        kernel_of(proj_kernel),
        "proj",
        steps,
        spots,
        [gelu_low, resid],
        [vectors],
        [proj_weight, *proj_parts],
        [((width * 4, width), BF16, False), ((length, width), BF16, True)],
        1,
        sem_count,
    )
    w_proj, proj_old = tie((w_proj, proj_old))
    proj_send = sent_part(proj_near, proj_old)
    proj_send, w_proj = tie((proj_send, w_proj))
    proj_came = swap(proj_send, "rep", reps, 2)
    grad_pre, fc_sums, proj_sums = row_call(
        back_gelu_kernel,
        "back_gelu",
        steps,
        spots,
        [cotangent, slope],
        [w_proj],
        [],
        [((length, ff), BF16, True), ((8, ff), F32, False), ((8, width), F32, False)],
        0,
        0,
    )
    fc_far, fc_near = grad_fc(norm_two, grad_pre, *call, first_of)
    grad_pre, fc_far, fc_near, proj_came = tie((grad_pre, fc_far, fc_near, proj_came))
    fc_old = swap(fc_far, "rep", reps, 1)
    proj_held, proj_onward = after_first(proj_near, proj_old, proj_came)
    grad_pre, proj_onward = tie((grad_pre, proj_onward))
    proj_came = second_swap(proj_onward, 4)
    grad_resid, grad_branch, grad_attended, resid_sums = row_call(
        back_norm_kernel,
        "back_norm",
        steps,
        spots,
        [grad_pre, resid, cotangent],
        [vectors, w_fc, w_out],
        [],
        [
            ((length, width), F32, True),
            ((length, width), BF16, True),
            ((length, width), BF16, True),
            ((8, width), F32, False),
        ],
        0,
        0,
    )
    grad_attended, fc_old = tie((grad_attended, fc_old))
    fc_send = sent_part(fc_near, fc_old)
    grad_attended, fc_send, proj_came = tie((grad_attended, fc_send, proj_came))
    fc_came = swap(fc_send, "rep", reps, first_of)
    *heads_one, sums_one = attend_backward(qkv, seg_row, grad_attended, lse_one, 0, 4)
    heads_one, fc_came, grad_attended, proj_came = tie(
        (heads_one, fc_came, grad_attended, proj_came)
    )
    proj_held = proj_held + proj_came.astype(F32)
    proj_shards = shard_swaps(proj_held)
    fc_held, fc_onward = after_first(fc_near, fc_old, fc_came)
    fc_onward, heads_one = tie((fc_onward, heads_one))
    fc_came = second_swap(fc_onward, 2)
    one_far, one_near = grad_heads(norm_one, heads_one, *call, first_of, (attended, grad_branch))
    heads_one, one_far, one_near, proj_shards, fc_came = tie(
        (heads_one, one_far, one_near, proj_shards, fc_came)
    )
    one_old = swap(one_far, "rep", reps, 1)
    proj_piece = shard_total(proj_held, proj_shards)
    fc_held = fc_held + fc_came.astype(F32)
    proj_piece, heads_one, fc_held = tie((proj_piece, heads_one, fc_held))
    fc_shards = shard_swaps(fc_held)
    part_one = back_one(w_qkv, heads_one)
    part_one, one_old, grad_attended = tie((part_one, one_old, grad_attended))
    one_send = sent_part(one_near, one_old)
    one_send, grad_attended = tie((one_send, grad_attended))
    one_came = swap(one_send, "rep", reps, first_of)
    *heads_two, sums_two = attend_backward(qkv, seg_row, grad_attended, lse_two, 4, 2)
    heads_two, fc_shards = tie((heads_two, fc_shards))
    two_far, two_near = grad_heads(norm_one, heads_two, *call, first_of)
    heads_two, two_far, two_near, one_came = tie((heads_two, two_far, two_near, one_came))
    two_old = swap(two_far, "rep", reps, 1)
    one_held, one_onward = after_first(one_near, one_old, one_came)
    fc_piece = shard_total(fc_held, fc_shards)
    two_old, one_onward, heads_two, fc_piece = tie((two_old, one_onward, heads_two, fc_piece))
    one_came = second_swap(one_onward, 2)
    two_send = sent_part(two_near, two_old)
    two_send, heads_two = tie((two_send, heads_two))
    two_came = swap(two_send, "rep", reps, first_of)
    input_grad, ln1_sums = back_two(
        w_qkv, heads_two, 128 * 4, part_one, hidden_in, vectors, grad_resid
    )
    small_grads = pack(ln1_sums, sums_one, sums_two, resid_sums, proj_sums, fc_sums)
    masks = [1 << i for i in range(reps.bit_length() - 1)]

    def vector_step(total, count=1):
        for mask in masks[:count]:
            total = total + swap(total, "rep", reps, mask)
        del masks[:count]
        return total

    small_grads = vector_step(small_grads)
    two_came, one_came, small_grads = tie((two_came, one_came, small_grads))
    two_held, two_onward = after_first(two_near, two_old, two_came)
    two_onward, small_grads = tie((two_onward, small_grads))
    two_came = second_swap(two_onward, 2)
    one_held = one_held + one_came.astype(F32)
    one_shards = shard_swaps(one_held)
    small_grads = vector_step(small_grads)
    every_fc, every_proj = every_owner(fc_piece), every_owner(proj_piece)
    two_came, one_held, small_grads, every_proj = tie(
        (two_came, one_held, small_grads, every_proj)
    )
    (d_proj_weight,) = settle(every_proj, (width,), pieces)
    two_held = two_held + two_came.astype(F32)
    two_shards = shard_swaps(two_held)
    small_grads = vector_step(small_grads, len(masks))
    two_shards, one_shards, small_grads, every_fc, d_proj_weight = tie(
        (two_shards, one_shards, small_grads, every_fc, d_proj_weight)
    )
    last_piece = jnp.concatenate(
        [shard_total(one_held, one_shards), shard_total(two_held, two_shards)], axis=-1
    )
    last_parts = across_chips(last_piece, 2)
    masks = [1 << i for i in range(shards.bit_length() - 1)]
    for mask in masks[:-1]:
        small_grads = small_grads + swap(small_grads, "shard", shards, mask)
    (d_fc_weight,) = settle(every_fc, (fc_weight.shape[1],), pieces)
    last_parts, small_grads, d_fc_weight = tie((last_parts, small_grads, d_fc_weight))
    last_parts = across_cores(last_parts)
    small_grads = small_grads + swap(small_grads, "shard", shards, masks[-1])
    d_qkv_weight, d_out_weight = settle_last(
        last_parts, spots, pieces, heads_one[0].shape[1] // 2, width
    )
    mine = lax.dynamic_slice(small_grads[:8], (0, spot_z * shard_rows), (8, shard_rows))
    fc_rows = fc_bias.shape[0]
    fc_row = small_grads[8 : 8 + ff // width].reshape(-1)
    d_fc_bias = lax.dynamic_slice(fc_row, (spot_z * fc_rows,), (fc_rows,))
    return (
        block_out,
        input_grad,
        mine[0],
        mine[1],
        d_qkv_weight,
        mine[2],
        mine[3],
        d_out_weight,
        mine[4],
        mine[5],
        mine[6],
        d_fc_weight,
        d_fc_bias,
        d_proj_weight,
        mine[7],
    )


def solution(mesh):
    tokens = P(("rep", "shard"), None)
    flat = P("shard")
    rows = P("shard", None)
    in_specs = (
        tokens,
        tokens,
        tokens,
        flat,
        flat,
        rows,
        flat,
        flat,
        rows,
        flat,
        flat,
        flat,
        rows,
        flat,
        rows,
        flat,
    )
    out_specs = (
        tokens,
        tokens,
        flat,
        flat,
        rows,
        flat,
        flat,
        rows,
        flat,
        flat,
        flat,
        rows,
        flat,
        rows,
        flat,
    )
    body = functools.partial(shards_of, mesh.shape["rep"], mesh.shape["shard"])
    return jax.shard_map(
        body, mesh=mesh, in_specs=in_specs, out_specs=out_specs, check_vma=False
    )
```
